256 devices in a mesh: gz: 32 (over y, z_hi, core), ch: 8 (over x, z_lo).
Axes of the slice: x: 4, y: 4, z: 8 (z_hi: 4, z_lo: 2; z = z_hi * 2 + z_lo), core: 2. Of those that a mesh axis runs over, the one named last changes fastest.
Arguments:
- volume: bfloat16 [16, 256, 64, 128], P(None, 'gz', 'ch'), may hold values from -6 to 6
- filters_two: bfloat16 [32, 16, 3, 3, 3], replicated, may hold values from -0.3125 to 0.3125
- filters_three: bfloat16 [64, 32, 3, 3, 3], P(None, 'ch'), may hold values from -0.21875 to 0.21875
- filters_four: bfloat16 [128, 64, 3, 3, 3], P(None, 'ch'), may hold values from -0.15625 to 0.15625
- cotangent: bfloat16 [128, 32, 8, 16], P('ch', 'gz'), may hold values from -6 to 6
Outputs:
- pooled_four: bfloat16 [128, 32, 8, 16], P('ch', 'gz')
- grad_two: float32 [32, 16, 3, 3, 3], replicated
- grad_three: float32 [64, 32, 3, 3, 3], P(None, 'ch')
- grad_four: float32 [128, 64, 3, 3, 3], P(None, 'ch')
The draws below stay inside these ranges and needn't reach their ends.
All inputs are finite; a program needn't handle non-finite values.
Results may differ from the reference program's by a relative error of at most 0.025.
Values may be sent and summed in bfloat16 or wider, within the bound.
No kernel may reach another device: no remote copies, remote signals or barrier semaphores. Data moves between devices by JAX's collectives and lax.ppermute only.
A program may use at most 128 MiB of HBM per device.

```python
import jax
import jax.numpy as jnp
from jax import lax

C_IN = 16
C_MID = 32
C_DEEP = 64
C_OUT = 128
X = 128
Z = 256
Y = 64


def shard_levels(rng, shape, pieces, low, largest):
    def one(position, parts):
        steps = jax.random.uniform(jax.random.fold_in(jax.random.fold_in(rng, 6), position), (parts,), jnp.float32, low / len(pieces), largest / len(pieces))
        return jnp.repeat(jnp.exp(steps), shape[position] // parts).reshape((-1,) + (1,) * (len(shape) - position - 1))

    factor_of = one(*pieces[0])
    for cut in pieces[1:]:
        factor_of = factor_of * one(*cut)
    return factor_of


def gaussian(key, extent, deviation, most, split=(), kind=jnp.bfloat16):
    values = jax.random.normal(key, extent, jnp.float32) * deviation
    if len(split) > 0:
        values = shard_levels(key, extent, split, -0.22, 0.18) * values
    return jnp.clip(values, min=-most, max=most).astype(kind)


def setup_inputs(seed: int = 0) -> dict:
    arg_keys = jax.random.split(jax.random.key(seed), 6)
    return {
        "volume": gaussian(arg_keys[0], (C_IN, Z, Y, X), 1.0, 6.0, ((1, 32), (2, 8))),
        "filters_two": gaussian(arg_keys[1], (C_MID, C_IN, 3, 3, 3), (27 * C_IN) ** -0.5, 0.3125),
        "filters_three": gaussian(arg_keys[2], (C_DEEP, C_MID, 3, 3, 3), (27 * C_MID) ** -0.5, 0.21875, ((1, 8),)),
        "filters_four": gaussian(arg_keys[3], (C_OUT, C_DEEP, 3, 3, 3), (27 * C_DEEP) ** -0.5, 0.15625, ((1, 8),)),
        "cotangent": gaussian(arg_keys[4], (C_OUT, Z // 8, Y // 8, X // 8), 1.0, 6.0, ((0, 8), (1, 32))),
    }


def activate(values):
    return 0.3 * values + 0.7 * values * jax.nn.sigmoid(values)

def slope_at(values):
    logistic = jax.nn.sigmoid(values)
    return 0.3 + 0.7 * (logistic + values * logistic * (1.0 - logistic))

def average_pool(values):
    c, z, y, x = values.shape
    return values.reshape(c, z // 2, 2, y // 2, 2, x // 2, 2).sum(axis=(2, 4, 6)) * 0.125

def spread_back(values):
    c, z, y, x = values.shape
    wide = jnp.broadcast_to(values[:, :, None, :, None, :, None], (c, z, 2, y, 2, x, 2))
    return wide.reshape(c, 2 * z, 2 * y, 2 * x) * 0.125

def conv_apply(field, filters):
    return lax.conv_general_dilated(field.astype(jnp.float32)[None], filters.astype(jnp.float32), (1, 1, 1), ((1, 1), (1, 1), (1, 1)), dimension_numbers=('NCDHW', 'OIDHW', 'NCDHW'), precision=lax.Precision.HIGHEST)[0]

def filter_grad(field, delta):
    return lax.conv_general_dilated(field.astype(jnp.float32)[None], delta.astype(jnp.float32)[None], (1, 1, 1), ((1, 1), (1, 1), (1, 1)), dimension_numbers=('CNDHW', 'IODHW', 'CNDHW'), precision=lax.Precision.HIGHEST)

def flip_filter(filters):
    return jnp.flip(filters, (2, 3, 4)).transpose(1, 0, 2, 3, 4)

def reference(volume, filters_two, filters_three, filters_four, cotangent):
    pre_two = conv_apply(volume, filters_two)
    pooled_two = average_pool(activate(pre_two)).astype(jnp.bfloat16)
    pre_three = conv_apply(pooled_two, filters_three)
    pooled_three = average_pool(activate(pre_three)).astype(jnp.bfloat16)
    pre_four = conv_apply(pooled_three, filters_four)
    pooled_four = average_pool(activate(pre_four)).astype(jnp.bfloat16)
    delta_four = (spread_back(cotangent.astype(jnp.float32)) * slope_at(pre_four)).astype(jnp.bfloat16)
    grad_four = filter_grad(pooled_three, delta_four)
    back_four = conv_apply(delta_four, flip_filter(filters_four)).astype(jnp.bfloat16)
    delta_three = (spread_back(back_four.astype(jnp.float32)) * slope_at(pre_three)).astype(jnp.bfloat16)
    grad_three = filter_grad(pooled_two, delta_three)
    back_three = conv_apply(delta_three, flip_filter(filters_three)).astype(jnp.bfloat16)
    delta_two = (spread_back(back_three.astype(jnp.float32)) * slope_at(pre_two)).astype(jnp.bfloat16)
    grad_two = filter_grad(volume, delta_two)
    return (pooled_four, grad_two, grad_three, grad_four)
```

```python
import jax
import jax.numpy as jnp
import numpy as np
from jax import lax
from jax.experimental import pallas as pl
from jax.experimental.pallas import tpu as pltpu
from jax.sharding import PartitionSpec as P

BF = jnp.bfloat16
F32 = jnp.float32
VMEM_LIMIT = 40 * 1024 * 1024


def grid(*extents):
    return np.meshgrid(*[np.arange(n) for n in extents], indexing="ij")


def shift_rows():
    out = np.zeros((128, 2, 128), np.float32)
    for x in range(128):
        if x > 0:
            out[x - 1, 0, x] = 1
        if x < 127:
            out[x + 1, 1, x] = 1
    return out.reshape(128, 256)


def shift_halves():
    out = np.zeros((2, 64, 2, 2, 64), np.float32)
    for h in range(2):
        for x in range(64):
            if x > 0:
                out[h, x - 1, 0, h, x] = 1
            if x < 63:
                out[h, x + 1, 1, h, x] = 1
    return out.reshape(128, 256)


def shift_straight():
    side = shift_halves()
    return np.concatenate([side[:, :128], np.eye(128, dtype=np.float32), side[:, 128:]], 1)


def shift_cross():
    straight = shift_straight()
    out = np.zeros((256, 384), np.float32)
    out[64:128] = straight[0:64]
    out[128:192] = straight[64:128]
    return out


def pool_two():
    out = np.zeros((2, 64, 2, 2, 64), np.float32)
    for h in range(2):
        for x in range(64):
            out[h, x, :, h, x] = 0.125
    return out.reshape(256, 128)


def pool_three():
    out = np.zeros((2, 2, 32, 2, 2, 2, 32), np.float32)
    for yc in range(2):
        for zc in range(2):
            for x in range(32):
                out[yc, zc, x, :, zc, yc, x] = 0.125
    return out.reshape(256, 128)


def gather_planes():
    out = np.zeros((5, 2, 2, 32, 2, 8, 32), np.float32)
    for b in range(5):
        for yy in range(2):
            y = 2 * b + yy - 1
            if 0 <= y < 8:
                for zz in range(2):
                    for x in range(32):
                        out[b, zz, yy, x, zz, y, x] = 1
    return out.reshape(640, 512)


def shift_planes():
    out = np.zeros((8, 32, 3, 3, 8, 32), np.float32)
    for ky in range(3):
        for kx in range(3):
            for y in range(8):
                for x in range(32):
                    sy, sx = y + ky, x + kx - 1
                    if sy < 8 and 0 <= sx < 32:
                        out[sy, sx, ky, kx, y, x] = 1
    return out.reshape(256, 2304)


def pool_four():
    out = np.zeros((8, 16, 2, 128), np.float32)
    for x in range(16):
        out[2:4, x, :, x] = 0.125
    return out.reshape(256, 128)


def spread_three():
    out = np.zeros((2, 8, 32, 6, 2, 32, 2), np.float32)
    for r in range(6):
        cell = (r - 1) // 2 + 1
        for h in range(2):
            for x in range(32):
                out[h, cell, x, r, h, x, :] = 0.125
    return out.reshape(512, 768)


def spread_two():
    out = np.zeros((2, 64, 2, 64, 2), np.float32)
    for h in range(2):
        for x in range(64):
            out[h, x, h, x, :] = 0.125
    return out.reshape(128, 256)


def const(build):
    return jnp.asarray(build(), BF)


def dot(a, b):
    return lax.dot_general(a, b, (((1,), (0,)), ((), ())), preferred_element_type=F32)


def dot_nt(a, b):
    return lax.dot_general(a, b, (((1,), (1,)), ((), ())), preferred_element_type=F32)


def sigmoid(u):
    return 0.5 * jnp.tanh(0.5 * u) + 0.5


def act_of(u, s):
    return u * (0.3 + 0.7 * s)


def slope_of(u, s):
    return 0.3 + 0.7 * (s + u * s * (1.0 - s))


def call(kernel, out_shape, scratch, flops, args):
    specs = [pl.BlockSpec(memory_space=pltpu.SMEM)] + [
        pl.BlockSpec(memory_space=pltpu.VMEM) for _ in args[1:]
    ]
    return pl.pallas_call(
        kernel,
        out_shape=out_shape,
        in_specs=specs,
        out_specs=jax.tree.map(lambda _: pl.BlockSpec(memory_space=pltpu.VMEM), out_shape),
        scratch_shapes=scratch,
        compiler_params=pltpu.CompilerParams(vmem_limit_bytes=VMEM_LIMIT),
        cost_estimate=pl.CostEstimate(flops=flops, bytes_accessed=1 << 20, transcendentals=0),
    )(*args)


def shift_volume(z, planes, shift, vx, zi):
    y = 0
    for ref, first, rows in planes:
        field = ref[z, first : first + rows].reshape(rows * 16, 128)
        sides = dot(field, shift)
        for r in range(rows):
            lanes = pl.ds((y + r) * 128, 128)
            vx[zi, 0:16, lanes] = sides[r * 16 : r * 16 + 16, :128].astype(BF)
            vx[zi, 16:32, lanes] = field[r * 16 : r * 16 + 16]
            vx[zi, 32:48, lanes] = sides[r * 16 : r * 16 + 16, 128:].astype(BF)
        y += rows


def forward_kernel(
    pos, ylo, mid, yhi, w2, w3, shift2, pool2, shift3, pool3, p3, sl3, sl2, vq, vx, sums
):
    gz, ch = pos[0], pos[1]
    shift = shift2[...]

    @pl.loop(0, 14)
    def _(z):
        shift_volume(z, ((ylo, 0, 5), (mid, 0, 8), (yhi, 0, 5)), shift, vx, z)

    filters = w2[...]

    @pl.loop(0, 6)
    def _(zc):
        zg = 4 * gz + zc - 1
        z_in = jnp.logical_and(zg >= 0, zg < 128)
        for q in range(4):
            total = [None, None]
            for dz in range(2):
                z = 2 * zc + dz
                rhs = jnp.concatenate(
                    [
                        vx[z + kz, :, (4 * q + ky) * 128 : (4 * q + ky + 4) * 128]
                        for kz in range(3)
                        for ky in range(3)
                    ],
                    axis=0,
                )
                pre = dot(filters, rhs)
                s = sigmoid(pre)
                a = act_of(pre, s)
                if q in (1, 2):
                    sl2[z, :, (q - 1) * 512 : q * 512] = slope_of(pre, s).astype(BF)
                for c in range(2):
                    part = a[:, c * 256 : c * 256 + 128] + a[:, c * 256 + 128 : c * 256 + 256]
                    total[c] = part if dz == 0 else total[c] + part
            for c in range(2):
                yc = 2 * q + c
                yg = 4 * ch + yc - 2
                inside = jnp.logical_and(z_in, jnp.logical_and(yg >= 0, yg < 32))
                sums[zc, yc * 32 : yc * 32 + 32] = jnp.where(inside, total[c], 0.0).astype(BF)

    pool = pool2[...]
    halves = shift3[...]
    for j in range(4):
        pair = jnp.concatenate([sums[j], sums[j + 2]], axis=1)
        pooled = dot(pair, pool).astype(BF)
        sides = dot(pooled, halves)
        for y in range(8):
            rows = slice(y * 32, y * 32 + 32)
            lanes = slice(y * 128, y * 128 + 128)
            vq[j, 0:32, lanes] = sides[rows, :128].astype(BF)
            vq[j, 32:64, lanes] = pooled[rows]
            vq[j, 64:96, lanes] = sides[rows, 128:].astype(BF)

    filters = w3[...]
    cells = [None, None]
    for zp in range(2):
        for n, (ya, yb) in enumerate(((1, 2), (3, 4), (0, 5))):
            blocks = []
            for kz in range(3):
                for ky in range(3):
                    if yb == ya + 1:
                        blocks.append(vq[zp + kz, :, (ya + ky) * 128 : (ya + ky + 2) * 128])
                    else:
                        blocks.append(
                            jnp.concatenate(
                                [
                                    vq[zp + kz, :, (ya + ky) * 128 : (ya + ky + 1) * 128],
                                    vq[zp + kz, :, (yb + ky) * 128 : (yb + ky + 1) * 128],
                                ],
                                axis=1,
                            )
                        )
            pre = dot(filters, jnp.concatenate(blocks, axis=0))
            s = sigmoid(pre)
            slope = slope_of(pre, s).astype(BF)
            sl3[zp, :, ya * 128 : ya * 128 + 128] = slope[:, :128]
            sl3[zp, :, yb * 128 : yb * 128 + 128] = slope[:, 128:]
            if n < 2:
                a = act_of(pre, s)
                part = a[:, :128] + a[:, 128:]
                cells[n] = part if zp == 0 else cells[n] + part
    both = jnp.concatenate(cells, axis=1).astype(BF)
    p3[...] = dot(both, pool3[...]).astype(BF)


def deep_kernel(
    pos, got, w4f, w4b, cot, sl3, planes_of, shift4, pool4, spread3, p4, d3, field, own, planes, back_in
):
    ch = pos[1]
    parts = []
    for b in range(5):
        yb = ch + (b - 2)
        inside = jnp.logical_and(yb >= 0, yb < 8)
        block = got[jnp.clip(yb, 0, 7)].reshape(192, 128)
        parts.append(jnp.where(inside, block.astype(F32), 0.0).astype(BF))
    flat = dot(jnp.concatenate(parts, axis=1), planes_of[...]).astype(BF)
    for zb in range(3):
        for zz in range(2):
            p = 2 * zb + zz
            planes[p * 64 : p * 64 + 64] = flat[zb * 64 : zb * 64 + 64, zz * 256 : zz * 256 + 256]
    for k in range(9):
        moved = dot(planes[...], shift4[:, k * 256 : k * 256 + 256]).astype(BF)
        for p in range(6):
            field[p, k * 64 : k * 64 + 64] = moved[p * 64 : p * 64 + 64]

    row = lax.broadcasted_iota(jnp.int32, (128, 256), 0)
    lane = lax.broadcasted_iota(jnp.int32, (128, 256), 1)
    source_y, source_x = row // 16, row % 16
    y, x = lane // 32, lane % 32
    match = (source_x == x // 2) & (source_y == ch - 1 + y // 2) & (y < 6)
    spread = jnp.where(match, 0.125, 0.0).astype(BF)
    mine = lax.broadcasted_iota(jnp.int32, (128, 256), 1) // 64 == 1

    filters = w4f[...]
    pooled = None
    deltas = []
    for z in range(4):
        pre = dot(filters, field[z : z + 3].reshape(1728, 256))
        s = sigmoid(pre)
        cell = (z + 1) // 2
        wide = dot(cot[:, cell].reshape(128, 128), spread)
        delta = wide * slope_of(pre, s)
        deltas.append(delta.astype(BF))
        if z in (1, 2):
            own[z - 1] = jnp.where(mine, delta, 0.0).astype(BF)
            a = act_of(pre, s)
            pooled = a if pooled is None else pooled + a
    high = pooled.astype(BF)
    low = (pooled - high.astype(F32)).astype(BF)
    p4[...] = dot(high, pool4[...]) + dot(low, pool4[...])

    stacked = jnp.concatenate(deltas, axis=0)
    for k in range(9):
        moved = dot(stacked, shift4[:, k * 256 : k * 256 + 256]).astype(BF)
        for z in range(4):
            back_in[z, k * 128 : k * 128 + 128] = moved[z * 128 : z * 128 + 128]
    filters = w4b[...]
    back = [
        dot(filters, back_in[z : z + 3].reshape(3456, 256)).astype(BF) for z in range(2)
    ]
    wide = dot(jnp.concatenate(back, axis=1), spread3[...])
    for r in range(6):
        yg = 4 * ch + r - 1
        inside = jnp.logical_and(yg >= 0, yg < 32)
        lanes = slice(r * 128, r * 128 + 128)
        value = jnp.where(inside, wide[:, lanes], 0.0)
        for zp in range(2):
            d3[zp, :, lanes] = (value * sl3[zp, :, lanes].astype(F32)).astype(BF)


def grads_kernel(pos, field, own, vq, d3, out):
    right = jnp.concatenate([own[0], own[1]], axis=1)
    for kz in range(3):
        left = jnp.concatenate([field[1 + kz], field[2 + kz]], axis=1)
        res = dot_nt(left, right)
        for k in range(9):
            for c in range(8):
                at = (kz * 9 + k) * 8
                out[c, at : at + 8] = res[k * 64 + c * 8 : k * 64 + c * 8 + 8]
    total = None
    zero = jnp.zeros((64, 512), BF)
    for j in range(4):
        rows = []
        for kz in range(3):
            zp = j - kz
            rows.append(d3[zp, :, 128:640] if 0 <= zp < 2 else zero)
        left = jnp.concatenate(
            [vq[j, :, (1 + ky) * 128 : (1 + ky) * 128 + 512] for ky in range(3)], axis=0
        )
        res = dot_nt(left, jnp.concatenate(rows, axis=0))
        total = res if total is None else total + res
    for k in range(9):
        for c in range(8):
            at = 216 + k * 4
            piece = total[k * 32 + c * 4 : k * 32 + c * 4 + 4]
            out[c, at : at + 4] = piece[:, :128]
            out[c, at + 36 : at + 40, 0:64] = piece[:, 128:]
    for c in range(8):
        out[c, 252:288, 64:128] = jnp.zeros((36, 64), F32)


def shallow_kernel(
    pos, d3, above, below, w3b, sl2, ylo, mid, yhi, shift2, straight, cross, spread2, g2, ds, vx, d2
):
    direct = straight[...]
    across = cross[...]
    for y in range(6):
        lanes = slice(y * 128, y * 128 + 128)
        first, second = d3[0, :, lanes], d3[1, :, lanes]
        moved = (
            dot(jnp.concatenate([above[:, lanes], second], axis=1), across),
            dot(first, direct),
            dot(second, direct),
            dot(jnp.concatenate([first, below[:, lanes]], axis=1), across),
        )
        for j in range(4):
            for kx in range(3):
                ds[j, kx * 64 : kx * 64 + 64, lanes] = moved[j][:, kx * 128 : kx * 128 + 128].astype(BF)

    shift = shift2[...]

    @pl.loop(0, 10)
    def _(z):
        shift_volume(z + 2, ((ylo, 4, 1), (mid, 0, 8), (yhi, 0, 1)), shift, vx, z)

    for z in (0, 1, 10, 11):
        d2[z] = jnp.zeros((32, 1024), BF)
    filters = w3b[...]
    widen = spread2[...]
    for zp in range(2):
        for q in range(2):
            rhs = jnp.concatenate(
                [
                    ds[zp + kz, :, (2 * q + ky) * 128 : (2 * q + ky + 2) * 128]
                    for kz in range(3)
                    for ky in range(3)
                ],
                axis=0,
            )
            back = dot(filters, rhs).astype(BF)
            for r in range(2):
                y = 2 * q + r
                wide = dot(back[:, r * 128 : r * 128 + 128], widen)
                for h in range(2):
                    value = wide[:, h * 128 : h * 128 + 128]
                    for dz in range(2):
                        z2 = 2 * (zp + 2 * h) + dz
                        for dy in range(2):
                            lanes = slice((2 * y + dy) * 128, (2 * y + dy) * 128 + 128)
                            slope = sl2[z2 + 2, :, lanes].astype(F32)
                            d2[z2 + 2, :, lanes] = (value * slope).astype(BF)

    def step(z, total):
        left = jnp.concatenate([vx[z, :, ky * 128 : ky * 128 + 1024] for ky in range(3)], axis=0)
        right = jnp.concatenate([d2[z + 2 - kz] for kz in range(3)], axis=0)
        return total + dot_nt(left, right)

    total = lax.fori_loop(0, 10, step, jnp.zeros((144, 96), F32))
    g2[...] = jnp.zeros((160, 128), F32)
    g2[0:144, 0:96] = total


def ladder(count):
    up = [(i, i + 1) for i in range(count - 1)]
    return up, [(b, a) for a, b in up]


def to_all(piece, axis):
    count = lax.axis_size(axis)
    copies = jnp.broadcast_to(piece[None], (count,) + piece.shape)
    return lax.all_to_all(copies, axis, 0, 0, tiled=True)


def body(volume, filters_two, filters_three, filters_four, cotangent):
    gz, ch = lax.axis_index("gz"), lax.axis_index("ch")
    pos = jnp.stack([gz, ch]).astype(jnp.int32)
    z_up, z_down = ladder(lax.axis_size("gz"))
    y_up, y_down = ladder(lax.axis_size("ch"))
    shape = jax.ShapeDtypeStruct

    field = volume.transpose(1, 2, 0, 3)
    cot = cotangent.reshape(1, 16, 128)
    low = lax.ppermute(
        jnp.concatenate([field[5:].reshape(24, 16, 128), cot], axis=0), "gz", z_up
    )
    high = lax.ppermute(
        jnp.concatenate([field[:3].reshape(24, 16, 128), cot], axis=0), "gz", z_down
    )
    mid = jnp.concatenate(
        [low[:24].reshape(3, 8, 16, 128), field, high[:24].reshape(3, 8, 16, 128)], axis=0
    )
    ylo = lax.ppermute(mid[:, 3:], "ch", y_up)
    yhi = lax.ppermute(mid[:, :5], "ch", y_down)

    four = filters_four.transpose(2, 3, 4, 1, 0).reshape(216, 128)
    three = filters_three.transpose(2, 3, 4, 1, 0).reshape(108, 64)
    three = jnp.pad(three, ((0, 0), (0, 64)))
    cots = jnp.concatenate([low[24:], cot, high[24:]], axis=0).reshape(48, 128)
    all_of = to_all(jnp.concatenate([four, three, cots], axis=0), "ch")
    four = all_of[:, :216].reshape(8, 27, 8, 128)
    three = all_of[:, 216:324, :64].reshape(8, 27, 4, 64)
    cots = all_of[:, 324:].reshape(8, 3, 16, 128)

    w2 = filters_two.transpose(0, 2, 3, 4, 1).reshape(32, 432)
    w3f = three.transpose(3, 1, 0, 2).reshape(64, 864)
    w3b = three[:, ::-1].transpose(0, 2, 1, 3).reshape(32, 1728)
    w4f = four.transpose(3, 1, 0, 2).reshape(128, 1728)
    w4b = four[:, ::-1].transpose(0, 2, 1, 3).reshape(64, 3456)

    shift2 = const(shift_rows)
    p3, sl3, sl2, vq = call(
        forward_kernel,
        (
            shape((64, 128), BF),
            shape((2, 64, 768), BF),
            shape((12, 32, 1024), BF),
            shape((4, 96, 1024), BF),
        ),
        [pltpu.VMEM((14, 48, 2304), BF), pltpu.VMEM((6, 256, 128), BF)],
        1 << 32,
        (pos, ylo, mid, yhi, w2, w3f, shift2, const(pool_two), const(shift_halves), const(pool_three)),
    )
    below = lax.ppermute(p3, "gz", z_up)
    above = lax.ppermute(p3, "gz", z_down)
    got = to_all(jnp.stack([below, p3, above]), "ch")
    p4, d3, field4, own4 = call(
        deep_kernel,
        (
            shape((128, 128), F32),
            shape((2, 64, 768), BF),
            shape((6, 576, 256), BF),
            shape((2, 128, 256), BF),
        ),
        [pltpu.VMEM((384, 256), BF), pltpu.VMEM((4, 1152, 256), BF)],
        1 << 32,
        (
            pos, got, w4f, w4b, cots, sl3,
            const(gather_planes), const(shift_planes), const(pool_four), const(spread_three),
        ),
    )
    above = lax.ppermute(d3[1], "gz", z_up)
    below = lax.ppermute(d3[0], "gz", z_down)

    grads = call(
        grads_kernel, shape((8, 288, 128), F32), [], 1 << 32, (pos, field4, own4, vq, d3)
    )
    grads = lax.all_to_all(grads.astype(BF), "ch", 0, 0, tiled=True)
    grads = grads.astype(F32).sum(axis=0).astype(BF)

    pooled_four = lax.all_to_all(
        p4[:, :16].astype(BF).reshape(8, 16, 16), "ch", 0, 0, tiled=True
    ).transpose(1, 0, 2)[:, None]

    g2 = call(
        shallow_kernel,
        shape((160, 128), F32),
        [
            pltpu.VMEM((4, 192, 768), BF),
            pltpu.VMEM((10, 48, 1280), BF),
            pltpu.VMEM((12, 32, 1024), BF),
        ],
        1 << 32,
        (
            pos, d3, above, below, w3b, sl2, ylo, mid, yhi,
            shift2, const(shift_straight), const(shift_cross), const(spread_two),
        ),
    )
    pieces = jnp.concatenate(
        [grads.reshape(32, 9, 128), g2.astype(BF).reshape(32, 5, 128)], axis=1
    )
    pieces = lax.all_to_all(pieces, "gz", 0, 0, tiled=True).astype(F32).sum(axis=0)
    two = to_all(pieces[9:].astype(BF), "ch").astype(F32).sum(axis=0)
    whole = to_all(jnp.concatenate([pieces[:9], two], axis=0).astype(BF), "gz")
    deep = whole[:, :9].reshape(288, 128).astype(F32)
    grad_four = deep[:216].reshape(3, 3, 3, 8, 128).transpose(4, 3, 0, 1, 2)
    lanes = jnp.concatenate([deep[216:252], deep[252:288, :64]], axis=1)
    grad_three = lanes.reshape(3, 3, 4, 3, 64).transpose(4, 2, 3, 0, 1)
    two = whole[:, 9:].reshape(160, 128)[:144, :96].astype(F32)
    grad_two = two.reshape(3, 3, 16, 3, 32).transpose(4, 2, 3, 0, 1)
    return (pooled_four, grad_two, grad_three, grad_four)


def solution(mesh):
    in_specs = (
        P(None, "gz", "ch", None),
        P(),
        P(None, "ch", None, None, None),
        P(None, "ch", None, None, None),
        P("ch", "gz", None, None),
    )
    out_specs = (
        P("ch", "gz", None, None),
        P(),
        P(None, "ch", None, None, None),
        P(None, "ch", None, None, None),
    )
    return jax.shard_map(body, mesh=mesh, in_specs=in_specs, out_specs=out_specs, check_vma=False)
```

```python
import jax
import jax.numpy as jnp
import numpy as np
from jax import lax
from jax.experimental import pallas as pl
from jax.experimental.pallas import tpu as pltpu
from jax.sharding import PartitionSpec as P

BF = jnp.bfloat16
F32 = jnp.float32
VMEM_LIMIT = 12 * 1024 * 1024


def grid(*extents):
    return np.meshgrid(*[np.arange(n) for n in extents], indexing="ij")


def shift_rows():
    out = np.zeros((128, 2, 128), np.float32)
    for x in range(128):
        if x > 0:
            out[x - 1, 0, x] = 1
        if x < 127:
            out[x + 1, 1, x] = 1
    return out.reshape(128, 256)


def shift_halves():
    out = np.zeros((2, 64, 2, 2, 64), np.float32)
    for h in range(2):
        for x in range(64):
            if x > 0:
                out[h, x - 1, 0, h, x] = 1
            if x < 63:
                out[h, x + 1, 1, h, x] = 1
    return out.reshape(128, 256)


def shift_straight():
    side = shift_halves()
    return np.concatenate([side[:, :128], np.eye(128, dtype=np.float32), side[:, 128:]], 1)


def shift_cross():
    straight = shift_straight()
    out = np.zeros((256, 384), np.float32)
    out[64:128] = straight[0:64]
    out[128:192] = straight[64:128]
    return out


def pool_two():
    out = np.zeros((2, 64, 2, 2, 64), np.float32)
    for h in range(2):
        for x in range(64):
            out[h, x, :, h, x] = 0.125
    return out.reshape(256, 128)


def pool_three():
    out = np.zeros((2, 2, 32, 2, 2, 2, 32), np.float32)
    for yc in range(2):
        for zc in range(2):
            for x in range(32):
                out[yc, zc, x, :, zc, yc, x] = 0.125
    return out.reshape(256, 128)


def gather_planes():
    out = np.zeros((5, 2, 2, 32, 2, 8, 32), np.float32)
    for b in range(5):
        for yy in range(2):
            y = 2 * b + yy - 1
            if 0 <= y < 8:
                for zz in range(2):
                    for x in range(32):
                        out[b, zz, yy, x, zz, y, x] = 1
    return out.reshape(640, 512)


def shift_planes():
    out = np.zeros((8, 32, 3, 3, 8, 32), np.float32)
    for ky in range(3):
        for kx in range(3):
            for y in range(8):
                for x in range(32):
                    sy, sx = y + ky, x + kx - 1
                    if sy < 8 and 0 <= sx < 32:
                        out[sy, sx, ky, kx, y, x] = 1
    return out.reshape(256, 2304)


def pool_four():
    out = np.zeros((8, 16, 2, 128), np.float32)
    for x in range(16):
        out[2:4, x, :, x] = 0.125
    return out.reshape(256, 128)


def spread_three():
    out = np.zeros((2, 8, 32, 6, 2, 32, 2), np.float32)
    for r in range(6):
        cell = (r - 1) // 2 + 1
        for h in range(2):
            for x in range(32):
                out[h, cell, x, r, h, x, :] = 0.125
    return out.reshape(512, 768)


def spread_two():
    out = np.zeros((2, 64, 2, 64, 2), np.float32)
    for h in range(2):
        for x in range(64):
            out[h, x, h, x, :] = 0.125
    return out.reshape(128, 256)


def deep_matrices():
    out = np.zeros((896, 2304), np.float32)
    out[:256] = shift_planes()
    out[256:896, :512] = gather_planes()
    out[256:768, 512:1280] = spread_three()
    return out


def const(build):
    return jnp.asarray(build(), BF)


def dot(a, b):
    return lax.dot_general(a, b, (((1,), (0,)), ((), ())), preferred_element_type=F32)


def dot_nt(a, b):
    return lax.dot_general(a, b, (((1,), (1,)), ((), ())), preferred_element_type=F32)


def sigmoid(u):
    return 0.5 * jnp.tanh(0.5 * u) + 0.5


def act_of(u, s):
    return u * (0.3 + 0.7 * s)


def slope_of(u, s):
    return 0.3 + 0.7 * (s + u * s * (1.0 - s))


def call(kernel, out_shape, scratch, flops, args, far_in=(), far_out=()):
    def place(far):
        return pl.BlockSpec(memory_space=pltpu.HBM if far else pltpu.VMEM)

    specs = [pl.BlockSpec(memory_space=pltpu.SMEM)] + [
        place(n in far_in) for n in range(1, len(args))
    ]
    args = [
        pltpu.with_memory_space_constraint(a, pltpu.HBM) if n in far_in else a
        for n, a in enumerate(args)
    ]
    return pl.pallas_call(
        kernel,
        out_shape=tuple(
            pltpu.HBM(o.shape, o.dtype) if n in far_out else o for n, o in enumerate(out_shape)
        ),
        in_specs=specs,
        out_specs=tuple(place(n in far_out) for n in range(len(out_shape))),
        scratch_shapes=scratch,
        compiler_params=pltpu.CompilerParams(vmem_limit_bytes=VMEM_LIMIT),
        cost_estimate=pl.CostEstimate(flops=flops, bytes_accessed=1 << 20, transcendentals=0),
    )(*args)


def copies(pairs, sems):
    out = [pltpu.make_async_copy(a, b, sems.at[n]) for n, (a, b) in enumerate(pairs)]
    for copy in out:
        copy.start()
    return out


def shallow_forward_kernel(
    pos, near, mid, far, w2, shift2, pool2, shift3, vq, sl2_far, vx_far, sums, sl2, vx, sems
):
    gz, ch = pos[0], pos[1]
    shift = shift2[...]

    odd = gz % 2 == 1
    for which, first, count in ((0, 0, 3), (1, 3, 8), (2, 11, 3)):

        @pl.loop(0, count, unroll=2 if count == 8 else 3)
        def _(z):
            if which == 1:
                field = mid[z].reshape(288, 128)
            else:
                one, two = near[z].reshape(288, 128), far[z].reshape(288, 128)
                if which == 2:
                    one, two = two, one
                field = jnp.where(odd, one.astype(F32), two.astype(F32)).astype(BF)
            sides = dot(field, shift)
            for y in range(18):
                lanes = slice(y * 128, y * 128 + 128)
                rows = slice(y * 16, y * 16 + 16)
                vx[z + first, 0:16, lanes] = sides[rows, :128].astype(BF)
                vx[z + first, 16:32, lanes] = field[rows]
                vx[z + first, 32:48, lanes] = sides[rows, 128:].astype(BF)

    vx_copy = pltpu.make_async_copy(
        vx.at[2:12, :, 512:1792], vx_far, sems.at[0]
    )
    vx_copy.start()
    filters = w2[...]

    @pl.loop(0, 6, unroll=2)
    def _(zc):
        zg = 4 * gz + zc - 1
        z_in = jnp.logical_and(zg >= 0, zg < 128)
        for q in range(4):
            rhs = jnp.concatenate(
                [
                    jnp.concatenate(
                        [
                            vx[2 * zc + zz, :, (4 * q + yy) * 128 : (4 * q + yy + 1) * 128],
                            vx[2 * zc + zz, :, (4 * q + yy + 2) * 128 : (4 * q + yy + 3) * 128],
                        ],
                        axis=1,
                    )
                    for zz in range(4)
                    for yy in range(4)
                ],
                axis=0,
            )
            pre = dot(filters, rhs)
            s = sigmoid(pre)
            a = act_of(pre, s)
            if q in (1, 2):
                sl2[zc, :, (q - 1) * 256 : q * 256] = slope_of(pre, s).astype(BF)
            total = (a[0:32] + a[32:64]) + (a[64:96] + a[96:128])
            for c in range(2):
                yc = 2 * q + c
                yg = 4 * ch + yc - 2
                inside = jnp.logical_and(z_in, jnp.logical_and(yg >= 0, yg < 32))
                cell = jnp.where(inside, total[:, c * 128 : c * 128 + 128], 0.0)
                sums[zc, yc * 32 : yc * 32 + 32] = cell.astype(BF)

    sl2_copy = pltpu.make_async_copy(sl2.at[1:5], sl2_far, sems.at[1])
    sl2_copy.start()
    pool = pool2[...]
    halves = shift3[...]
    for j in range(4):
        pair = jnp.concatenate([sums[j], sums[j + 2]], axis=1)
        pooled = dot(pair, pool).astype(BF)
        sides = dot(pooled, halves)
        for y in range(8):
            rows = slice(y * 32, y * 32 + 32)
            lanes = slice(y * 128, y * 128 + 128)
            vq[j, 0:32, lanes] = sides[rows, :128].astype(BF)
            vq[j, 32:64, lanes] = pooled[rows]
            vq[j, 64:96, lanes] = sides[rows, 128:].astype(BF)
    vx_copy.wait()
    sl2_copy.wait()


def middle_forward_kernel(pos, vq, w3, pool3, p3, sl3_far, vq_far, sl3, sems):
    vq_copy = pltpu.make_async_copy(vq, vq_far, sems.at[0])
    vq_copy.start()
    filters = w3[...]
    cells = [None, None]
    for zp in range(2):
        for n, (ya, yb) in enumerate(((1, 2), (3, 4), (0, 5))):
            blocks = []
            for kz in range(3):
                for ky in range(3):
                    if yb == ya + 1:
                        blocks.append(vq[zp + kz, :, (ya + ky) * 128 : (ya + ky + 2) * 128])
                    else:
                        blocks.append(
                            jnp.concatenate(
                                [
                                    vq[zp + kz, :, (ya + ky) * 128 : (ya + ky + 1) * 128],
                                    vq[zp + kz, :, (yb + ky) * 128 : (yb + ky + 1) * 128],
                                ],
                                axis=1,
                            )
                        )
            pre = dot(filters, jnp.concatenate(blocks, axis=0))
            s = sigmoid(pre)
            slope = slope_of(pre, s).astype(BF)
            sl3[zp, :, ya * 128 : ya * 128 + 128] = slope[:, :128]
            sl3[zp, :, yb * 128 : yb * 128 + 128] = slope[:, 128:]
            if n < 2:
                a = act_of(pre, s)
                part = a[:, :128] + a[:, 128:]
                cells[n] = part if zp == 0 else cells[n] + part
    sl3_copy = pltpu.make_async_copy(sl3, sl3_far, sems.at[1])
    sl3_copy.start()
    both = jnp.concatenate(cells, axis=1).astype(BF)
    p3[...] = dot(both, pool3[...]).astype(BF)
    vq_copy.wait()
    sl3_copy.wait()


def deep_kernel(
    pos, got, w4f, w4b, pool4, w3b, sl3_far, matrices,
    p4, d3, near_out, far_out, field, own,
    planes, back_in, sl3, planes_of, shift4, spread3, sems,
):
    planes_copy, shift_copy, spread_copy, sl3_copy = copies(
        (
            (matrices.at[256:896, 0:512], planes_of),
            (matrices.at[0:256], shift4),
            (matrices.at[256:768, 512:1280], spread3),
            (sl3_far, sl3),
        ),
        sems,
    )
    odd, ch = pos[0] % 2, pos[1]
    low = 2 - 2 * odd
    parts = []
    for b in range(5):
        yb = ch + (b - 2)
        inside = jnp.logical_and(yb >= 0, yb < 8)
        source = jnp.clip(yb, 0, 7)
        block = jnp.concatenate(
            [got[source, zb, 0:64] for zb in (low, 1, 2 - low)], axis=0
        )
        parts.append(jnp.where(inside, block.astype(F32), 0.0).astype(BF))
    planes_copy.wait()
    flat = dot(jnp.concatenate(parts, axis=1), planes_of[...]).astype(BF)
    for zb in range(3):
        for zz in range(2):
            p = 2 * zb + zz
            planes[p * 64 : p * 64 + 64] = flat[zb * 64 : zb * 64 + 64, zz * 256 : zz * 256 + 256]
    shift_copy.wait()
    for k in range(9):
        moved = dot(planes[...], shift4[:, k * 256 : k * 256 + 256]).astype(BF)
        for p in range(6):
            field[p, k * 64 : k * 64 + 64] = moved[p * 64 : p * 64 + 64]

    row = lax.broadcasted_iota(jnp.int32, (128, 256), 0)
    lane = lax.broadcasted_iota(jnp.int32, (128, 256), 1)
    source_y, source_x = row // 16, row % 16
    y, x = lane // 32, lane % 32
    match = (source_x == x // 2) & (source_y == ch - 1 + y // 2) & (y < 6)
    spread = jnp.where(match, 0.125, 0.0).astype(BF)
    mine = lax.broadcasted_iota(jnp.int32, (128, 256), 1) // 64 == 1

    filters = w4f[...]
    pooled = None
    deltas = []
    for z in range(4):
        pre = dot(filters, field[z : z + 3].reshape(1728, 256))
        s = sigmoid(pre)
        cell = (low, 1, 2 - low)[(z + 1) // 2]
        wide = dot(got[:, cell, 64:80].reshape(128, 128), spread)
        delta = wide * slope_of(pre, s)
        deltas.append(delta.astype(BF))
        if z in (1, 2):
            own[z - 1] = jnp.where(mine, delta, 0.0).astype(BF)
            a = act_of(pre, s)
            pooled = a if pooled is None else pooled + a
    high = pooled.astype(BF)
    low = (pooled - high.astype(F32)).astype(BF)
    p4[...] = dot(high, pool4[...]) + dot(low, pool4[...])

    stacked = jnp.concatenate(deltas, axis=0)
    for k in range(9):
        moved = dot(stacked, shift4[:, k * 256 : k * 256 + 256]).astype(BF)
        for z in range(4):
            back_in[z, k * 128 : k * 128 + 128] = moved[z * 128 : z * 128 + 128]
    filters = w4b[...]
    back = [
        dot(filters, back_in[z : z + 3].reshape(3456, 256)).astype(BF) for z in range(2)
    ]
    spread_copy.wait()
    sl3_copy.wait()
    wide = dot(jnp.concatenate(back, axis=1), spread3[...])
    for r in range(6):
        yg = 4 * ch + r - 1
        inside = jnp.logical_and(yg >= 0, yg < 32)
        lanes = slice(r * 128, r * 128 + 128)
        value = jnp.where(inside, wide[:, lanes], 0.0)
        for zp in range(2):
            d3[zp, :, lanes] = (value * sl3[zp, :, lanes].astype(F32)).astype(BF)
    near_out[...] = d3[1 - odd]
    far_out[...] = d3[odd]


def grads_kernel(pos, field, own, d3, p4, vq_far, sent, out, vq, sems):
    vq_copy = pltpu.make_async_copy(vq_far, vq, sems.at[0])
    vq_copy.start()
    right = jnp.concatenate([own[0], own[1]], axis=1)
    for kz in range(3):
        left = jnp.concatenate([field[1 + kz], field[2 + kz]], axis=1)
        res = dot_nt(left, right)
        for k in range(9):
            for c in range(8):
                at = (kz * 9 + k) * 8
                out[c, at : at + 8] = res[k * 64 + c * 8 : k * 64 + c * 8 + 8]
    vq_copy.wait()
    total = None
    zero = jnp.zeros((64, 512), BF)
    for j in range(4):
        rows = []
        for kz in range(3):
            zp = j - kz
            rows.append(d3[zp, :, 128:640] if 0 <= zp < 2 else zero)
        left = jnp.concatenate(
            [vq[j, :, (1 + ky) * 128 : (1 + ky) * 128 + 512] for ky in range(3)], axis=0
        )
        res = dot_nt(left, jnp.concatenate(rows, axis=0))
        total = res if total is None else total + res
    for k in range(9):
        for c in range(8):
            at = 216 + k * 4
            piece = total[k * 32 + c * 4 : k * 32 + c * 4 + 4]
            out[c, at : at + 4] = piece[:, :128]
            out[c, at + 36 : at + 40, 0:64] = piece[:, 128:]
    for c in range(8):
        out[c, 252:288, 64:128] = jnp.zeros((36, 64), F32)
        out[c, 288:304] = p4[c * 16 : c * 16 + 16]
        sent[c] = out[c].astype(BF)


def shallow_back_kernel(
    pos, d3, near, far, w3b, straight, cross, spread2, sl2_far, vx_far,
    g2, ds, d2, sl2, vx, sems,
):
    sl2_copy, vx_copy = copies(
        ((sl2_far, sl2), (vx_far, vx)), sems
    )

    def rows_of(ref, lead=None):
        parts = []
        for y in range(6):
            lanes = slice(y * 128, y * 128 + 128)
            parts.append(ref[:, lanes] if lead is None else ref[lead, :, lanes])
        return jnp.concatenate(parts, axis=0)

    odd = pos[0] % 2 == 1
    one, two = rows_of(near).astype(F32), rows_of(far).astype(F32)
    above = jnp.where(odd, one, two).astype(BF)
    below = jnp.where(odd, two, one).astype(BF)
    first, second = rows_of(d3, 0), rows_of(d3, 1)
    direct, across = straight[...], cross[...]
    sources = (
        (jnp.concatenate([above, second], axis=1), across),
        (first, direct),
        (second, direct),
        (jnp.concatenate([first, below], axis=1), across),
    )
    for j, (source, matrix) in enumerate(sources):
        moved = dot(source, matrix).astype(BF)
        for y in range(6):
            for kx in range(3):
                piece = moved[y * 64 : y * 64 + 64, kx * 128 : kx * 128 + 128]
                ds[j, kx * 64 : kx * 64 + 64, y * 128 : y * 128 + 128] = piece

    for z in (0, 1, 10, 11):
        d2[z] = jnp.zeros((32, 1024), BF)
    filters = w3b[...]
    backs = []
    for zp in range(2):
        for q in range(2):
            rhs = jnp.concatenate(
                [
                    ds[zp + kz, :, (2 * q + ky) * 128 : (2 * q + ky + 2) * 128]
                    for kz in range(3)
                    for ky in range(3)
                ],
                axis=0,
            )
            back = dot(filters, rhs).astype(BF)
            backs += [back[:, :128], back[:, 128:]]
    wide = dot(jnp.concatenate(backs, axis=0), spread2[...])
    sl2_copy.wait()
    for zp in range(2):
        for y in range(4):
            at = (zp * 4 + y) * 32
            for h in range(2):
                value = wide[at : at + 32, h * 128 : h * 128 + 128]
                z = zp + 2 * h
                for dz in range(2):
                    for dy in range(2):
                        rows = slice((dz * 2 + dy) * 32, (dz * 2 + dy) * 32 + 32)
                        slope = sl2[z, rows, y * 128 : y * 128 + 128].astype(F32)
                        lanes = slice((2 * y + dy) * 128, (2 * y + dy) * 128 + 128)
                        d2[2 * z + dz + 2, :, lanes] = (value * slope).astype(BF)

    vx_copy.wait()
    total = None
    for z in range(10):
        left = jnp.concatenate(
            [vx[z, :, ky * 128 : ky * 128 + 1024] for ky in range(3)], axis=0
        )
        right = jnp.concatenate([d2[z + 2 - kz] for kz in range(3)], axis=0)
        part = dot_nt(left, right)
        total = part if total is None else total + part
    g2[...] = jnp.zeros((160, 128), F32)
    g2[0:144, 0:96] = total


def write_kernel(pos, whole, four, three, two):
    deep = whole[:, 0:9].astype(F32).reshape(288, 128)
    four[...] = deep[:216]
    for k in range(9):
        low = deep[216 + k * 4 : 220 + k * 4]
        high = deep[252 + k * 4 : 256 + k * 4]
        three[k] = low[:, 0:64]
        three[9 + k] = low[:, 64:128]
        three[18 + k] = high[:, 0:64]
    shallow = whole[:, 9:14].astype(F32).reshape(160, 128)
    for kz in range(3):
        two[kz] = shallow[:144, kz * 32 : kz * 32 + 32]


def swap(one, two, axis):
    count = lax.axis_size(axis)
    inside = [(i, i ^ 1) for i in range(count)]
    outside = [(i, i + 1) for i in range(1, count - 1, 2)]
    outside = outside + [(b, a) for a, b in outside]
    return lax.ppermute(one, axis, inside), lax.ppermute(two, axis, outside)


def to_all(piece, axis):
    count = lax.axis_size(axis)
    copies = jnp.broadcast_to(piece[None], (count,) + piece.shape)
    return lax.all_to_all(copies, axis, 0, 0, tiled=True)


def band(filters):
    taps = filters.transpose(0, 2, 3, 4, 1).reshape(32, 3, 3, 48)
    rows = [
        jnp.pad(taps, ((0, 0), (dz, 1 - dz), (dy, 1 - dy), (0, 0)))
        for dz in range(2)
        for dy in range(2)
    ]
    return jnp.stack(rows).reshape(128, 768)


def body(volume, filters_two, filters_three, filters_four, cotangent):
    gz, ch = lax.axis_index("gz"), lax.axis_index("ch")
    pos = jnp.stack([gz, ch]).astype(jnp.int32)
    odd_z, odd_y = gz % 2, ch % 2
    shape = jax.ShapeDtypeStruct

    field = volume.transpose(1, 2, 0, 3)
    near, far = swap(
        lax.dynamic_slice_in_dim(field, 3 * (1 - odd_y), 5, 1),
        lax.dynamic_slice_in_dim(field, 3 * odd_y, 5, 1),
        "ch",
    )
    low = jnp.where(odd_y == 1, near, far)
    high = jnp.where(odd_y == 1, far, near)
    mid = jnp.concatenate([low, field, high], axis=1)
    near, far = swap(
        lax.dynamic_slice_in_dim(mid, 5 * (1 - odd_z), 3, 0),
        lax.dynamic_slice_in_dim(mid, 5 * odd_z, 3, 0),
        "gz",
    )
    w2 = band(filters_two)

    four = filters_four.transpose(2, 3, 4, 1, 0).reshape(216, 128)
    three = filters_three.transpose(2, 3, 4, 1, 0).reshape(108, 64)
    three = jnp.pad(three, ((0, 0), (0, 64)))
    held = jnp.concatenate([four, three], axis=0)
    near, far, held, w2 = lax.optimization_barrier((near, far, held, w2))
    all_of = to_all(held, "ch")
    four = all_of[:, :216].reshape(8, 27, 8, 128)
    three = all_of[:, 216:324, :64].reshape(8, 27, 4, 64)
    w3f = three.transpose(3, 1, 0, 2).reshape(64, 864)
    w3b = three[:, ::-1].transpose(0, 2, 1, 3).reshape(32, 1728)
    w4f = four.transpose(3, 1, 0, 2).reshape(128, 1728)
    w4b = four[:, ::-1].transpose(0, 2, 1, 3).reshape(64, 3456)

    vq, sl2, vx = call(
        shallow_forward_kernel,
        (
            shape((4, 96, 1024), BF),
            shape((4, 128, 512), BF),
            shape((10, 48, 1280), BF),
        ),
        [
            pltpu.VMEM((6, 256, 128), BF),
            pltpu.VMEM((6, 128, 512), BF),
            pltpu.VMEM((14, 48, 2304), BF),
            pltpu.SemaphoreType.DMA((2,)),
        ],
        1 << 32,
        (
            pos, near, mid, far, w2,
            const(shift_rows), const(pool_two), const(shift_halves),
        ),
        far_out=(1, 2),
    )
    p3, sl3, vq = call(
        middle_forward_kernel,
        (shape((64, 128), BF), shape((2, 64, 768), BF), shape((4, 96, 1024), BF)),
        [pltpu.VMEM((2, 64, 768), BF), pltpu.SemaphoreType.DMA((2,))],
        1 << 30,
        (pos, vq, w3f, const(pool_three)),
        far_out=(1, 2),
    )
    cot = cotangent.reshape(16, 128)
    sent = jnp.concatenate([p3, cot], axis=0)
    near, far = swap(sent, sent, "gz")
    got = to_all(jnp.stack([near, sent, far]), "ch")
    p4, d3, near, far, field4, own4 = call(
        deep_kernel,
        (
            shape((128, 128), F32),
            shape((2, 64, 768), BF),
            shape((64, 768), BF),
            shape((64, 768), BF),
            shape((6, 576, 256), BF),
            shape((2, 128, 256), BF),
        ),
        [
            pltpu.VMEM((384, 256), BF),
            pltpu.VMEM((4, 1152, 256), BF),
            pltpu.VMEM((2, 64, 768), BF),
            pltpu.VMEM((640, 512), BF),
            pltpu.VMEM((256, 2304), BF),
            pltpu.VMEM((512, 768), BF),
            pltpu.SemaphoreType.DMA((4,)),
        ],
        1 << 32,
        (
            pos, got, w4f, w4b, const(pool_four), w3b, sl3, const(deep_matrices),
        ),
        far_in=(5, 6, 7),
    )
    near, far = swap(near, far, "gz")
    (sent,) = call(
        grads_kernel,
        (shape((8, 304, 128), BF),),
        [
            pltpu.VMEM((8, 304, 128), F32),
            pltpu.VMEM((4, 96, 1024), BF),
            pltpu.SemaphoreType.DMA((1,)),
        ],
        1 << 31,
        (pos, field4, own4, d3, p4, vq),
        far_in=(5,),
    )
    near, far, sent = lax.optimization_barrier((near, far, sent))
    got = lax.all_to_all(sent, "ch", 0, 0, tiled=True)
    grads = got[:, :288].astype(F32).sum(axis=0).astype(BF)
    pooled_four = got[:, 288:, :16].transpose(1, 0, 2)[:, None]

    (g2,) = call(
        shallow_back_kernel,
        (shape((160, 128), F32),),
        [
            pltpu.VMEM((4, 192, 768), BF),
            pltpu.VMEM((12, 32, 1024), BF),
            pltpu.VMEM((4, 128, 512), BF),
            pltpu.VMEM((10, 48, 1280), BF),
            pltpu.SemaphoreType.DMA((2,)),
        ],
        1 << 32,
        (
            pos, d3, near, far, w3b,
            const(shift_straight), const(shift_cross), const(spread_two), sl2, vx,
        ),
        far_in=(8, 9),
    )
    pieces = jnp.concatenate(
        [grads.reshape(32, 9, 128), g2.astype(BF).reshape(32, 5, 128)], axis=1
    )
    pieces = lax.all_to_all(pieces, "gz", 0, 0, tiled=True).astype(F32).sum(axis=0)
    two = to_all(pieces[9:].astype(BF), "ch").astype(F32).sum(axis=0)
    whole = to_all(jnp.concatenate([pieces[:9], two], axis=0).astype(BF), "gz")
    four, three, two = call(
        write_kernel,
        (shape((216, 128), F32), shape((27, 4, 64), F32), shape((3, 144, 32), F32)),
        [],
        1 << 20,
        (pos, whole),
    )
    grad_four = four.reshape(3, 3, 3, 8, 128).transpose(4, 3, 0, 1, 2)
    grad_three = three.reshape(3, 3, 3, 4, 64).transpose(4, 3, 0, 1, 2)
    grad_two = two.reshape(3, 3, 3, 16, 32).transpose(4, 3, 0, 1, 2)
    return (pooled_four, grad_two, grad_three, grad_four)


def solution(mesh):
    in_specs = (
        P(None, "gz", "ch", None),
        P(),
        P(None, "ch", None, None, None),
        P(None, "ch", None, None, None),
        P("ch", "gz", None, None),
    )
    out_specs = (
        P("ch", "gz", None, None),
        P(),
        P(None, "ch", None, None, None),
        P(None, "ch", None, None, None),
    )
    return jax.shard_map(body, mesh=mesh, in_specs=in_specs, out_specs=out_specs, check_vma=False)
```

```python
import jax
import jax.numpy as jnp
import numpy as np
from jax import lax
from jax.experimental import pallas as pl
from jax.experimental.pallas import tpu as pltpu
from jax.sharding import PartitionSpec as P

BF = jnp.bfloat16
F32 = jnp.float32
VMEM_LIMIT = 12 * 1024 * 1024


def grid(*extents):
    return np.meshgrid(*[np.arange(n) for n in extents], indexing="ij")


def shift_rows():
    out = np.zeros((128, 2, 128), np.float32)
    for x in range(128):
        if x > 0:
            out[x - 1, 0, x] = 1
        if x < 127:
            out[x + 1, 1, x] = 1
    return out.reshape(128, 256)


def shift_halves():
    out = np.zeros((2, 64, 2, 2, 64), np.float32)
    for h in range(2):
        for x in range(64):
            if x > 0:
                out[h, x - 1, 0, h, x] = 1
            if x < 63:
                out[h, x + 1, 1, h, x] = 1
    return out.reshape(128, 256)


def shift_straight():
    side = shift_halves()
    return np.concatenate([side[:, :128], np.eye(128, dtype=np.float32), side[:, 128:]], 1)


def shift_cross():
    straight = shift_straight()
    out = np.zeros((256, 384), np.float32)
    out[64:128] = straight[0:64]
    out[128:192] = straight[64:128]
    return out


def pool_two():
    out = np.zeros((2, 64, 2, 2, 64), np.float32)
    for h in range(2):
        for x in range(64):
            out[h, x, :, h, x] = 0.125
    return out.reshape(256, 128)


def pool_three():
    out = np.zeros((2, 2, 32, 2, 2, 2, 32), np.float32)
    for yc in range(2):
        for zc in range(2):
            for x in range(32):
                out[yc, zc, x, :, zc, yc, x] = 0.125
    return out.reshape(256, 128)


def gather_planes():
    out = np.zeros((5, 2, 2, 32, 2, 8, 32), np.float32)
    for b in range(5):
        for yy in range(2):
            y = 2 * b + yy - 1
            if 0 <= y < 8:
                for zz in range(2):
                    for x in range(32):
                        out[b, zz, yy, x, zz, y, x] = 1
    return out.reshape(640, 512)


def shift_planes():
    out = np.zeros((8, 32, 3, 3, 8, 32), np.float32)
    for ky in range(3):
        for kx in range(3):
            for y in range(8):
                for x in range(32):
                    sy, sx = y + ky, x + kx - 1
                    if sy < 8 and 0 <= sx < 32:
                        out[sy, sx, ky, kx, y, x] = 1
    return out.reshape(256, 2304)


def pool_four():
    out = np.zeros((8, 16, 2, 128), np.float32)
    for x in range(16):
        out[2:4, x, :, x] = 0.125
    return out.reshape(256, 128)


def spread_three():
    out = np.zeros((2, 8, 32, 6, 2, 32, 2), np.float32)
    for r in range(6):
        cell = (r - 1) // 2 + 1
        for h in range(2):
            for x in range(32):
                out[h, cell, x, r, h, x, :] = 0.125
    return out.reshape(512, 768)


def spread_two():
    out = np.zeros((2, 64, 2, 64, 2), np.float32)
    for h in range(2):
        for x in range(64):
            out[h, x, h, x, :] = 0.125
    return out.reshape(128, 256)


def deep_matrices():
    out = np.zeros((768, 2304), np.float32)
    out[:256] = shift_planes()
    out[256:768, :768] = spread_three()
    return out


def const(build):
    return jnp.asarray(build(), BF)


def dot(a, b):
    return lax.dot_general(a, b, (((1,), (0,)), ((), ())), preferred_element_type=F32)


def dot_nt(a, b):
    return lax.dot_general(a, b, (((1,), (1,)), ((), ())), preferred_element_type=F32)


def sigmoid(u):
    return 0.5 * jnp.tanh(0.5 * u) + 0.5


def act_of(u, s):
    return u * (0.3 + 0.7 * s)


def slope_of(u, s):
    return 0.3 + 0.7 * (s + u * s * (1.0 - s))


def call(kernel, out_shape, scratch, flops, args, far_in=(), far_out=()):
    def place(far):
        return pl.BlockSpec(memory_space=pltpu.HBM if far else pltpu.VMEM)

    specs = [pl.BlockSpec(memory_space=pltpu.SMEM)] + [
        place(n in far_in) for n in range(1, len(args))
    ]
    args = [
        pltpu.with_memory_space_constraint(a, pltpu.HBM) if n in far_in else a
        for n, a in enumerate(args)
    ]
    return pl.pallas_call(
        kernel,
        out_shape=tuple(
            pltpu.HBM(o.shape, o.dtype) if n in far_out else o for n, o in enumerate(out_shape)
        ),
        in_specs=specs,
        out_specs=tuple(place(n in far_out) for n in range(len(out_shape))),
        scratch_shapes=scratch,
        compiler_params=pltpu.CompilerParams(vmem_limit_bytes=VMEM_LIMIT),
        cost_estimate=pl.CostEstimate(flops=flops, bytes_accessed=1 << 20, transcendentals=0),
    )(*args)


def copies(pairs, sems):
    out = [pltpu.make_async_copy(a, b, sems.at[n]) for n, (a, b) in enumerate(pairs)]
    for copy in out:
        copy.start()
    return out


def shallow_forward_kernel(
    pos, near, mid, far, w2, shift2, pool2, shift3, vq, sl2_far, vx_far, sums, sl2, vx, sems
):
    gz, ch = pos[0], pos[1]
    shift = shift2[...]

    odd = gz % 2 == 1
    for which, first, count in ((0, 0, 3), (1, 3, 8), (2, 11, 3)):

        @pl.loop(0, count, unroll=2 if count == 8 else 3)
        def _(z):
            if which == 1:
                field = mid[z].reshape(224, 128)
            else:
                one, two = near[z].reshape(224, 128), far[z].reshape(224, 128)
                if which == 2:
                    one, two = two, one
                field = jnp.where(odd, one.astype(F32), two.astype(F32)).astype(BF)
            sides = dot(field, shift)
            for y in range(14):
                lanes = slice(y * 128, y * 128 + 128)
                rows = slice(y * 16, y * 16 + 16)
                vx[z + first, 0:16, lanes] = sides[rows, :128].astype(BF)
                vx[z + first, 16:32, lanes] = field[rows]
                vx[z + first, 32:48, lanes] = sides[rows, 128:].astype(BF)

    vx_copy = pltpu.make_async_copy(
        vx.at[2:12, :, 256:1536], vx_far, sems.at[0]
    )
    vx_copy.start()
    filters = w2[...]

    @pl.loop(0, 6, unroll=2)
    def _(zc):
        zg = 4 * gz + zc - 1
        z_in = jnp.logical_and(zg >= 0, zg < 128)
        for q, (ya, yb) in enumerate(((1, 2), (3, 4), (0, 5))):
            rhs = jnp.concatenate(
                [
                    jnp.concatenate(
                        [
                            vx[2 * zc + zz, :, (2 * ya + yy) * 128 : (2 * ya + yy + 1) * 128],
                            vx[2 * zc + zz, :, (2 * yb + yy) * 128 : (2 * yb + yy + 1) * 128],
                        ],
                        axis=1,
                    )
                    for zz in range(4)
                    for yy in range(4)
                ],
                axis=0,
            )
            pre = dot(filters, rhs)
            s = sigmoid(pre)
            a = act_of(pre, s)
            if q < 2:
                sl2[zc, :, q * 256 : q * 256 + 256] = slope_of(pre, s).astype(BF)
            total = (a[0:32] + a[32:64]) + (a[64:96] + a[96:128])
            for c, yc in enumerate((ya, yb)):
                yg = 4 * ch + yc - 1
                inside = jnp.logical_and(z_in, jnp.logical_and(yg >= 0, yg < 32))
                cell = jnp.where(inside, total[:, c * 128 : c * 128 + 128], 0.0)
                sums[zc, yc * 32 : yc * 32 + 32] = cell.astype(BF)

    sl2_copy = pltpu.make_async_copy(sl2.at[1:5], sl2_far, sems.at[1])
    sl2_copy.start()
    pool = pool2[...]
    halves = shift3[...]
    for j in range(4):
        pair = jnp.concatenate([sums[j], sums[j + 2]], axis=1)
        pooled = dot(pair, pool).astype(BF)
        sides = dot(pooled, halves)
        for y in range(6):
            rows = slice(y * 32, y * 32 + 32)
            lanes = slice(y * 128, y * 128 + 128)
            vq[j, 0:32, lanes] = sides[rows, :128].astype(BF)
            vq[j, 32:64, lanes] = pooled[rows]
            vq[j, 64:96, lanes] = sides[rows, 128:].astype(BF)
    vx_copy.wait()
    sl2_copy.wait()


def middle_forward_kernel(pos, vq, w3, pool3, cot, sent, edges, sl3):
    sent[64:192] = cot[...]
    filters = w3[...]
    cells = [None, None]
    for zp in range(2):
        for n in range(2):
            blocks = [
                vq[zp + kz, :, (2 * n + ky) * 128 : (2 * n + ky + 2) * 128]
                for kz in range(3)
                for ky in range(3)
            ]
            pre = dot(filters, jnp.concatenate(blocks, axis=0))
            s = sigmoid(pre)
            sl3[zp, :, n * 256 : n * 256 + 256] = slope_of(pre, s).astype(BF)
            a = act_of(pre, s)
            part = a[:, :128] + a[:, 128:]
            cells[n] = part if zp == 0 else cells[n] + part
    both = jnp.concatenate(cells, axis=1).astype(BF)
    sent[0:64] = dot(both, pool3[...]).astype(BF)
    odd = pos[1] % 2
    for zp in range(2):
        top, bottom = sl3[zp, :, 384:512], sl3[zp, :, 0:128]
        edges[odd, zp * 64 : zp * 64 + 64] = top
        edges[1 - odd, zp * 64 : zp * 64 + 64] = bottom


def deep_kernel(
    pos, own3, near, far, in1, out1, in2, out2, w4f, w4b, pool4, sl3, planes_of, w3b, matrices,
    p4, d3, near_out, far_out, field, own,
    planes, back_in, shift4, spread3, sems,
):
    shift_copy, spread_copy = copies(
        ((matrices.at[0:256], shift4), (matrices.at[256:768, 0:768], spread3)), sems
    )
    odd, ch = pos[0] % 2, pos[1]

    def pick(cond, one, two):
        return jnp.where(cond, one.astype(F32), two.astype(F32)).astype(BF)

    def in_order(blocks):
        first, second, third = blocks
        return [pick(odd == 1, first, third), second, pick(odd == 1, third, first)]

    def neighbour(inside, outside, upper, rows):
        one, two = inside[rows], outside[rows]
        return pick(upper, one, two), pick(upper, two, one)

    odd_y, odd_pair = ch % 2 == 1, ch % 4 >= 2
    mine = jnp.concatenate([near[0:64], own3[0:64], far[0:64]], axis=0)
    below1, above1 = neighbour(in1, out1, odd_y, slice(0, 192))
    below2, above2 = neighbour(in2, out2, odd_pair, slice(0, 192))
    parts = [
        jnp.concatenate(in_order([p[0:64], p[64:128], p[128:192]]), axis=0)
        for p in (below2, below1, mine, above1, above2)
    ]
    cots = in_order([near[64:192], own3[64:192], far[64:192]])
    edge_low, edge_high = neighbour(in1, out1, odd_y, slice(192, 320))
    flat = dot(jnp.concatenate(parts, axis=1), planes_of[...]).astype(BF)
    for zb in range(3):
        for zz in range(2):
            p = 2 * zb + zz
            planes[p * 64 : p * 64 + 64] = flat[zb * 64 : zb * 64 + 64, zz * 256 : zz * 256 + 256]
    shift_copy.wait()
    for k in range(9):
        moved = dot(planes[...], shift4[:, k * 256 : k * 256 + 256]).astype(BF)
        for p in range(6):
            field[p, k * 64 : k * 64 + 64] = moved[p * 64 : p * 64 + 64]

    row = lax.broadcasted_iota(jnp.int32, (128, 256), 0)
    lane = lax.broadcasted_iota(jnp.int32, (128, 256), 1)
    source_y, source_x = row // 16, row % 16
    y, x = lane // 32, lane % 32
    match = (source_x == x // 2) & (source_y == ch - 1 + y // 2) & (y < 6)
    spread = jnp.where(match, 0.125, 0.0).astype(BF)
    inner = lax.broadcasted_iota(jnp.int32, (128, 256), 1) // 64 == 1

    filters = w4f[...]
    pooled = None
    deltas = []
    for z in range(4):
        pre = dot(filters, field[z : z + 3].reshape(1728, 256))
        s = sigmoid(pre)
        wide = dot(cots[(z + 1) // 2], spread)
        delta = wide * slope_of(pre, s)
        deltas.append(delta.astype(BF))
        if z in (1, 2):
            own[z - 1] = jnp.where(inner, delta, 0.0).astype(BF)
            a = act_of(pre, s)
            pooled = a if pooled is None else pooled + a
    high = pooled.astype(BF)
    low = (pooled - high.astype(F32)).astype(BF)
    p4[...] = dot(high, pool4[...]) + dot(low, pool4[...])

    stacked = jnp.concatenate(deltas, axis=0)
    for k in range(9):
        moved = dot(stacked, shift4[:, k * 256 : k * 256 + 256]).astype(BF)
        for z in range(4):
            back_in[z, k * 128 : k * 128 + 128] = moved[z * 128 : z * 128 + 128]
    filters = w4b[...]
    back = [
        dot(filters, back_in[z : z + 3].reshape(3456, 256)).astype(BF) for z in range(2)
    ]
    spread_copy.wait()
    wide = dot(jnp.concatenate(back, axis=1), spread3[...])
    for r in range(6):
        yg = 4 * ch + r - 1
        inside = jnp.logical_and(yg >= 0, yg < 32)
        lanes = slice(r * 128, r * 128 + 128)
        value = jnp.where(inside, wide[:, lanes], 0.0)
        for zp in range(2):
            rows = slice(zp * 64, zp * 64 + 64)
            if r == 0:
                slope = edge_low[rows]
            elif r == 5:
                slope = edge_high[rows]
            else:
                slope = sl3[zp, :, (r - 1) * 128 : r * 128]
            d3[zp, :, lanes] = (value * slope.astype(F32)).astype(BF)
    near_out[...] = d3[1 - odd]
    far_out[...] = d3[odd]


def grads_kernel(pos, field, own, d3, p4, vq, sent, out):
    right = jnp.concatenate([own[0], own[1]], axis=1)
    for kz in range(3):
        left = jnp.concatenate([field[1 + kz], field[2 + kz]], axis=1)
        res = dot_nt(left, right)
        for k in range(9):
            for c in range(8):
                at = (kz * 9 + k) * 8
                out[c, at : at + 8] = res[k * 64 + c * 8 : k * 64 + c * 8 + 8]
    total = None
    zero = jnp.zeros((64, 512), BF)
    for j in range(4):
        rows = []
        for kz in range(3):
            zp = j - kz
            rows.append(d3[zp, :, 128:640] if 0 <= zp < 2 else zero)
        left = jnp.concatenate(
            [vq[j, :, ky * 128 : ky * 128 + 512] for ky in range(3)], axis=0
        )
        res = dot_nt(left, jnp.concatenate(rows, axis=0))
        total = res if total is None else total + res
    for k in range(9):
        for c in range(8):
            at = 216 + k * 4
            piece = total[k * 32 + c * 4 : k * 32 + c * 4 + 4]
            out[c, at : at + 4] = piece[:, :128]
            at, lanes = (252 + k * 4, slice(0, 64)) if k < 5 else (232 + k * 4, slice(64, 128))
            out[c, at : at + 4, lanes] = piece[:, 128:]
    for c in range(8):
        out[c, 268:272, 64:128] = jnp.zeros((4, 64), F32)
        out[c, 272:288] = p4[c * 16 : c * 16 + 16]
        sent[c] = out[c].astype(BF)


def shallow_back_kernel(
    pos, d3, near, far, w3b, straight, cross, spread2, sl2, vx_far,
    g2, ds, d2, vx, sems,
):
    vx_copy = pltpu.make_async_copy(vx_far, vx, sems.at[0])
    vx_copy.start()

    def rows_of(ref, lead=None):
        parts = []
        for y in range(6):
            lanes = slice(y * 128, y * 128 + 128)
            parts.append(ref[:, lanes] if lead is None else ref[lead, :, lanes])
        return jnp.concatenate(parts, axis=0)

    odd = pos[0] % 2 == 1
    one, two = rows_of(near).astype(F32), rows_of(far).astype(F32)
    above = jnp.where(odd, one, two).astype(BF)
    below = jnp.where(odd, two, one).astype(BF)
    first, second = rows_of(d3, 0), rows_of(d3, 1)
    direct, across = straight[...], cross[...]
    sources = (
        (jnp.concatenate([above, second], axis=1), across),
        (first, direct),
        (second, direct),
        (jnp.concatenate([first, below], axis=1), across),
    )
    for j, (source, matrix) in enumerate(sources):
        moved = dot(source, matrix).astype(BF)
        for y in range(6):
            for kx in range(3):
                piece = moved[y * 64 : y * 64 + 64, kx * 128 : kx * 128 + 128]
                ds[j, kx * 64 : kx * 64 + 64, y * 128 : y * 128 + 128] = piece

    for z in (0, 1, 10, 11):
        d2[z] = jnp.zeros((32, 1024), BF)
    filters = w3b[...]
    backs = []
    for zp in range(2):
        for q in range(2):
            rhs = jnp.concatenate(
                [
                    ds[zp + kz, :, (2 * q + ky) * 128 : (2 * q + ky + 2) * 128]
                    for kz in range(3)
                    for ky in range(3)
                ],
                axis=0,
            )
            back = dot(filters, rhs).astype(BF)
            backs += [back[:, :128], back[:, 128:]]
    wide = dot(jnp.concatenate(backs, axis=0), spread2[...])
    for zp in range(2):
        for y in range(4):
            at = (zp * 4 + y) * 32
            for h in range(2):
                value = wide[at : at + 32, h * 128 : h * 128 + 128]
                z = zp + 2 * h
                for dz in range(2):
                    for dy in range(2):
                        rows = slice((dz * 2 + dy) * 32, (dz * 2 + dy) * 32 + 32)
                        slope = sl2[z, rows, y * 128 : y * 128 + 128].astype(F32)
                        lanes = slice((2 * y + dy) * 128, (2 * y + dy) * 128 + 128)
                        d2[2 * z + dz + 2, :, lanes] = (value * slope).astype(BF)

    vx_copy.wait()
    total = None
    for z in range(10):
        left = jnp.concatenate(
            [vx[z, :, ky * 128 : ky * 128 + 1024] for ky in range(3)], axis=0
        )
        right = jnp.concatenate([d2[z + 2 - kz] for kz in range(3)], axis=0)
        part = dot_nt(left, right)
        total = part if total is None else total + part
    g2[...] = jnp.zeros((160, 128), F32)
    g2[0:144, 0:96] = total


def write_kernel(pos, whole, four, three, two):
    deep = whole[:, 0:9].astype(F32).reshape(288, 128)
    four[...] = deep[:216]
    for k in range(9):
        low = deep[216 + k * 4 : 220 + k * 4]
        at, lanes = (252 + k * 4, slice(0, 64)) if k < 5 else (232 + k * 4, slice(64, 128))
        high = deep[at : at + 4, lanes]
        three[k] = low[:, 0:64]
        three[9 + k] = low[:, 64:128]
        three[18 + k] = high
    shallow = whole[:, 9:14].astype(F32).reshape(160, 128)
    for kz in range(3):
        two[kz] = shallow[:144, kz * 32 : kz * 32 + 32]


def swap(one, two, axis, step=1):
    count = lax.axis_size(axis)
    inside = [(i, i ^ step) for i in range(count)]
    outside = [(i, i + step) for i in range(count - step) if i % (2 * step) >= step]
    outside = outside + [(b, a) for a, b in outside]
    return lax.ppermute(one, axis, inside), lax.ppermute(two, axis, outside)


def swap_cores(value):
    return lax.ppermute(value, "gz", [(i, i ^ 1) for i in range(lax.axis_size("gz"))])


def to_all(piece, axis):
    count = lax.axis_size(axis)
    copies = jnp.broadcast_to(piece[None], (count,) + piece.shape)
    return lax.all_to_all(copies, axis, 0, 0, tiled=True)


def band(filters):
    taps = filters.transpose(0, 2, 3, 4, 1).reshape(32, 3, 3, 48)
    rows = [
        jnp.pad(taps, ((0, 0), (dz, 1 - dz), (dy, 1 - dy), (0, 0)))
        for dz in range(2)
        for dy in range(2)
    ]
    return jnp.stack(rows).reshape(128, 768)


def body(volume, filters_two, filters_three, filters_four, cotangent):
    gz, ch = lax.axis_index("gz"), lax.axis_index("ch")
    pos = jnp.stack([gz, ch]).astype(jnp.int32)
    odd_z, odd_y = gz % 2, ch % 2
    shape = jax.ShapeDtypeStruct

    field = volume.transpose(1, 2, 0, 3)
    near, far = swap(
        lax.dynamic_slice_in_dim(volume, 5 * (1 - odd_y), 3, 2).transpose(1, 2, 0, 3),
        lax.dynamic_slice_in_dim(volume, 5 * odd_y, 3, 2).transpose(1, 2, 0, 3),
        "ch",
    )
    low = jnp.where(odd_y == 1, near, far)
    high = jnp.where(odd_y == 1, far, near)
    mid = jnp.concatenate([low, field, high], axis=1)

    four = filters_four.transpose(2, 3, 4, 1, 0).reshape(216, 128)
    three = filters_three.transpose(2, 3, 4, 1, 0).reshape(108, 64)
    three = jnp.pad(three, ((0, 0), (0, 64)))
    cot = cotangent.reshape(16, 128)
    held = jnp.concatenate(
        [
            cot,
            lax.dynamic_slice_in_dim(four, 108 * odd_z, 108, 0),
            lax.dynamic_slice_in_dim(three, 54 * odd_z, 54, 0),
        ],
        axis=0,
    )
    held = jnp.broadcast_to(held[None], (8, 178, 128))
    w2 = band(filters_two)
    mid, held = lax.optimization_barrier((mid, held))
    near, far = swap(
        lax.dynamic_slice_in_dim(mid, 5 * (1 - odd_z), 3, 0),
        lax.dynamic_slice_in_dim(mid, 5 * odd_z, 3, 0),
        "gz",
    )
    all_of = lax.all_to_all(held, "ch", 0, 0, tiled=True)
    cots = all_of[:, :16].reshape(128, 128)
    mine, w2 = lax.optimization_barrier((all_of[:, 16:], w2))
    other = swap_cores(mine)
    first = jnp.where(odd_z == 1, other, mine)
    second = jnp.where(odd_z == 1, mine, other)
    four = jnp.concatenate([first[:, :108], second[:, :108]], axis=1).reshape(8, 27, 8, 128)
    three = jnp.concatenate([first[:, 108:, :64], second[:, 108:, :64]], axis=1)
    three = three.reshape(8, 27, 4, 64)
    w3f = three.transpose(3, 1, 0, 2).reshape(64, 864)
    w3b = three[:, ::-1].transpose(0, 2, 1, 3).reshape(32, 1728)
    w4f = four.transpose(3, 1, 0, 2).reshape(128, 1728)
    w4b = four[:, ::-1].transpose(0, 2, 1, 3).reshape(64, 3456)

    vq, sl2, vx = call(
        shallow_forward_kernel,
        (
            shape((4, 96, 768), BF),
            shape((4, 128, 512), BF),
            shape((10, 48, 1280), BF),
        ),
        [
            pltpu.VMEM((6, 192, 128), BF),
            pltpu.VMEM((6, 128, 512), BF),
            pltpu.VMEM((14, 48, 1792), BF),
            pltpu.SemaphoreType.DMA((2,)),
        ],
        1 << 32,
        (
            pos, near, mid, far, w2,
            const(shift_rows), const(pool_two), const(shift_halves),
        ),
        far_out=(1, 2),
    )
    sent, edges, sl3 = call(
        middle_forward_kernel,
        (
            shape((192, 128), BF),
            shape((2, 128, 128), BF),
            shape((2, 64, 512), BF),
        ),
        [],
        1 << 30,
        (pos, vq, w3f, const(pool_three), cots),
    )
    near, far = swap(sent, sent, "gz")
    planes = jnp.concatenate([near[:64], sent[:64], far[:64]], axis=0)
    in1, out1 = swap(
        jnp.concatenate([planes, edges[0]], axis=0),
        jnp.concatenate([planes, edges[1]], axis=0),
        "ch",
    )
    in2, out2 = swap(planes, planes, "ch", 2)
    p4, d3, near, far, field4, own4 = call(
        deep_kernel,
        (
            shape((128, 128), F32),
            shape((2, 64, 768), BF),
            shape((64, 768), BF),
            shape((64, 768), BF),
            shape((6, 576, 256), BF),
            shape((2, 128, 256), BF),
        ),
        [
            pltpu.VMEM((384, 256), BF),
            pltpu.VMEM((4, 1152, 256), BF),
            pltpu.VMEM((256, 2304), BF),
            pltpu.VMEM((512, 768), BF),
            pltpu.SemaphoreType.DMA((2,)),
        ],
        1 << 32,
        (
            pos, sent, near, far, in1, out1, in2, out2,
            w4f, w4b, const(pool_four), sl3, const(gather_planes), w3b, const(deep_matrices),
        ),
        far_in=(13, 14),
    )
    near, far = swap(near, far, "gz")
    (sent,) = call(
        grads_kernel,
        (shape((8, 288, 128), BF),),
        [pltpu.VMEM((8, 288, 128), F32)],
        1 << 31,
        (pos, field4, own4, d3, p4, vq),
    )
    got = lax.all_to_all(sent, "ch", 0, 0, tiled=True)
    grads = got.astype(F32).sum(axis=0).astype(BF)
    pooled_four = got[:, 272:, :16].transpose(1, 0, 2)[:, None]

    (g2,) = call(
        shallow_back_kernel,
        (shape((160, 128), F32),),
        [
            pltpu.VMEM((4, 192, 768), BF),
            pltpu.VMEM((12, 32, 1024), BF),
            pltpu.VMEM((10, 48, 1280), BF),
            pltpu.SemaphoreType.DMA((1,)),
        ],
        1 << 32,
        (
            pos, d3, near, far, w3b,
            const(shift_straight), const(shift_cross), const(spread_two), sl2, vx,
        ),
        far_in=(9,),
    )
    pieces = jnp.concatenate(
        [grads.reshape(32, 9, 128), g2.astype(BF).reshape(32, 5, 128)], axis=1
    )
    pieces = lax.all_to_all(pieces, "gz", 0, 0, tiled=True).astype(F32).sum(axis=0)
    two = to_all(pieces[9:].astype(BF), "ch").astype(F32).sum(axis=0)
    whole = to_all(jnp.concatenate([pieces[:9], two], axis=0).astype(BF), "gz")
    four, three, two = call(
        write_kernel,
        (shape((216, 128), F32), shape((27, 4, 64), F32), shape((3, 144, 32), F32)),
        [],
        1 << 20,
        (pos, whole),
    )
    grad_four = four.reshape(3, 3, 3, 8, 128).transpose(4, 3, 0, 1, 2)
    grad_three = three.reshape(3, 3, 3, 4, 64).transpose(4, 3, 0, 1, 2)
    grad_two = two.reshape(3, 3, 3, 16, 32).transpose(4, 3, 0, 1, 2)
    return (pooled_four, grad_two, grad_three, grad_four)


def solution(mesh):
    in_specs = (
        P(None, "gz", "ch", None),
        P(),
        P(None, "ch", None, None, None),
        P(None, "ch", None, None, None),
        P("ch", "gz", None, None),
    )
    out_specs = (
        P("ch", "gz", None, None),
        P(),
        P(None, "ch", None, None, None),
        P(None, "ch", None, None, None),
    )
    return jax.shard_map(body, mesh=mesh, in_specs=in_specs, out_specs=out_specs, check_vma=False)
```

```python
import jax
import jax.numpy as jnp
import numpy as np
from jax import lax
from jax.experimental import pallas as pl
from jax.experimental.pallas import tpu as pltpu
from jax.sharding import PartitionSpec as P

BF = jnp.bfloat16
F32 = jnp.float32
VMEM_LIMIT = 12 * 1024 * 1024


def grid(*extents):
    return np.meshgrid(*[np.arange(n) for n in extents], indexing="ij")


def shift_rows():
    out = np.zeros((128, 2, 128), np.float32)
    for x in range(128):
        if x > 0:
            out[x - 1, 0, x] = 1
        if x < 127:
            out[x + 1, 1, x] = 1
    return out.reshape(128, 256)


def shift_halves():
    out = np.zeros((2, 64, 2, 2, 64), np.float32)
    for h in range(2):
        for x in range(64):
            if x > 0:
                out[h, x - 1, 0, h, x] = 1
            if x < 63:
                out[h, x + 1, 1, h, x] = 1
    return out.reshape(128, 256)


def shift_straight():
    side = shift_halves()
    return np.concatenate([side[:, :128], np.eye(128, dtype=np.float32), side[:, 128:]], 1)


def shift_cross():
    straight = shift_straight()
    out = np.zeros((256, 384), np.float32)
    out[64:128] = straight[0:64]
    out[128:192] = straight[64:128]
    return out


def pool_two():
    out = np.zeros((2, 64, 2, 2, 64), np.float32)
    for h in range(2):
        for x in range(64):
            out[h, x, :, h, x] = 0.125
    return out.reshape(256, 128)


def pool_three():
    out = np.zeros((2, 2, 32, 2, 2, 2, 32), np.float32)
    for yc in range(2):
        for zc in range(2):
            for x in range(32):
                out[yc, zc, x, :, zc, yc, x] = 0.125
    return out.reshape(256, 128)


def gather_planes():
    out = np.zeros((5, 2, 2, 32, 2, 8, 32), np.float32)
    for b in range(5):
        for yy in range(2):
            y = 2 * b + yy - 1
            if 0 <= y < 8:
                for zz in range(2):
                    for x in range(32):
                        out[b, zz, yy, x, zz, y, x] = 1
    return out.reshape(640, 512)


def shift_planes():
    out = np.zeros((8, 32, 3, 8, 32), np.float32)
    for kx in range(3):
        for y in range(8):
            for x in range(32):
                if 0 <= x + kx - 1 < 32:
                    out[y, x + kx - 1, kx, y, x] = 1
    return out.reshape(256, 768)


def pool_four():
    out = np.zeros((8, 16, 2, 128), np.float32)
    for x in range(16):
        out[2:4, x, :, x] = 0.125
    return out.reshape(256, 128)


def spread_three():
    out = np.zeros((2, 8, 32, 6, 2, 32, 2), np.float32)
    for r in range(6):
        cell = (r - 1) // 2 + 1
        for h in range(2):
            for x in range(32):
                out[h, cell, x, r, h, x, :] = 0.125
    return out.reshape(512, 768)


def spread_two():
    out = np.zeros((2, 64, 2, 64, 2), np.float32)
    for h in range(2):
        for x in range(64):
            out[h, x, h, x, :] = 0.125
    return out.reshape(128, 256)


def const(build):
    return jnp.asarray(build(), BF)


def dot(a, b):
    return lax.dot_general(a, b, (((1,), (0,)), ((), ())), preferred_element_type=F32)


def dot_nt(a, b):
    return lax.dot_general(a, b, (((1,), (1,)), ((), ())), preferred_element_type=F32)


def fold_rows(parts):
    third = parts.shape[0] // 3
    total = parts[:third]
    for ky in (1, 2):
        total = total + pltpu.roll(parts[ky * third : (ky + 1) * third], 256 - 32 * ky, 1)
    return total


def sigmoid(u):
    return 0.5 * jnp.tanh(0.5 * u) + 0.5


def act_of(u, s):
    return u * (0.3 + 0.7 * s)


def slope_of(u, s):
    return 0.3 + 0.7 * (s + u * s * (1.0 - s))


def call(kernel, out_shape, scratch, flops, args, far_in=(), far_out=()):
    def place(far):
        return pl.BlockSpec(memory_space=pltpu.HBM if far else pltpu.VMEM)

    specs = [pl.BlockSpec(memory_space=pltpu.SMEM)] + [
        place(n in far_in) for n in range(1, len(args))
    ]
    args = [
        pltpu.with_memory_space_constraint(a, pltpu.HBM) if n in far_in else a
        for n, a in enumerate(args)
    ]
    return pl.pallas_call(
        kernel,
        out_shape=tuple(
            pltpu.HBM(o.shape, o.dtype) if n in far_out else o for n, o in enumerate(out_shape)
        ),
        in_specs=specs,
        out_specs=tuple(place(n in far_out) for n in range(len(out_shape))),
        scratch_shapes=scratch,
        compiler_params=pltpu.CompilerParams(vmem_limit_bytes=VMEM_LIMIT),
        cost_estimate=pl.CostEstimate(flops=flops, bytes_accessed=1 << 20, transcendentals=0),
    )(*args)


def shallow_forward_kernel(
    pos, near, mid, far, w2, shift2, pool2, shift3, vq, sl2_far, vx_far, sums, sl2, vx, sems
):
    gz, ch = pos[0], pos[1]
    shift = shift2[...]

    odd = gz % 2 == 1
    for which, first, count in ((0, 0, 3), (1, 3, 8), (2, 11, 3)):

        @pl.loop(0, count, unroll=2 if count == 8 else 3)
        def _(z):
            if which == 1:
                field = mid[z].reshape(224, 128)
            else:
                one, two = near[z].reshape(224, 128), far[z].reshape(224, 128)
                if which == 2:
                    one, two = two, one
                field = jnp.where(odd, one.astype(F32), two.astype(F32)).astype(BF)
            sides = dot(field, shift)
            for y in range(14):
                lanes = slice(y * 128, y * 128 + 128)
                rows = slice(y * 16, y * 16 + 16)
                vx[z + first, 0:16, lanes] = sides[rows, :128].astype(BF)
                vx[z + first, 16:32, lanes] = field[rows]
                vx[z + first, 32:48, lanes] = sides[rows, 128:].astype(BF)

    vx_copy = pltpu.make_async_copy(
        vx.at[2:12, :, 256:1536], vx_far, sems.at[0]
    )
    vx_copy.start()
    filters = w2[...]

    @pl.loop(0, 6, unroll=3)
    def _(zc):
        zg = 4 * gz + zc - 1
        z_in = jnp.logical_and(zg >= 0, zg < 128)
        for q, (ya, yb) in enumerate(((1, 2), (3, 4), (0, 5))):
            rhs = jnp.concatenate(
                [
                    jnp.concatenate(
                        [
                            vx[2 * zc + zz, :, (2 * ya + yy) * 128 : (2 * ya + yy + 1) * 128],
                            vx[2 * zc + zz, :, (2 * yb + yy) * 128 : (2 * yb + yy + 1) * 128],
                        ],
                        axis=1,
                    )
                    for zz in range(4)
                    for yy in range(4)
                ],
                axis=0,
            )
            pre = dot(filters, rhs)
            s = sigmoid(pre)
            a = act_of(pre, s)
            if q < 2:
                sl2[zc, :, q * 256 : q * 256 + 256] = slope_of(pre, s).astype(BF)
            total = (a[0:32] + a[32:64]) + (a[64:96] + a[96:128])
            for c, yc in enumerate((ya, yb)):
                yg = 4 * ch + yc - 1
                inside = jnp.logical_and(z_in, jnp.logical_and(yg >= 0, yg < 32))
                cell = jnp.where(inside, total[:, c * 128 : c * 128 + 128], 0.0)
                sums[zc, yc * 32 : yc * 32 + 32] = cell.astype(BF)

    sl2_copy = pltpu.make_async_copy(sl2.at[1:5], sl2_far, sems.at[1])
    sl2_copy.start()
    pool = pool2[...]
    halves = shift3[...]
    for j in range(4):
        pair = jnp.concatenate([sums[j], sums[j + 2]], axis=1)
        pooled = dot(pair, pool).astype(BF)
        sides = dot(pooled, halves)
        for y in range(6):
            rows = slice(y * 32, y * 32 + 32)
            lanes = slice(y * 128, y * 128 + 128)
            vq[j, 0:32, lanes] = sides[rows, :128].astype(BF)
            vq[j, 32:64, lanes] = pooled[rows]
            vq[j, 64:96, lanes] = sides[rows, 128:].astype(BF)
    vx_copy.wait()
    sl2_copy.wait()


def middle_forward_kernel(pos, vq, w3, pool3, cot, sent, edges, sl3):
    sent[64:192] = cot[...]
    filters = w3[...]
    cells = [None, None]
    for zp in range(2):
        for n in range(2):
            blocks = [
                vq[zp + kz, :, (2 * n + ky) * 128 : (2 * n + ky + 2) * 128]
                for kz in range(3)
                for ky in range(3)
            ]
            pre = dot(filters, jnp.concatenate(blocks, axis=0))
            s = sigmoid(pre)
            sl3[zp, :, n * 256 : n * 256 + 256] = slope_of(pre, s).astype(BF)
            a = act_of(pre, s)
            part = a[:, :128] + a[:, 128:]
            cells[n] = part if zp == 0 else cells[n] + part
    both = jnp.concatenate(cells, axis=1).astype(BF)
    sent[0:64] = dot(both, pool3[...]).astype(BF)
    odd = pos[1] % 2
    for zp in range(2):
        top, bottom = sl3[zp, :, 384:512], sl3[zp, :, 0:128]
        edges[odd, zp * 64 : zp * 64 + 64] = top
        edges[1 - odd, zp * 64 : zp * 64 + 64] = bottom


def deep_kernel(
    pos, own3, near, far, in1, out1, in2, out2, w4f, w4b, pool4, sl3, planes_of, shift4, w3b, spread_far,
    p4, near_out, far_out, field, own,
    planes, back_in, d3, spread3, sems,
):
    spread_copy = pltpu.make_async_copy(spread_far, spread3, sems.at[0])
    spread_copy.start()
    odd, ch = pos[0] % 2, pos[1]

    def pick(cond, one, two):
        return jnp.where(cond, one.astype(F32), two.astype(F32)).astype(BF)

    def in_order(blocks):
        first, second, third = blocks
        return [pick(odd == 1, first, third), second, pick(odd == 1, third, first)]

    def neighbour(inside, outside, upper, rows):
        one, two = inside[rows], outside[rows]
        return pick(upper, one, two), pick(upper, two, one)

    odd_y, odd_pair = ch % 2 == 1, ch % 4 >= 2
    mine = jnp.concatenate([near[0:64], own3[0:64], far[0:64]], axis=0)
    below1, above1 = neighbour(in1, out1, odd_y, slice(0, 192))
    below2, above2 = neighbour(in2, out2, odd_pair, slice(0, 192))
    parts = [
        jnp.concatenate(in_order([p[0:64], p[64:128], p[128:192]]), axis=0)
        for p in (below2, below1, mine, above1, above2)
    ]
    cots = in_order([near[64:192], own3[64:192], far[64:192]])
    edge_low, edge_high = neighbour(in1, out1, odd_y, slice(192, 320))
    flat = dot(jnp.concatenate(parts, axis=1), planes_of[...]).astype(BF)
    for zb in range(3):
        for zz in range(2):
            p = 2 * zb + zz
            planes[p * 64 : p * 64 + 64] = flat[zb * 64 : zb * 64 + 64, zz * 256 : zz * 256 + 256]
    for kx in range(3):
        moved = dot(planes[...], shift4[:, kx * 256 : kx * 256 + 256]).astype(BF)
        for p in range(6):
            field[p, kx * 64 : kx * 64 + 64] = moved[p * 64 : p * 64 + 64]

    row = lax.broadcasted_iota(jnp.int32, (128, 256), 0)
    lane = lax.broadcasted_iota(jnp.int32, (128, 256), 1)
    source_y, source_x = row // 16, row % 16
    y, x = lane // 32, lane % 32
    match = (source_x == x // 2) & (source_y == ch - 1 + y // 2) & (y < 6)
    spread = jnp.where(match, 0.125, 0.0).astype(BF)
    inner = lax.broadcasted_iota(jnp.int32, (128, 256), 1) // 64 == 1

    filters = w4f[...]
    pooled = None
    deltas = []
    for z in range(4):
        pre = fold_rows(dot(filters, field[z : z + 3].reshape(576, 256)))
        s = sigmoid(pre)
        wide = dot(cots[(z + 1) // 2], spread)
        delta = wide * slope_of(pre, s)
        deltas.append(delta.astype(BF))
        if z in (1, 2):
            own[z - 1] = jnp.where(inner, delta, 0.0).astype(BF)
            a = act_of(pre, s)
            pooled = a if pooled is None else pooled + a
    high = pooled.astype(BF)
    low = (pooled - high.astype(F32)).astype(BF)
    p4[...] = dot(high, pool4[...]) + dot(low, pool4[...])

    stacked = jnp.concatenate(deltas, axis=0)
    for kx in range(3):
        moved = dot(stacked, shift4[:, kx * 256 : kx * 256 + 256]).astype(BF)
        for z in range(4):
            back_in[z, kx * 128 : kx * 128 + 128] = moved[z * 128 : z * 128 + 128]
    filters = w4b[...]
    back = [
        fold_rows(dot(filters, back_in[z : z + 3].reshape(1152, 256))).astype(BF)
        for z in range(2)
    ]
    spread_copy.wait()
    wide = dot(jnp.concatenate(back, axis=1), spread3[...])
    for r in range(6):
        yg = 4 * ch + r - 1
        inside = jnp.logical_and(yg >= 0, yg < 32)
        lanes = slice(r * 128, r * 128 + 128)
        value = jnp.where(inside, wide[:, lanes], 0.0)
        for zp in range(2):
            rows = slice(zp * 64, zp * 64 + 64)
            if r == 0:
                slope = edge_low[rows]
            elif r == 5:
                slope = edge_high[rows]
            else:
                slope = sl3[zp, :, (r - 1) * 128 : r * 128]
            d3[zp, :, lanes] = (value * slope.astype(F32)).astype(BF)
    near_out[...] = d3[1 - odd]
    far_out[...] = d3[odd]


def own_packs(pos, near, far):
    odd = pos[0] % 2 == 1
    one, two = near[...].astype(F32), far[...].astype(F32)
    return jnp.where(odd, one, two).astype(BF), jnp.where(odd, two, one).astype(BF)


def grads_kernel(pos, field, own, near, far, p4, vq, sent, out):
    packs = own_packs(pos, near, far)
    rows = []
    for ky in range(3):
        moved = [own[z].astype(F32) for z in range(2)]
        if ky > 0:
            moved = [pltpu.roll(m, 32 * ky, 1) for m in moved]
        rows.append(jnp.concatenate([m.astype(BF) for m in moved], axis=1))
    right = jnp.concatenate(rows, axis=0)
    for kz in range(3):
        left = jnp.concatenate([field[1 + kz], field[2 + kz]], axis=1)
        res = dot_nt(left, right)
        for k in range(9):
            for c in range(8):
                at = (kz * 9 + k) * 8
                row, lane = k % 3 * 64 + c * 8, k // 3 * 128
                out[c, at : at + 8] = res[row : row + 8, lane : lane + 128]
    total = None
    zero = jnp.zeros((64, 512), BF)
    for j in range(4):
        rows = []
        for kz in range(3):
            zp = j - kz
            rows.append(packs[zp][:, 128:640] if 0 <= zp < 2 else zero)
        left = jnp.concatenate(
            [vq[j, :, ky * 128 : ky * 128 + 512] for ky in range(3)], axis=0
        )
        res = dot_nt(left, jnp.concatenate(rows, axis=0))
        total = res if total is None else total + res
    for k in range(9):
        for c in range(8):
            at = 216 + k * 4
            piece = total[k * 32 + c * 4 : k * 32 + c * 4 + 4]
            out[c, at : at + 4] = piece[:, :128]
            at, lanes = (252 + k * 4, slice(0, 64)) if k < 5 else (232 + k * 4, slice(64, 128))
            out[c, at : at + 4, lanes] = piece[:, 128:]
    for c in range(8):
        out[c, 268:272, 64:128] = jnp.zeros((4, 64), F32)
        out[c, 272:288] = p4[c * 16 : c * 16 + 16]
        sent[c] = out[c].astype(BF)


def shallow_back_kernel(
    pos, own_near, own_far, near, far, w3b, straight, cross, spread2, sl2, vx_far,
    g2, ds, d2, vx, sems,
):
    vx_copy = pltpu.make_async_copy(vx_far, vx, sems.at[0])
    vx_copy.start()

    def rows_of(value):
        return jnp.concatenate([value[:, y * 128 : y * 128 + 128] for y in range(6)], axis=0)

    odd = pos[0] % 2 == 1
    one, two = rows_of(near).astype(F32), rows_of(far).astype(F32)
    above = jnp.where(odd, one, two).astype(BF)
    below = jnp.where(odd, two, one).astype(BF)
    first, second = [rows_of(pack) for pack in own_packs(pos, own_near, own_far)]
    direct, across = straight[...], cross[...]
    sources = (
        (jnp.concatenate([above, second], axis=1), across),
        (first, direct),
        (second, direct),
        (jnp.concatenate([first, below], axis=1), across),
    )
    for j, (source, matrix) in enumerate(sources):
        moved = dot(source, matrix).astype(BF)
        for y in range(6):
            for kx in range(3):
                piece = moved[y * 64 : y * 64 + 64, kx * 128 : kx * 128 + 128]
                ds[j, kx * 64 : kx * 64 + 64, y * 128 : y * 128 + 128] = piece

    for z in (0, 1, 10, 11):
        d2[z] = jnp.zeros((32, 1024), BF)
    filters = w3b[...]
    backs = []
    for zp in range(2):
        parts = dot(filters, ds[zp : zp + 3].reshape(576, 768))
        for y in range(4):
            back = parts[0:32, y * 128 : y * 128 + 128]
            for ky in (1, 2):
                back = back + parts[ky * 32 : ky * 32 + 32, (y + ky) * 128 : (y + ky + 1) * 128]
            backs.append(back.astype(BF))
    wide = dot(jnp.concatenate(backs, axis=0), spread2[...])
    for zp in range(2):
        for y in range(4):
            at = (zp * 4 + y) * 32
            for h in range(2):
                value = wide[at : at + 32, h * 128 : h * 128 + 128]
                z = zp + 2 * h
                for dz in range(2):
                    for dy in range(2):
                        rows = slice((dz * 2 + dy) * 32, (dz * 2 + dy) * 32 + 32)
                        slope = sl2[z, rows, y * 128 : y * 128 + 128].astype(F32)
                        lanes = slice((2 * y + dy) * 128, (2 * y + dy) * 128 + 128)
                        d2[2 * z + dz + 2, :, lanes] = (value * slope).astype(BF)

    vx_copy.wait()
    total = None
    for z in range(10):
        left = jnp.concatenate(
            [vx[z, :, ky * 128 : ky * 128 + 1024] for ky in range(3)], axis=0
        )
        right = jnp.concatenate([d2[z + 2 - kz] for kz in range(3)], axis=0)
        part = dot_nt(left, right)
        total = part if total is None else total + part
    g2[...] = jnp.zeros((160, 128), F32)
    g2[0:144, 0:96] = total


def write_kernel(pos, whole, four, three, two):
    deep = whole[:, 0:9].astype(F32).reshape(288, 128)
    four[...] = deep[:216]
    for k in range(9):
        low = deep[216 + k * 4 : 220 + k * 4]
        at, lanes = (252 + k * 4, slice(0, 64)) if k < 5 else (232 + k * 4, slice(64, 128))
        high = deep[at : at + 4, lanes]
        three[k] = low[:, 0:64]
        three[9 + k] = low[:, 64:128]
        three[18 + k] = high
    shallow = whole[:, 9:14].astype(F32).reshape(160, 128)
    for kz in range(3):
        two[kz] = shallow[:144, kz * 32 : kz * 32 + 32]


def swap(one, two, axis, step=1):
    count = lax.axis_size(axis)
    inside = [(i, i ^ step) for i in range(count)]
    outside = [(i, i + step) for i in range(count - step) if i % (2 * step) >= step]
    outside = outside + [(b, a) for a, b in outside]
    return lax.ppermute(one, axis, inside), lax.ppermute(two, axis, outside)


def swap_cores(value):
    return lax.ppermute(value, "gz", [(i, i ^ 1) for i in range(lax.axis_size("gz"))])


def to_all(piece, axis):
    count = lax.axis_size(axis)
    copies = jnp.broadcast_to(piece[None], (count,) + piece.shape)
    return lax.all_to_all(copies, axis, 0, 0, tiled=True)


def band(filters):
    taps = filters.transpose(0, 2, 3, 4, 1).reshape(32, 3, 3, 48)
    rows = [
        jnp.pad(taps, ((0, 0), (dz, 1 - dz), (dy, 1 - dy), (0, 0)))
        for dz in range(2)
        for dy in range(2)
    ]
    return jnp.stack(rows).reshape(128, 768)


def body(volume, filters_two, filters_three, filters_four, cotangent):
    gz, ch = lax.axis_index("gz"), lax.axis_index("ch")
    pos = jnp.stack([gz, ch]).astype(jnp.int32)
    odd_z, odd_y = gz % 2, ch % 2
    shape = jax.ShapeDtypeStruct

    field = volume.transpose(1, 2, 0, 3)
    near, far = swap(
        lax.dynamic_slice_in_dim(volume, 5 * (1 - odd_y), 3, 2).transpose(1, 2, 0, 3),
        lax.dynamic_slice_in_dim(volume, 5 * odd_y, 3, 2).transpose(1, 2, 0, 3),
        "ch",
    )
    low = jnp.where(odd_y == 1, near, far)
    high = jnp.where(odd_y == 1, far, near)
    mid = jnp.concatenate([low, field, high], axis=1)

    four = filters_four.transpose(2, 3, 4, 1, 0).reshape(216, 128)
    three = filters_three.transpose(2, 3, 4, 1, 0).reshape(108, 64)
    three = jnp.pad(three, ((0, 0), (0, 64)))
    cot = cotangent.reshape(16, 128)
    held = jnp.concatenate(
        [
            cot,
            lax.dynamic_slice_in_dim(four, 108 * odd_z, 108, 0),
            lax.dynamic_slice_in_dim(three, 54 * odd_z, 54, 0),
        ],
        axis=0,
    )
    held = jnp.broadcast_to(held[None], (8, 178, 128))
    w2 = band(filters_two)
    near, far = swap(
        lax.dynamic_slice_in_dim(mid, 5 * (1 - odd_z), 3, 0),
        lax.dynamic_slice_in_dim(mid, 5 * odd_z, 3, 0),
        "gz",
    )
    all_of = lax.all_to_all(held, "ch", 0, 0, tiled=True)
    cots = all_of[:, :16].reshape(128, 128)
    mine, w2 = lax.optimization_barrier((all_of[:, 16:], w2))
    other = swap_cores(mine)
    first = jnp.where(odd_z == 1, other, mine)
    second = jnp.where(odd_z == 1, mine, other)
    four = jnp.concatenate([first[:, :108], second[:, :108]], axis=1).reshape(8, 27, 8, 128)
    three = jnp.concatenate([first[:, 108:, :64], second[:, 108:, :64]], axis=1)
    three = three.reshape(8, 27, 4, 64)
    w3f = three.transpose(3, 1, 0, 2).reshape(64, 864)
    back = three[:, ::-1].reshape(8, 3, 3, 3, 4, 64)
    w3b = back.transpose(2, 0, 4, 1, 3, 5).reshape(96, 576)
    w4f = four.reshape(8, 3, 3, 3, 8, 128).transpose(2, 5, 1, 3, 0, 4).reshape(384, 576)
    back = four[:, ::-1].reshape(8, 3, 3, 3, 8, 128)
    w4b = back.transpose(2, 0, 4, 1, 3, 5).reshape(192, 1152)

    vq, sl2, vx = call(
        shallow_forward_kernel,
        (
            shape((4, 96, 768), BF),
            shape((4, 128, 512), BF),
            shape((10, 48, 1280), BF),
        ),
        [
            pltpu.VMEM((6, 192, 128), BF),
            pltpu.VMEM((6, 128, 512), BF),
            pltpu.VMEM((14, 48, 1792), BF),
            pltpu.SemaphoreType.DMA((2,)),
        ],
        1 << 32,
        (
            pos, near, mid, far, w2,
            const(shift_rows), const(pool_two), const(shift_halves),
        ),
        far_out=(1, 2),
    )
    sent, edges, sl3 = call(
        middle_forward_kernel,
        (
            shape((192, 128), BF),
            shape((2, 128, 128), BF),
            shape((2, 64, 512), BF),
        ),
        [],
        1 << 30,
        (pos, vq, w3f, const(pool_three), cots),
    )
    near, far = swap(sent, sent, "gz")
    near, w4f, w4b, w3b = lax.optimization_barrier((near, w4f, w4b, w3b))
    planes = jnp.concatenate([near[:64], sent[:64], far[:64]], axis=0)
    in1, out1 = swap(
        jnp.concatenate([planes, edges[0]], axis=0),
        jnp.concatenate([planes, edges[1]], axis=0),
        "ch",
    )
    in2, out2 = swap(planes, planes, "ch", 2)
    p4, own_near, own_far, field4, own4 = call(
        deep_kernel,
        (
            shape((128, 128), F32),
            shape((64, 768), BF),
            shape((64, 768), BF),
            shape((6, 192, 256), BF),
            shape((2, 128, 256), BF),
        ),
        [
            pltpu.VMEM((384, 256), BF),
            pltpu.VMEM((4, 384, 256), BF),
            pltpu.VMEM((2, 64, 768), BF),
            pltpu.VMEM((512, 768), BF),
            pltpu.SemaphoreType.DMA((1,)),
        ],
        1 << 32,
        (
            pos, sent, near, far, in1, out1, in2, out2,
            w4f, w4b, const(pool_four), sl3, const(gather_planes), const(shift_planes),
            w3b, const(spread_three),
        ),
        far_in=(14, 15),
    )
    near, far = swap(own_near, own_far, "gz")
    (sent,) = call(
        grads_kernel,
        (shape((8, 288, 128), BF),),
        [pltpu.VMEM((8, 288, 128), F32)],
        1 << 31,
        (pos, field4, own4, own_near, own_far, p4, vq),
    )
    got = lax.all_to_all(sent, "ch", 0, 0, tiled=True)
    grads = got.astype(F32).sum(axis=0).astype(BF)
    pooled_four = got[:, 272:, :16].transpose(1, 0, 2)[:, None]

    (g2,) = call(
        shallow_back_kernel,
        (shape((160, 128), F32),),
        [
            pltpu.VMEM((4, 192, 768), BF),
            pltpu.VMEM((12, 32, 1024), BF),
            pltpu.VMEM((10, 48, 1280), BF),
            pltpu.SemaphoreType.DMA((1,)),
        ],
        1 << 32,
        (
            pos, own_near, own_far, near, far, w3b,
            const(shift_straight), const(shift_cross), const(spread_two), sl2, vx,
        ),
        far_in=(10,),
    )
    pieces = jnp.concatenate(
        [grads.reshape(32, 9, 128), g2.astype(BF).reshape(32, 5, 128)], axis=1
    )
    pieces = lax.all_to_all(pieces, "gz", 0, 0, tiled=True).astype(F32).sum(axis=0)
    two = to_all(pieces[9:].astype(BF), "ch").astype(F32).sum(axis=0)
    whole = to_all(jnp.concatenate([pieces[:9], two], axis=0).astype(BF), "gz")
    four, three, two = call(
        write_kernel,
        (shape((216, 128), F32), shape((27, 4, 64), F32), shape((3, 144, 32), F32)),
        [],
        1 << 20,
        (pos, whole),
    )
    grad_four = four.reshape(3, 3, 3, 8, 128).transpose(4, 3, 0, 1, 2)
    grad_three = three.reshape(3, 3, 3, 4, 64).transpose(4, 3, 0, 1, 2)
    grad_two = two.reshape(3, 3, 3, 16, 32).transpose(4, 3, 0, 1, 2)
    return (pooled_four, grad_two, grad_three, grad_four)


def solution(mesh):
    in_specs = (
        P(None, "gz", "ch", None),
        P(),
        P(None, "ch", None, None, None),
        P(None, "ch", None, None, None),
        P("ch", "gz", None, None),
    )
    out_specs = (
        P("ch", "gz", None, None),
        P(),
        P(None, "ch", None, None, None),
        P(None, "ch", None, None, None),
    )
    return jax.shard_map(body, mesh=mesh, in_specs=in_specs, out_specs=out_specs, check_vma=False)
```

```python
import jax
import jax.numpy as jnp
import numpy as np
from jax import lax
from jax.experimental import pallas as pl
from jax.experimental.pallas import tpu as pltpu
from jax.sharding import PartitionSpec as P

BF = jnp.bfloat16
F32 = jnp.float32
VMEM_LIMIT = 12 * 1024 * 1024


def grid(*extents):
    return np.meshgrid(*[np.arange(n) for n in extents], indexing="ij")


def shift_rows():
    out = np.zeros((128, 2, 128), np.float32)
    for x in range(128):
        if x > 0:
            out[x - 1, 0, x] = 1
        if x < 127:
            out[x + 1, 1, x] = 1
    return out.reshape(128, 256)


def shift_halves():
    out = np.zeros((2, 64, 2, 2, 64), np.float32)
    for h in range(2):
        for x in range(64):
            if x > 0:
                out[h, x - 1, 0, h, x] = 1
            if x < 63:
                out[h, x + 1, 1, h, x] = 1
    return out.reshape(128, 256)


def shift_straight():
    side = shift_halves()
    return np.concatenate([side[:, :128], np.eye(128, dtype=np.float32), side[:, 128:]], 1)


def shift_cross():
    straight = shift_straight()
    out = np.zeros((256, 384), np.float32)
    out[64:128] = straight[0:64]
    out[128:192] = straight[64:128]
    return out


def pool_two():
    out = np.zeros((2, 64, 2, 2, 64), np.float32)
    for h in range(2):
        for x in range(64):
            out[h, x, :, h, x] = 0.125
    return out.reshape(256, 128)


def pool_three():
    out = np.zeros((2, 2, 32, 2, 2, 2, 32), np.float32)
    for yc in range(2):
        for zc in range(2):
            for x in range(32):
                out[yc, zc, x, :, zc, yc, x] = 0.125
    return out.reshape(256, 128)


def gather_planes():
    out = np.zeros((5, 2, 2, 32, 2, 8, 32), np.float32)
    for b in range(5):
        for yy in range(2):
            y = 2 * b + yy - 1
            if 0 <= y < 8:
                for zz in range(2):
                    for x in range(32):
                        out[b, zz, yy, x, zz, y, x] = 1
    return out.reshape(640, 512)


def shift_planes():
    out = np.zeros((8, 32, 3, 8, 32), np.float32)
    for kx in range(3):
        for y in range(8):
            for x in range(32):
                if 0 <= x + kx - 1 < 32:
                    out[y, x + kx - 1, kx, y, x] = 1
    return out.reshape(256, 768)


def pool_four():
    out = np.zeros((8, 16, 2, 128), np.float32)
    for x in range(16):
        out[2:4, x, :, x] = 0.125
    return out.reshape(256, 128)


def spread_three():
    out = np.zeros((2, 8, 32, 6, 2, 32, 2), np.float32)
    for r in range(6):
        cell = (r - 1) // 2 + 1
        for h in range(2):
            for x in range(32):
                out[h, cell, x, r, h, x, :] = 0.125
    return out.reshape(512, 768)


def spread_two():
    out = np.zeros((2, 64, 2, 64, 2), np.float32)
    for h in range(2):
        for x in range(64):
            out[h, x, h, x, :] = 0.125
    return out.reshape(128, 256)


def const(build):
    return jnp.asarray(build(), BF)


def dot(a, b):
    return lax.dot_general(a, b, (((1,), (0,)), ((), ())), preferred_element_type=F32)


def dot_nt(a, b):
    return lax.dot_general(a, b, (((1,), (1,)), ((), ())), preferred_element_type=F32)


def fold_rows(parts):
    third = parts.shape[0] // 3
    total = parts[:third]
    for ky in (1, 2):
        total = total + pltpu.roll(parts[ky * third : (ky + 1) * third], 256 - 32 * ky, 1)
    return total


def sigmoid(u):
    return 0.5 * jnp.tanh(0.5 * u) + 0.5


def act_of(u, s):
    return u * (0.3 + 0.7 * s)


def slope_of(u, s):
    return 0.3 + 0.7 * (s + u * s * (1.0 - s))


def call(kernel, out_shape, scratch, flops, args, far_in=(), far_out=()):
    def place(far):
        return pl.BlockSpec(memory_space=pltpu.HBM if far else pltpu.VMEM)

    specs = [pl.BlockSpec(memory_space=pltpu.SMEM)] + [
        place(n in far_in) for n in range(1, len(args))
    ]
    args = [
        pltpu.with_memory_space_constraint(a, pltpu.HBM) if n in far_in else a
        for n, a in enumerate(args)
    ]
    return pl.pallas_call(
        kernel,
        out_shape=tuple(
            pltpu.HBM(o.shape, o.dtype) if n in far_out else o for n, o in enumerate(out_shape)
        ),
        in_specs=specs,
        out_specs=tuple(place(n in far_out) for n in range(len(out_shape))),
        scratch_shapes=scratch,
        compiler_params=pltpu.CompilerParams(vmem_limit_bytes=VMEM_LIMIT),
        cost_estimate=pl.CostEstimate(flops=flops, bytes_accessed=1 << 20, transcendentals=0),
    )(*args)


def shift_plane(field, shift, out):
    sides = dot(field, shift)
    for y in range(14):
        lanes = slice(y * 128, y * 128 + 128)
        rows = slice(y * 16, y * 16 + 16)
        out[0:16, lanes] = sides[rows, :128].astype(BF)
        out[16:32, lanes] = field[rows]
        out[32:48, lanes] = sides[rows, 128:].astype(BF)


def layer_two(pos, zc, planes, filters, sums, slopes):
    zg = 4 * pos[0] + zc - 1
    z_in = jnp.logical_and(zg >= 0, zg < 128)
    for q, (ya, yb) in enumerate(((1, 2), (3, 4), (0, 5))):
        rhs = jnp.concatenate(
            [
                jnp.concatenate(
                    [
                        plane[:, (2 * ya + yy) * 128 : (2 * ya + yy + 1) * 128],
                        plane[:, (2 * yb + yy) * 128 : (2 * yb + yy + 1) * 128],
                    ],
                    axis=1,
                )
                for plane in planes
                for yy in range(4)
            ],
            axis=0,
        )
        pre = dot(filters, rhs)
        s = sigmoid(pre)
        a = act_of(pre, s)
        if q < 2 and slopes is not None:
            slopes[:, q * 256 : q * 256 + 256] = slope_of(pre, s).astype(BF)
        total = (a[0:32] + a[32:64]) + (a[64:96] + a[96:128])
        for c, yc in enumerate((ya, yb)):
            yg = 4 * pos[1] + yc - 1
            inside = jnp.logical_and(z_in, jnp.logical_and(yg >= 0, yg < 32))
            cell = jnp.where(inside, total[:, c * 128 : c * 128 + 128], 0.0)
            sums[yc * 32 : yc * 32 + 32] = cell.astype(BF)


def inner_forward_kernel(pos, mid, w2, shift2, sums, slopes_far, vx_far, vm, slopes, sems):
    shift = shift2[...]

    @pl.loop(0, 8, unroll=2)
    def _(z):
        shift_plane(mid[z].reshape(224, 128), shift, vm.at[z])

    vx_copy = pltpu.make_async_copy(vm.at[:, :, 256:1536], vx_far, sems.at[0])
    vx_copy.start()
    filters = w2[...]
    for n in range(2):
        planes = [vm.at[1 + 2 * n + zz] for zz in range(4)]
        layer_two(pos, n + 2, planes, filters, sums.at[n], slopes.at[n])
    slopes_copy = pltpu.make_async_copy(slopes, slopes_far, sems.at[1])
    slopes_copy.start()
    vx_copy.wait()
    slopes_copy.wait()


def outer_forward_kernel(
    pos, near, mid, far, inner, w2, shift2, pool2, shift3, vq, slopes_far, vx_far,
    sums, slopes, vh, sems,
):
    odd = pos[0] % 2 == 1
    shift = shift2[...]
    for z in range(3):
        one = near[z].reshape(224, 128).astype(F32)
        two = far[z].reshape(224, 128).astype(F32)
        shift_plane(jnp.where(odd, one, two).astype(BF), shift, vh.at[z])
        shift_plane(jnp.where(odd, two, one).astype(BF), shift, vh.at[9 + z])
        shift_plane(mid[z].reshape(224, 128), shift, vh.at[3 + z])
        shift_plane(mid[5 + z].reshape(224, 128), shift, vh.at[6 + z])
    late = [
        pltpu.make_async_copy(vh.at[2, :, 256:1536], vx_far.at[0], sems.at[0]),
        pltpu.make_async_copy(vh.at[9, :, 256:1536], vx_far.at[1], sems.at[1]),
        pltpu.make_async_copy(slopes.at[0], slopes_far.at[0], sems.at[2]),
        pltpu.make_async_copy(slopes.at[1], slopes_far.at[1], sems.at[3]),
    ]
    late[0].start()
    late[1].start()
    filters = w2[...]
    held = [vh.at[z] for z in range(6)] + [None, None] + [vh.at[z] for z in range(6, 12)]
    for zc, at, slot in ((1, 1, 0), (4, 2, 1), (0, 0, None), (5, 3, None)):
        out = None if slot is None else slopes.at[slot]
        layer_two(pos, zc, held[2 * zc : 2 * zc + 4], filters, sums.at[at], out)
        if slot is not None:
            late[2 + slot].start()

    pool = pool2[...]
    halves = shift3[...]
    cells = [sums[0], sums[1], inner[0], inner[1], sums[2], sums[3]]
    for j in range(4):
        pair = jnp.concatenate([cells[j], cells[j + 2]], axis=1)
        pooled = dot(pair, pool).astype(BF)
        sides = dot(pooled, halves)
        for y in range(6):
            rows = slice(y * 32, y * 32 + 32)
            lanes = slice(y * 128, y * 128 + 128)
            vq[j, 0:32, lanes] = sides[rows, :128].astype(BF)
            vq[j, 32:64, lanes] = pooled[rows]
            vq[j, 64:96, lanes] = sides[rows, 128:].astype(BF)
    for copy in late:
        copy.wait()


def middle_forward_kernel(pos, vq, w3, pool3, cot, sent, edges, sl3):
    sent[64:192] = cot[...]
    filters = w3[...]
    cells = [None, None]
    for zp in range(2):
        for n in range(2):
            blocks = [
                vq[zp + kz, :, (2 * n + ky) * 128 : (2 * n + ky + 2) * 128]
                for kz in range(3)
                for ky in range(3)
            ]
            pre = dot(filters, jnp.concatenate(blocks, axis=0))
            s = sigmoid(pre)
            sl3[zp, :, n * 256 : n * 256 + 256] = slope_of(pre, s).astype(BF)
            a = act_of(pre, s)
            part = a[:, :128] + a[:, 128:]
            cells[n] = part if zp == 0 else cells[n] + part
    both = jnp.concatenate(cells, axis=1).astype(BF)
    sent[0:64] = dot(both, pool3[...]).astype(BF)
    odd = pos[1] % 2
    for zp in range(2):
        top, bottom = sl3[zp, :, 384:512], sl3[zp, :, 0:128]
        edges[odd, zp * 64 : zp * 64 + 64] = top
        edges[1 - odd, zp * 64 : zp * 64 + 64] = bottom


def deep_kernel(
    pos, own3, near, far, in1, out1, in2, out2, w4f, w4b, pool4, sl3, planes_of, shift4, w3b, spread_far,
    p4, near_out, far_out, field, own,
    planes, back_in, d3, spread3, sems,
):
    spread_copy = pltpu.make_async_copy(spread_far, spread3, sems.at[0])
    spread_copy.start()
    odd, ch = pos[0] % 2, pos[1]

    def pick(cond, one, two):
        return jnp.where(cond, one.astype(F32), two.astype(F32)).astype(BF)

    def in_order(blocks):
        first, second, third = blocks
        return [pick(odd == 1, first, third), second, pick(odd == 1, third, first)]

    def neighbour(inside, outside, upper, rows):
        one, two = inside[rows], outside[rows]
        return pick(upper, one, two), pick(upper, two, one)

    odd_y, odd_pair = ch % 2 == 1, ch % 4 >= 2
    mine = jnp.concatenate([near[0:64], own3[0:64], far[0:64]], axis=0)
    below1, above1 = neighbour(in1, out1, odd_y, slice(0, 192))
    below2, above2 = neighbour(in2, out2, odd_pair, slice(0, 192))
    parts = [
        jnp.concatenate(in_order([p[0:64], p[64:128], p[128:192]]), axis=0)
        for p in (below2, below1, mine, above1, above2)
    ]
    cots = in_order([near[64:192], own3[64:192], far[64:192]])
    edge_low, edge_high = neighbour(in1, out1, odd_y, slice(192, 320))
    flat = dot(jnp.concatenate(parts, axis=1), planes_of[...]).astype(BF)
    for zb in range(3):
        for zz in range(2):
            p = 2 * zb + zz
            planes[p * 64 : p * 64 + 64] = flat[zb * 64 : zb * 64 + 64, zz * 256 : zz * 256 + 256]
    for kx in range(3):
        moved = dot(planes[...], shift4[:, kx * 256 : kx * 256 + 256]).astype(BF)
        for p in range(6):
            field[p, kx * 64 : kx * 64 + 64] = moved[p * 64 : p * 64 + 64]

    row = lax.broadcasted_iota(jnp.int32, (128, 256), 0)
    lane = lax.broadcasted_iota(jnp.int32, (128, 256), 1)
    source_y, source_x = row // 16, row % 16
    y, x = lane // 32, lane % 32
    match = (source_x == x // 2) & (source_y == ch - 1 + y // 2) & (y < 6)
    spread = jnp.where(match, 0.125, 0.0).astype(BF)
    inner = lax.broadcasted_iota(jnp.int32, (128, 256), 1) // 64 == 1

    filters = w4f[...]
    pooled = None
    deltas = []
    for z in range(4):
        pre = fold_rows(dot(filters, field[z : z + 3].reshape(576, 256)))
        s = sigmoid(pre)
        wide = dot(cots[(z + 1) // 2], spread)
        delta = wide * slope_of(pre, s)
        deltas.append(delta.astype(BF))
        if z in (1, 2):
            own[z - 1] = jnp.where(inner, delta, 0.0).astype(BF)
            a = act_of(pre, s)
            pooled = a if pooled is None else pooled + a
    high = pooled.astype(BF)
    low = (pooled - high.astype(F32)).astype(BF)
    p4[...] = dot(high, pool4[...]) + dot(low, pool4[...])

    stacked = jnp.concatenate(deltas, axis=0)
    for kx in range(3):
        moved = dot(stacked, shift4[:, kx * 256 : kx * 256 + 256]).astype(BF)
        for z in range(4):
            back_in[z, kx * 128 : kx * 128 + 128] = moved[z * 128 : z * 128 + 128]
    filters = w4b[...]
    back = [
        fold_rows(dot(filters, back_in[z : z + 3].reshape(1152, 256))).astype(BF)
        for z in range(2)
    ]
    spread_copy.wait()
    wide = dot(jnp.concatenate(back, axis=1), spread3[...])
    for r in range(6):
        yg = 4 * ch + r - 1
        inside = jnp.logical_and(yg >= 0, yg < 32)
        lanes = slice(r * 128, r * 128 + 128)
        value = jnp.where(inside, wide[:, lanes], 0.0)
        for zp in range(2):
            rows = slice(zp * 64, zp * 64 + 64)
            if r == 0:
                slope = edge_low[rows]
            elif r == 5:
                slope = edge_high[rows]
            else:
                slope = sl3[zp, :, (r - 1) * 128 : r * 128]
            d3[zp, :, lanes] = (value * slope.astype(F32)).astype(BF)
    near_out[...] = d3[1 - odd]
    far_out[...] = d3[odd]


def own_packs(pos, near, far):
    odd = pos[0] % 2 == 1
    one, two = near[...].astype(F32), far[...].astype(F32)
    return jnp.where(odd, one, two).astype(BF), jnp.where(odd, two, one).astype(BF)


def grads_kernel(pos, field, own, near, far, p4, vq, sent, out):
    packs = own_packs(pos, near, far)
    rows = []
    for ky in range(3):
        moved = [own[z].astype(F32) for z in range(2)]
        if ky > 0:
            moved = [pltpu.roll(m, 32 * ky, 1) for m in moved]
        rows.append(jnp.concatenate([m.astype(BF) for m in moved], axis=1))
    right = jnp.concatenate(rows, axis=0)
    for kz in range(3):
        left = jnp.concatenate([field[1 + kz], field[2 + kz]], axis=1)
        res = dot_nt(left, right)
        for k in range(9):
            for c in range(8):
                at = (kz * 9 + k) * 8
                row, lane = k % 3 * 64 + c * 8, k // 3 * 128
                out[c, at : at + 8] = res[row : row + 8, lane : lane + 128]
    total = None
    zero = jnp.zeros((64, 512), BF)
    for j in range(4):
        rows = []
        for kz in range(3):
            zp = j - kz
            rows.append(packs[zp][:, 128:640] if 0 <= zp < 2 else zero)
        left = jnp.concatenate(
            [vq[j, :, ky * 128 : ky * 128 + 512] for ky in range(3)], axis=0
        )
        res = dot_nt(left, jnp.concatenate(rows, axis=0))
        total = res if total is None else total + res
    for k in range(9):
        for c in range(8):
            at = 216 + k * 4
            piece = total[k * 32 + c * 4 : k * 32 + c * 4 + 4]
            out[c, at : at + 4] = piece[:, :128]
            at, lanes = (252 + k * 4, slice(0, 64)) if k < 5 else (232 + k * 4, slice(64, 128))
            out[c, at : at + 4, lanes] = piece[:, 128:]
    for c in range(8):
        out[c, 268:272, 64:128] = jnp.zeros((4, 64), F32)
        out[c, 272:288] = p4[c * 16 : c * 16 + 16]
        sent[c] = out[c].astype(BF)


def shallow_back_kernel(
    pos, own_near, own_far, near, far, w3b, straight, cross, spread2, sl2_mid, sl2_edge, vx_mid, vx_edge,
    g2, ds, d2, vx, sems,
):
    vx_copies = [
        pltpu.make_async_copy(vx_mid, vx.at[1:9], sems.at[0]),
        pltpu.make_async_copy(vx_edge.at[0], vx.at[0], sems.at[1]),
        pltpu.make_async_copy(vx_edge.at[1], vx.at[9], sems.at[2]),
    ]
    for copy in vx_copies:
        copy.start()
    sl2 = (sl2_edge.at[0], sl2_mid.at[0], sl2_mid.at[1], sl2_edge.at[1])

    def rows_of(value):
        return jnp.concatenate([value[:, y * 128 : y * 128 + 128] for y in range(6)], axis=0)

    odd = pos[0] % 2 == 1
    one, two = rows_of(near).astype(F32), rows_of(far).astype(F32)
    above = jnp.where(odd, one, two).astype(BF)
    below = jnp.where(odd, two, one).astype(BF)
    first, second = [rows_of(pack) for pack in own_packs(pos, own_near, own_far)]
    direct, across = straight[...], cross[...]
    sources = (
        (jnp.concatenate([above, second], axis=1), across),
        (first, direct),
        (second, direct),
        (jnp.concatenate([first, below], axis=1), across),
    )
    for j, (source, matrix) in enumerate(sources):
        moved = dot(source, matrix).astype(BF)
        for y in range(6):
            for kx in range(3):
                piece = moved[y * 64 : y * 64 + 64, kx * 128 : kx * 128 + 128]
                ds[j, kx * 64 : kx * 64 + 64, y * 128 : y * 128 + 128] = piece

    for z in (0, 1, 10, 11):
        d2[z] = jnp.zeros((32, 1024), BF)
    filters = w3b[...]
    backs = []
    for zp in range(2):
        parts = dot(filters, ds[zp : zp + 3].reshape(576, 768))
        for y in range(4):
            back = parts[0:32, y * 128 : y * 128 + 128]
            for ky in (1, 2):
                back = back + parts[ky * 32 : ky * 32 + 32, (y + ky) * 128 : (y + ky + 1) * 128]
            backs.append(back.astype(BF))
    wide = dot(jnp.concatenate(backs, axis=0), spread2[...])
    for zp in range(2):
        for y in range(4):
            at = (zp * 4 + y) * 32
            for h in range(2):
                value = wide[at : at + 32, h * 128 : h * 128 + 128]
                z = zp + 2 * h
                for dz in range(2):
                    for dy in range(2):
                        rows = slice((dz * 2 + dy) * 32, (dz * 2 + dy) * 32 + 32)
                        slope = sl2[z][rows, y * 128 : y * 128 + 128].astype(F32)
                        lanes = slice((2 * y + dy) * 128, (2 * y + dy) * 128 + 128)
                        d2[2 * z + dz + 2, :, lanes] = (value * slope).astype(BF)

    vx_copies[0].wait()
    total = None
    for z in (1, 2, 3, 4, 5, 6, 7, 8, 0, 9):
        if z == 0:
            vx_copies[1].wait()
            vx_copies[2].wait()
        left = jnp.concatenate(
            [vx[z, :, ky * 128 : ky * 128 + 1024] for ky in range(3)], axis=0
        )
        right = jnp.concatenate([d2[z + 2 - kz] for kz in range(3)], axis=0)
        part = dot_nt(left, right)
        total = part if total is None else total + part
    g2[...] = jnp.zeros((160, 128), F32)
    g2[0:144, 0:96] = total


def write_kernel(pos, whole, four, three, two):
    deep = whole[:, 0:9].astype(F32).reshape(288, 128)
    four[...] = deep[:216]
    for k in range(9):
        low = deep[216 + k * 4 : 220 + k * 4]
        at, lanes = (252 + k * 4, slice(0, 64)) if k < 5 else (232 + k * 4, slice(64, 128))
        high = deep[at : at + 4, lanes]
        three[k] = low[:, 0:64]
        three[9 + k] = low[:, 64:128]
        three[18 + k] = high
    shallow = whole[:, 9:14].astype(F32).reshape(160, 128)
    for kz in range(3):
        two[kz] = shallow[:144, kz * 32 : kz * 32 + 32]


def swap(one, two, axis, step=1):
    count = lax.axis_size(axis)
    inside = [(i, i ^ step) for i in range(count)]
    outside = [(i, i + step) for i in range(count - step) if i % (2 * step) >= step]
    outside = outside + [(b, a) for a, b in outside]
    return lax.ppermute(one, axis, inside), lax.ppermute(two, axis, outside)


def swap_cores(value):
    return lax.ppermute(value, "gz", [(i, i ^ 1) for i in range(lax.axis_size("gz"))])


def to_all(piece, axis):
    count = lax.axis_size(axis)
    copies = jnp.broadcast_to(piece[None], (count,) + piece.shape)
    return lax.all_to_all(copies, axis, 0, 0, tiled=True)


def band(filters):
    taps = filters.transpose(0, 2, 3, 4, 1).reshape(32, 3, 3, 48)
    rows = [
        jnp.pad(taps, ((0, 0), (dz, 1 - dz), (dy, 1 - dy), (0, 0)))
        for dz in range(2)
        for dy in range(2)
    ]
    return jnp.stack(rows).reshape(128, 768)


def body(volume, filters_two, filters_three, filters_four, cotangent):
    gz, ch = lax.axis_index("gz"), lax.axis_index("ch")
    pos = jnp.stack([gz, ch]).astype(jnp.int32)
    odd_z, odd_y = gz % 2, ch % 2
    shape = jax.ShapeDtypeStruct

    field = volume.transpose(1, 2, 0, 3)
    near, far = swap(
        lax.dynamic_slice_in_dim(volume, 5 * (1 - odd_y), 3, 2).transpose(1, 2, 0, 3),
        lax.dynamic_slice_in_dim(volume, 5 * odd_y, 3, 2).transpose(1, 2, 0, 3),
        "ch",
    )
    low = jnp.where(odd_y == 1, near, far)
    high = jnp.where(odd_y == 1, far, near)
    mid = jnp.concatenate([low, field, high], axis=1)

    four = filters_four.transpose(2, 3, 4, 1, 0).reshape(216, 128)
    three = filters_three.transpose(2, 3, 4, 1, 0).reshape(108, 64)
    three = jnp.pad(three, ((0, 0), (0, 64)))
    cot = cotangent.reshape(16, 128)
    held = jnp.concatenate(
        [
            cot,
            lax.dynamic_slice_in_dim(four, 108 * odd_z, 108, 0),
            lax.dynamic_slice_in_dim(three, 54 * odd_z, 54, 0),
        ],
        axis=0,
    )
    held = jnp.broadcast_to(held[None], (8, 178, 128))
    near, far = swap(
        lax.dynamic_slice_in_dim(mid, 5 * (1 - odd_z), 3, 0),
        lax.dynamic_slice_in_dim(mid, 5 * odd_z, 3, 0),
        "gz",
    )
    near, two = lax.optimization_barrier((near, filters_two))
    w2 = band(two)
    all_of = lax.all_to_all(held, "ch", 0, 0, tiled=True)
    mine, cots = lax.optimization_barrier((all_of[:, 16:], all_of[:, :16].reshape(128, 128)))
    other = swap_cores(mine)
    first = jnp.where(odd_z == 1, other, mine)
    second = jnp.where(odd_z == 1, mine, other)
    four = jnp.concatenate([first[:, :108], second[:, :108]], axis=1).reshape(8, 27, 8, 128)
    three = jnp.concatenate([first[:, 108:, :64], second[:, 108:, :64]], axis=1)
    three = three.reshape(8, 27, 4, 64)
    w3f = three.transpose(3, 1, 0, 2).reshape(64, 864)
    back = three[:, ::-1].reshape(8, 3, 3, 3, 4, 64)
    w3b = back.transpose(2, 0, 4, 1, 3, 5).reshape(96, 576)
    w4f = four.reshape(8, 3, 3, 3, 8, 128).transpose(2, 5, 1, 3, 0, 4).reshape(384, 576)
    back = four[:, ::-1].reshape(8, 3, 3, 3, 8, 128)
    w4b = back.transpose(2, 0, 4, 1, 3, 5).reshape(192, 1152)

    inner, sl2_mid, vx_mid = call(
        inner_forward_kernel,
        (
            shape((2, 192, 128), BF),
            shape((2, 128, 512), BF),
            shape((8, 48, 1280), BF),
        ),
        [
            pltpu.VMEM((8, 48, 1792), BF),
            pltpu.VMEM((2, 128, 512), BF),
            pltpu.SemaphoreType.DMA((2,)),
        ],
        1 << 31,
        (pos, mid, w2, const(shift_rows)),
        far_out=(1, 2),
    )
    vq, sl2_edge, vx_edge = call(
        outer_forward_kernel,
        (
            shape((4, 96, 768), BF),
            shape((2, 128, 512), BF),
            shape((2, 48, 1280), BF),
        ),
        [
            pltpu.VMEM((4, 192, 128), BF),
            pltpu.VMEM((2, 128, 512), BF),
            pltpu.VMEM((12, 48, 1792), BF),
            pltpu.SemaphoreType.DMA((4,)),
        ],
        1 << 32,
        (
            pos, near, mid, far, inner, w2,
            const(shift_rows), const(pool_two), const(shift_halves),
        ),
        far_out=(1, 2),
    )
    sent, edges, sl3 = call(
        middle_forward_kernel,
        (
            shape((192, 128), BF),
            shape((2, 128, 128), BF),
            shape((2, 64, 512), BF),
        ),
        [],
        1 << 30,
        (pos, vq, w3f, const(pool_three), cots),
    )
    near, far = swap(sent, sent, "gz")
    near, w4f, w4b, w3b = lax.optimization_barrier((near, w4f, w4b, w3b))
    planes = jnp.concatenate([near[:64], sent[:64], far[:64]], axis=0)
    in1, out1 = swap(
        jnp.concatenate([planes, edges[0]], axis=0),
        jnp.concatenate([planes, edges[1]], axis=0),
        "ch",
    )
    in2, out2 = swap(planes, planes, "ch", 2)
    p4, own_near, own_far, field4, own4 = call(
        deep_kernel,
        (
            shape((128, 128), F32),
            shape((64, 768), BF),
            shape((64, 768), BF),
            shape((6, 192, 256), BF),
            shape((2, 128, 256), BF),
        ),
        [
            pltpu.VMEM((384, 256), BF),
            pltpu.VMEM((4, 384, 256), BF),
            pltpu.VMEM((2, 64, 768), BF),
            pltpu.VMEM((512, 768), BF),
            pltpu.SemaphoreType.DMA((1,)),
        ],
        1 << 32,
        (
            pos, sent, near, far, in1, out1, in2, out2,
            w4f, w4b, const(pool_four), sl3, const(gather_planes), const(shift_planes),
            w3b, const(spread_three),
        ),
        far_in=(14, 15),
    )
    near, far = swap(own_near, own_far, "gz")
    (sent,) = call(
        grads_kernel,
        (shape((8, 288, 128), BF),),
        [pltpu.VMEM((8, 288, 128), F32)],
        1 << 31,
        (pos, field4, own4, own_near, own_far, p4, vq),
    )
    got = lax.all_to_all(sent, "ch", 0, 0, tiled=True)
    grads = got.astype(F32).sum(axis=0).astype(BF)
    pooled_four = got[:, 272:, :16].transpose(1, 0, 2)[:, None]

    (g2,) = call(
        shallow_back_kernel,
        (shape((160, 128), F32),),
        [
            pltpu.VMEM((4, 192, 768), BF),
            pltpu.VMEM((12, 32, 1024), BF),
            pltpu.VMEM((10, 48, 1280), BF),
            pltpu.SemaphoreType.DMA((3,)),
        ],
        1 << 32,
        (
            pos, own_near, own_far, near, far, w3b,
            const(shift_straight), const(shift_cross), const(spread_two),
            sl2_mid, sl2_edge, vx_mid, vx_edge,
        ),
        far_in=(11, 12),
    )
    pieces = jnp.concatenate(
        [grads.reshape(32, 9, 128), g2.astype(BF).reshape(32, 5, 128)], axis=1
    )
    pieces = lax.all_to_all(pieces, "gz", 0, 0, tiled=True).astype(F32).sum(axis=0)
    two = to_all(pieces[9:].astype(BF), "ch").astype(F32).sum(axis=0)
    whole = to_all(jnp.concatenate([pieces[:9], two], axis=0).astype(BF), "gz")
    four, three, two = call(
        write_kernel,
        (shape((216, 128), F32), shape((27, 4, 64), F32), shape((3, 144, 32), F32)),
        [],
        1 << 20,
        (pos, whole),
    )
    grad_four = four.reshape(3, 3, 3, 8, 128).transpose(4, 3, 0, 1, 2)
    grad_three = three.reshape(3, 3, 3, 4, 64).transpose(4, 3, 0, 1, 2)
    grad_two = two.reshape(3, 3, 3, 16, 32).transpose(4, 3, 0, 1, 2)
    return (pooled_four, grad_two, grad_three, grad_four)


def solution(mesh):
    in_specs = (
        P(None, "gz", "ch", None),
        P(),
        P(None, "ch", None, None, None),
        P(None, "ch", None, None, None),
        P("ch", "gz", None, None),
    )
    out_specs = (
        P("ch", "gz", None, None),
        P(),
        P(None, "ch", None, None, None),
        P(None, "ch", None, None, None),
    )
    return jax.shard_map(body, mesh=mesh, in_specs=in_specs, out_specs=out_specs, check_vma=False)
```

```python
import jax
import jax.numpy as jnp
import numpy as np
from jax import lax
from jax.experimental import pallas as pl
from jax.experimental.pallas import tpu as pltpu
from jax.sharding import PartitionSpec as P

BF = jnp.bfloat16
F32 = jnp.float32
VMEM_LIMIT = 12 * 1024 * 1024


def grid(*extents):
    return np.meshgrid(*[np.arange(n) for n in extents], indexing="ij")


def shift_rows():
    out = np.zeros((128, 2, 128), np.float32)
    for x in range(128):
        if x > 0:
            out[x - 1, 0, x] = 1
        if x < 127:
            out[x + 1, 1, x] = 1
    return out.reshape(128, 256)


def shift_halves():
    out = np.zeros((2, 64, 2, 2, 64), np.float32)
    for h in range(2):
        for x in range(64):
            if x > 0:
                out[h, x - 1, 0, h, x] = 1
            if x < 63:
                out[h, x + 1, 1, h, x] = 1
    return out.reshape(128, 256)


def shift_straight():
    side = shift_halves()
    return np.concatenate([side[:, :128], np.eye(128, dtype=np.float32), side[:, 128:]], 1)


def shift_cross():
    straight = shift_straight()
    out = np.zeros((256, 384), np.float32)
    out[64:128] = straight[0:64]
    out[128:192] = straight[64:128]
    return out


def pool_two():
    out = np.zeros((2, 64, 2, 2, 64), np.float32)
    for h in range(2):
        for x in range(64):
            out[h, x, :, h, x] = 0.125
    return out.reshape(256, 128)


def pool_three():
    out = np.zeros((2, 2, 32, 2, 2, 2, 32), np.float32)
    for yc in range(2):
        for zc in range(2):
            for x in range(32):
                out[yc, zc, x, :, zc, yc, x] = 0.125
    return out.reshape(256, 128)


def gather_planes():
    out = np.zeros((5, 2, 2, 32, 2, 8, 32), np.float32)
    for b in range(5):
        for yy in range(2):
            y = 2 * b + yy - 1
            if 0 <= y < 8:
                for zz in range(2):
                    for x in range(32):
                        out[b, zz, yy, x, zz, y, x] = 1
    return out.reshape(640, 512)


def shift_planes():
    out = np.zeros((8, 32, 3, 8, 32), np.float32)
    for kx in range(3):
        for y in range(8):
            for x in range(32):
                if 0 <= x + kx - 1 < 32:
                    out[y, x + kx - 1, kx, y, x] = 1
    return out.reshape(256, 768)


def pool_four():
    out = np.zeros((8, 16, 2, 128), np.float32)
    for x in range(16):
        out[2:4, x, :, x] = 0.125
    return out.reshape(256, 128)


def spread_three():
    out = np.zeros((2, 8, 32, 6, 2, 32, 2), np.float32)
    for r in range(6):
        cell = (r - 1) // 2 + 1
        for h in range(2):
            for x in range(32):
                out[h, cell, x, r, h, x, :] = 0.125
    return out.reshape(512, 768)


def spread_two():
    out = np.zeros((2, 64, 2, 64, 2), np.float32)
    for h in range(2):
        for x in range(64):
            out[h, x, h, x, :] = 0.125
    return out.reshape(128, 256)


def const(build):
    return jnp.asarray(build(), BF)


def dot(a, b):
    return lax.dot_general(a, b, (((1,), (0,)), ((), ())), preferred_element_type=F32)


def dot_nt(a, b):
    return lax.dot_general(a, b, (((1,), (1,)), ((), ())), preferred_element_type=F32)


def fold_rows(parts):
    third = parts.shape[0] // 3
    total = parts[:third]
    for ky in (1, 2):
        total = total + pltpu.roll(parts[ky * third : (ky + 1) * third], 256 - 32 * ky, 1)
    return total


def sigmoid(u):
    return 0.5 * jnp.tanh(0.5 * u) + 0.5


def act_of(u, s):
    return u * (0.3 + 0.7 * s)


def slope_of(u, s):
    return 0.3 + 0.7 * (s + u * s * (1.0 - s))


def call(kernel, out_shape, scratch, flops, args, far_in=(), far_out=()):
    def place(far):
        return pl.BlockSpec(memory_space=pltpu.HBM if far else pltpu.VMEM)

    specs = [pl.BlockSpec(memory_space=pltpu.SMEM)] + [
        place(n in far_in) for n in range(1, len(args))
    ]
    args = [
        pltpu.with_memory_space_constraint(a, pltpu.HBM) if n in far_in else a
        for n, a in enumerate(args)
    ]
    return pl.pallas_call(
        kernel,
        out_shape=tuple(
            pltpu.HBM(o.shape, o.dtype) if n in far_out else o for n, o in enumerate(out_shape)
        ),
        in_specs=specs,
        out_specs=tuple(place(n in far_out) for n in range(len(out_shape))),
        scratch_shapes=scratch,
        compiler_params=pltpu.CompilerParams(vmem_limit_bytes=VMEM_LIMIT),
        cost_estimate=pl.CostEstimate(flops=flops, bytes_accessed=1 << 20, transcendentals=0),
    )(*args)


def shift_plane(field, shift, out):
    sides = dot(field, shift)
    for y in range(14):
        lanes = slice(y * 128, y * 128 + 128)
        rows = slice(y * 16, y * 16 + 16)
        out[0:16, lanes] = sides[rows, :128].astype(BF)
        out[16:32, lanes] = field[rows]
        out[32:48, lanes] = sides[rows, 128:].astype(BF)


def layer_two(pos, zc, planes, filters, sums, slopes):
    zg = 4 * pos[0] + zc - 1
    z_in = jnp.logical_and(zg >= 0, zg < 128)
    for q, (ya, yb) in enumerate(((1, 2), (3, 4), (0, 5))):
        rhs = jnp.concatenate(
            [
                jnp.concatenate(
                    [
                        plane[:, (2 * ya + yy) * 128 : (2 * ya + yy + 1) * 128],
                        plane[:, (2 * yb + yy) * 128 : (2 * yb + yy + 1) * 128],
                    ],
                    axis=1,
                )
                for plane in planes
                for yy in range(4)
            ],
            axis=0,
        )
        pre = dot(filters, rhs)
        s = sigmoid(pre)
        a = act_of(pre, s)
        if q < 2 and slopes is not None:
            slopes[:, q * 256 : q * 256 + 256] = slope_of(pre, s).astype(BF)
        total = (a[0:32] + a[32:64]) + (a[64:96] + a[96:128])
        for c, yc in enumerate((ya, yb)):
            yg = 4 * pos[1] + yc - 1
            inside = jnp.logical_and(z_in, jnp.logical_and(yg >= 0, yg < 32))
            cell = jnp.where(inside, total[:, c * 128 : c * 128 + 128], 0.0)
            sums[yc * 32 : yc * 32 + 32] = cell.astype(BF)


def inner_forward_kernel(pos, mid, w2, shift2, sums, slopes_far, vx_far, vm, slopes, sems):
    shift = shift2[...]

    @pl.loop(0, 8, unroll=2)
    def _(z):
        shift_plane(mid[z].reshape(224, 128), shift, vm.at[z])

    vx_copy = pltpu.make_async_copy(vm.at[:, :, 256:1536], vx_far, sems.at[0])
    vx_copy.start()
    filters = w2[...]
    for n in range(2):
        planes = [vm.at[1 + 2 * n + zz] for zz in range(4)]
        layer_two(pos, n + 2, planes, filters, sums.at[n], slopes.at[n])
    slopes_copy = pltpu.make_async_copy(slopes, slopes_far, sems.at[1])
    slopes_copy.start()
    vx_copy.wait()
    slopes_copy.wait()


def outer_forward_kernel(
    pos, near, mid, far, inner, w2, shift2, pool2, shift3, pool3, vq, pool3_out, slopes_far, vx_far,
    sums, slopes, vh, sems,
):
    odd = pos[0] % 2 == 1
    pool3_out[...] = pool3[...]
    shift = shift2[...]
    for z in range(3):
        one = near[z].reshape(224, 128).astype(F32)
        two = far[z].reshape(224, 128).astype(F32)
        shift_plane(jnp.where(odd, one, two).astype(BF), shift, vh.at[z])
        shift_plane(jnp.where(odd, two, one).astype(BF), shift, vh.at[9 + z])
        shift_plane(mid[z].reshape(224, 128), shift, vh.at[3 + z])
        shift_plane(mid[5 + z].reshape(224, 128), shift, vh.at[6 + z])
    late = [
        pltpu.make_async_copy(vh.at[2, :, 256:1536], vx_far.at[0], sems.at[0]),
        pltpu.make_async_copy(vh.at[9, :, 256:1536], vx_far.at[1], sems.at[1]),
        pltpu.make_async_copy(slopes.at[0], slopes_far.at[0], sems.at[2]),
        pltpu.make_async_copy(slopes.at[1], slopes_far.at[1], sems.at[3]),
    ]
    late[0].start()
    late[1].start()
    filters = w2[...]
    held = [vh.at[z] for z in range(6)] + [None, None] + [vh.at[z] for z in range(6, 12)]
    for zc, at, slot in ((1, 1, 0), (4, 2, 1), (0, 0, None), (5, 3, None)):
        out = None if slot is None else slopes.at[slot]
        layer_two(pos, zc, held[2 * zc : 2 * zc + 4], filters, sums.at[at], out)
        if slot is not None:
            late[2 + slot].start()

    pool = pool2[...]
    halves = shift3[...]
    cells = [sums[0], sums[1], inner[0], inner[1], sums[2], sums[3]]
    for j in range(4):
        pair = jnp.concatenate([cells[j], cells[j + 2]], axis=1)
        pooled = dot(pair, pool).astype(BF)
        sides = dot(pooled, halves)
        for y in range(6):
            rows = slice(y * 32, y * 32 + 32)
            lanes = slice(y * 128, y * 128 + 128)
            vq[j, 0:32, lanes] = sides[rows, :128].astype(BF)
            vq[j, 32:64, lanes] = pooled[rows]
            vq[j, 64:96, lanes] = sides[rows, 128:].astype(BF)
    for copy in late:
        copy.wait()


def middle_forward_kernel(pos, vq, w3, pool3, cot, sent, edges, sl3):
    sent[64:192] = cot[...]
    filters = w3[...]
    cells = [None, None]
    for zp in range(2):
        for n in range(2):
            blocks = [
                vq[zp + kz, :, (2 * n + ky) * 128 : (2 * n + ky + 2) * 128]
                for kz in range(3)
                for ky in range(3)
            ]
            pre = dot(filters, jnp.concatenate(blocks, axis=0))
            s = sigmoid(pre)
            sl3[zp, :, n * 256 : n * 256 + 256] = slope_of(pre, s).astype(BF)
            a = act_of(pre, s)
            part = a[:, :128] + a[:, 128:]
            cells[n] = part if zp == 0 else cells[n] + part
    both = jnp.concatenate(cells, axis=1).astype(BF)
    sent[0:64] = dot(both, pool3[...]).astype(BF)
    odd = pos[1] % 2
    for zp in range(2):
        top, bottom = sl3[zp, :, 384:512], sl3[zp, :, 0:128]
        edges[odd, zp * 64 : zp * 64 + 64] = top
        edges[1 - odd, zp * 64 : zp * 64 + 64] = bottom


def deep_kernel(
    pos, own3, near, far, in1, out1, in2, out2, w4f, w4b, pool4, sl3, planes_of, shift4, w3b, spread_far,
    p4, near_out, far_out, field, own,
    planes, back_in, d3, spread3, sems,
):
    spread_copy = pltpu.make_async_copy(spread_far, spread3, sems.at[0])
    spread_copy.start()
    odd, ch = pos[0] % 2, pos[1]

    def pick(cond, one, two):
        return jnp.where(cond, one.astype(F32), two.astype(F32)).astype(BF)

    def in_order(blocks):
        first, second, third = blocks
        return [pick(odd == 1, first, third), second, pick(odd == 1, third, first)]

    def neighbour(inside, outside, upper, rows):
        one, two = inside[rows], outside[rows]
        return pick(upper, one, two), pick(upper, two, one)

    odd_y, odd_pair = ch % 2 == 1, ch % 4 >= 2
    mine = jnp.concatenate([near[0:64], own3[0:64], far[0:64]], axis=0)
    below1, above1 = neighbour(in1, out1, odd_y, slice(0, 192))
    below2, above2 = neighbour(in2, out2, odd_pair, slice(0, 192))
    parts = [
        jnp.concatenate(in_order([p[0:64], p[64:128], p[128:192]]), axis=0)
        for p in (below2, below1, mine, above1, above2)
    ]
    cots = in_order([near[64:192], own3[64:192], far[64:192]])
    edge_low, edge_high = neighbour(in1, out1, odd_y, slice(192, 320))
    flat = dot(jnp.concatenate(parts, axis=1), planes_of[...]).astype(BF)
    for zb in range(3):
        for zz in range(2):
            p = 2 * zb + zz
            planes[p * 64 : p * 64 + 64] = flat[zb * 64 : zb * 64 + 64, zz * 256 : zz * 256 + 256]
    for kx in range(3):
        moved = dot(planes[...], shift4[:, kx * 256 : kx * 256 + 256]).astype(BF)
        for p in range(6):
            field[p, kx * 64 : kx * 64 + 64] = moved[p * 64 : p * 64 + 64]

    row = lax.broadcasted_iota(jnp.int32, (128, 256), 0)
    lane = lax.broadcasted_iota(jnp.int32, (128, 256), 1)
    source_y, source_x = row // 16, row % 16
    y, x = lane // 32, lane % 32
    match = (source_x == x // 2) & (source_y == ch - 1 + y // 2) & (y < 6)
    spread = jnp.where(match, 0.125, 0.0).astype(BF)
    inner = lax.broadcasted_iota(jnp.int32, (128, 256), 1) // 64 == 1

    filters = w4f[...]
    pooled = None
    deltas = []
    for z in range(4):
        pre = fold_rows(dot(filters, field[z : z + 3].reshape(576, 256)))
        s = sigmoid(pre)
        wide = dot(cots[(z + 1) // 2], spread)
        delta = wide * slope_of(pre, s)
        deltas.append(delta.astype(BF))
        if z in (1, 2):
            own[z - 1] = jnp.where(inner, delta, 0.0).astype(BF)
            a = act_of(pre, s)
            pooled = a if pooled is None else pooled + a
    high = pooled.astype(BF)
    low = (pooled - high.astype(F32)).astype(BF)
    p4[...] = dot(high, pool4[...]) + dot(low, pool4[...])

    stacked = jnp.concatenate(deltas, axis=0)
    for kx in range(3):
        moved = dot(stacked, shift4[:, kx * 256 : kx * 256 + 256]).astype(BF)
        for z in range(4):
            back_in[z, kx * 128 : kx * 128 + 128] = moved[z * 128 : z * 128 + 128]
    filters = w4b[...]
    back = [
        fold_rows(dot(filters, back_in[z : z + 3].reshape(1152, 256))).astype(BF)
        for z in range(2)
    ]
    spread_copy.wait()
    wide = dot(jnp.concatenate(back, axis=1), spread3[...])
    for r in range(6):
        yg = 4 * ch + r - 1
        inside = jnp.logical_and(yg >= 0, yg < 32)
        lanes = slice(r * 128, r * 128 + 128)
        value = jnp.where(inside, wide[:, lanes], 0.0)
        for zp in range(2):
            rows = slice(zp * 64, zp * 64 + 64)
            if r == 0:
                slope = edge_low[rows]
            elif r == 5:
                slope = edge_high[rows]
            else:
                slope = sl3[zp, :, (r - 1) * 128 : r * 128]
            d3[zp, :, lanes] = (value * slope.astype(F32)).astype(BF)
    near_out[...] = d3[1 - odd]
    far_out[...] = d3[odd]


def own_packs(pos, near, far):
    odd = pos[0] % 2 == 1
    one, two = near[...].astype(F32), far[...].astype(F32)
    return jnp.where(odd, one, two).astype(BF), jnp.where(odd, two, one).astype(BF)


def grads_kernel(pos, field, own, near, far, p4, vq, sent, out):
    packs = own_packs(pos, near, far)
    rows = []
    for ky in range(3):
        moved = [own[z].astype(F32) for z in range(2)]
        if ky > 0:
            moved = [pltpu.roll(m, 32 * ky, 1) for m in moved]
        rows.append(jnp.concatenate([m.astype(BF) for m in moved], axis=1))
    right = jnp.concatenate(rows, axis=0)
    for kz in range(3):
        left = jnp.concatenate([field[1 + kz], field[2 + kz]], axis=1)
        res = dot_nt(left, right)
        for k in range(9):
            for c in range(8):
                at = (kz * 9 + k) * 8
                row, lane = k % 3 * 64 + c * 8, k // 3 * 128
                out[c, at : at + 8] = res[row : row + 8, lane : lane + 128]
    total = None
    zero = jnp.zeros((64, 512), BF)
    for j in range(4):
        rows = []
        for kz in range(3):
            zp = j - kz
            rows.append(packs[zp][:, 128:640] if 0 <= zp < 2 else zero)
        left = jnp.concatenate(
            [vq[j, :, ky * 128 : ky * 128 + 512] for ky in range(3)], axis=0
        )
        res = dot_nt(left, jnp.concatenate(rows, axis=0))
        total = res if total is None else total + res
    for k in range(9):
        for c in range(8):
            at = 216 + k * 4
            piece = total[k * 32 + c * 4 : k * 32 + c * 4 + 4]
            out[c, at : at + 4] = piece[:, :128]
            at, lanes = (252 + k * 4, slice(0, 64)) if k < 5 else (232 + k * 4, slice(64, 128))
            out[c, at : at + 4, lanes] = piece[:, 128:]
    for c in range(8):
        out[c, 268:272, 64:128] = jnp.zeros((4, 64), F32)
        out[c, 272:288] = p4[c * 16 : c * 16 + 16]
        sent[c] = out[c].astype(BF)


def shallow_back_kernel(
    pos, own_near, own_far, near, far, w3b, straight, cross, spread2, sl2_mid, sl2_edge, vx_mid, vx_edge,
    g2, ds, d2, vx, sems,
):
    vx_copies = [
        pltpu.make_async_copy(vx_mid, vx.at[1:9], sems.at[0]),
        pltpu.make_async_copy(vx_edge.at[0], vx.at[0], sems.at[1]),
        pltpu.make_async_copy(vx_edge.at[1], vx.at[9], sems.at[2]),
    ]
    for copy in vx_copies:
        copy.start()
    sl2 = (sl2_edge.at[0], sl2_mid.at[0], sl2_mid.at[1], sl2_edge.at[1])

    def rows_of(value):
        return jnp.concatenate([value[:, y * 128 : y * 128 + 128] for y in range(6)], axis=0)

    odd = pos[0] % 2 == 1
    one, two = rows_of(near).astype(F32), rows_of(far).astype(F32)
    above = jnp.where(odd, one, two).astype(BF)
    below = jnp.where(odd, two, one).astype(BF)
    first, second = [rows_of(pack) for pack in own_packs(pos, own_near, own_far)]
    direct, across = straight[...], cross[...]
    sources = (
        (jnp.concatenate([above, second], axis=1), across),
        (first, direct),
        (second, direct),
        (jnp.concatenate([first, below], axis=1), across),
    )
    for j, (source, matrix) in enumerate(sources):
        moved = dot(source, matrix).astype(BF)
        for y in range(6):
            for kx in range(3):
                piece = moved[y * 64 : y * 64 + 64, kx * 128 : kx * 128 + 128]
                ds[j, kx * 64 : kx * 64 + 64, y * 128 : y * 128 + 128] = piece

    for z in (0, 1, 10, 11):
        d2[z] = jnp.zeros((32, 1024), BF)
    filters = w3b[...]
    backs = []
    for zp in range(2):
        parts = dot(filters, ds[zp : zp + 3].reshape(576, 768))
        for y in range(4):
            back = parts[0:32, y * 128 : y * 128 + 128]
            for ky in (1, 2):
                back = back + parts[ky * 32 : ky * 32 + 32, (y + ky) * 128 : (y + ky + 1) * 128]
            backs.append(back.astype(BF))
    wide = dot(jnp.concatenate(backs, axis=0), spread2[...])
    for zp in range(2):
        for y in range(4):
            at = (zp * 4 + y) * 32
            for h in range(2):
                value = wide[at : at + 32, h * 128 : h * 128 + 128]
                z = zp + 2 * h
                for dz in range(2):
                    for dy in range(2):
                        rows = slice((dz * 2 + dy) * 32, (dz * 2 + dy) * 32 + 32)
                        slope = sl2[z][rows, y * 128 : y * 128 + 128].astype(F32)
                        lanes = slice((2 * y + dy) * 128, (2 * y + dy) * 128 + 128)
                        d2[2 * z + dz + 2, :, lanes] = (value * slope).astype(BF)

    vx_copies[0].wait()
    total = None
    for z in (1, 2, 3, 4, 5, 6, 7, 8, 0, 9):
        if z == 0:
            vx_copies[1].wait()
            vx_copies[2].wait()
        left = jnp.concatenate(
            [vx[z, :, ky * 128 : ky * 128 + 1024] for ky in range(3)], axis=0
        )
        right = jnp.concatenate([d2[z + 2 - kz] for kz in range(3)], axis=0)
        part = dot_nt(left, right)
        total = part if total is None else total + part
    g2[...] = jnp.zeros((160, 128), F32)
    g2[0:144, 0:96] = total


def write_kernel(pos, whole, four, three, two):
    deep = whole[:, 0:9].astype(F32).reshape(288, 128)
    four[...] = deep[:216]
    for k in range(9):
        low = deep[216 + k * 4 : 220 + k * 4]
        at, lanes = (252 + k * 4, slice(0, 64)) if k < 5 else (232 + k * 4, slice(64, 128))
        high = deep[at : at + 4, lanes]
        three[k] = low[:, 0:64]
        three[9 + k] = low[:, 64:128]
        three[18 + k] = high
    shallow = whole[:, 9:14].astype(F32).reshape(160, 128)
    for kz in range(3):
        two[kz] = shallow[:144, kz * 32 : kz * 32 + 32]


def swap(one, two, axis, step=1):
    count = lax.axis_size(axis)
    inside = [(i, i ^ step) for i in range(count)]
    outside = [(i, i + step) for i in range(count - step) if i % (2 * step) >= step]
    outside = outside + [(b, a) for a, b in outside]
    return lax.ppermute(one, axis, inside), lax.ppermute(two, axis, outside)


def swap_cores(value):
    return lax.ppermute(value, "gz", [(i, i ^ 1) for i in range(lax.axis_size("gz"))])


def to_all(piece, axis):
    count = lax.axis_size(axis)
    copies = jnp.broadcast_to(piece[None], (count,) + piece.shape)
    return lax.all_to_all(copies, axis, 0, 0, tiled=True)


def band(filters):
    taps = filters.transpose(0, 2, 3, 4, 1).reshape(32, 3, 3, 48)
    rows = [
        jnp.pad(taps, ((0, 0), (dz, 1 - dz), (dy, 1 - dy), (0, 0)))
        for dz in range(2)
        for dy in range(2)
    ]
    return jnp.stack(rows).reshape(128, 768)


def body(volume, filters_two, filters_three, filters_four, cotangent):
    gz, ch = lax.axis_index("gz"), lax.axis_index("ch")
    pos = jnp.stack([gz, ch]).astype(jnp.int32)
    odd_z, odd_y = gz % 2, ch % 2
    shape = jax.ShapeDtypeStruct

    field = volume.transpose(1, 2, 0, 3)
    near, far = swap(
        lax.dynamic_slice_in_dim(volume, 5 * (1 - odd_y), 3, 2).transpose(1, 2, 0, 3),
        lax.dynamic_slice_in_dim(volume, 5 * odd_y, 3, 2).transpose(1, 2, 0, 3),
        "ch",
    )
    low = jnp.where(odd_y == 1, near, far)
    high = jnp.where(odd_y == 1, far, near)
    mid = jnp.concatenate([low, field, high], axis=1)

    four = filters_four.transpose(2, 3, 4, 1, 0).reshape(216, 128)
    three = filters_three.transpose(2, 3, 4, 1, 0).reshape(108, 64)
    three = jnp.pad(three, ((0, 0), (0, 64)))
    cot = cotangent.reshape(16, 128)
    held = jnp.concatenate(
        [
            cot,
            lax.dynamic_slice_in_dim(four, 108 * odd_z, 108, 0),
            lax.dynamic_slice_in_dim(three, 54 * odd_z, 54, 0),
        ],
        axis=0,
    )
    held = jnp.broadcast_to(held[None], (8, 178, 128))
    near, far = swap(
        lax.dynamic_slice_in_dim(mid, 5 * (1 - odd_z), 3, 0),
        lax.dynamic_slice_in_dim(mid, 5 * odd_z, 3, 0),
        "gz",
    )
    near, two = lax.optimization_barrier((near, filters_two))
    w2 = band(two)
    all_of = lax.all_to_all(held, "ch", 0, 0, tiled=True)
    mine, cots = lax.optimization_barrier((all_of[:, 16:], all_of[:, :16].reshape(128, 128)))
    other = swap_cores(mine)
    first = jnp.where(odd_z == 1, other, mine)
    second = jnp.where(odd_z == 1, mine, other)
    four = jnp.concatenate([first[:, :108], second[:, :108]], axis=1).reshape(8, 27, 8, 128)
    three = jnp.concatenate([first[:, 108:, :64], second[:, 108:, :64]], axis=1)
    three = three.reshape(8, 27, 4, 64)
    w3f = three.transpose(3, 1, 0, 2).reshape(64, 864)
    back = three[:, ::-1].reshape(8, 3, 3, 3, 4, 64)
    w3b = back.transpose(2, 0, 4, 1, 3, 5).reshape(96, 576)
    w4f = four.reshape(8, 3, 3, 3, 8, 128).transpose(2, 5, 1, 3, 0, 4).reshape(384, 576)
    back = four[:, ::-1].reshape(8, 3, 3, 3, 8, 128)
    w4b = back.transpose(2, 0, 4, 1, 3, 5).reshape(192, 1152)

    inner, sl2_mid, vx_mid = call(
        inner_forward_kernel,
        (
            shape((2, 192, 128), BF),
            shape((2, 128, 512), BF),
            shape((8, 48, 1280), BF),
        ),
        [
            pltpu.VMEM((8, 48, 1792), BF),
            pltpu.VMEM((2, 128, 512), BF),
            pltpu.SemaphoreType.DMA((2,)),
        ],
        1 << 31,
        (pos, mid, w2, const(shift_rows)),
        far_out=(1, 2),
    )
    vq, pool3, sl2_edge, vx_edge = call(
        outer_forward_kernel,
        (
            shape((4, 96, 768), BF),
            shape((256, 128), BF),
            shape((2, 128, 512), BF),
            shape((2, 48, 1280), BF),
        ),
        [
            pltpu.VMEM((4, 192, 128), BF),
            pltpu.VMEM((2, 128, 512), BF),
            pltpu.VMEM((12, 48, 1792), BF),
            pltpu.SemaphoreType.DMA((4,)),
        ],
        1 << 32,
        (
            pos, near, mid, far, inner, w2,
            const(shift_rows), const(pool_two), const(shift_halves), const(pool_three),
        ),
        far_out=(2, 3),
    )
    sent, edges, sl3 = call(
        middle_forward_kernel,
        (
            shape((192, 128), BF),
            shape((2, 128, 128), BF),
            shape((2, 64, 512), BF),
        ),
        [],
        1 << 30,
        (pos, vq, w3f, pool3, cots),
    )
    near, far = swap(sent, sent, "gz")
    near, w4f, w4b, w3b = lax.optimization_barrier((near, w4f, w4b, w3b))
    planes = jnp.concatenate([near[:64], sent[:64], far[:64]], axis=0)
    in1, out1 = swap(
        jnp.concatenate([planes, edges[0]], axis=0),
        jnp.concatenate([planes, edges[1]], axis=0),
        "ch",
    )
    in2, out2 = swap(planes, planes, "ch", 2)
    p4, own_near, own_far, field4, own4 = call(
        deep_kernel,
        (
            shape((128, 128), F32),
            shape((64, 768), BF),
            shape((64, 768), BF),
            shape((6, 192, 256), BF),
            shape((2, 128, 256), BF),
        ),
        [
            pltpu.VMEM((384, 256), BF),
            pltpu.VMEM((4, 384, 256), BF),
            pltpu.VMEM((2, 64, 768), BF),
            pltpu.VMEM((512, 768), BF),
            pltpu.SemaphoreType.DMA((1,)),
        ],
        1 << 32,
        (
            pos, sent, near, far, in1, out1, in2, out2,
            w4f, w4b, const(pool_four), sl3, const(gather_planes), const(shift_planes),
            w3b, const(spread_three),
        ),
        far_in=(14, 15),
    )
    near, far = swap(own_near, own_far, "gz")
    (sent,) = call(
        grads_kernel,
        (shape((8, 288, 128), BF),),
        [pltpu.VMEM((8, 288, 128), F32)],
        1 << 31,
        (pos, field4, own4, own_near, own_far, p4, vq),
    )
    got = lax.all_to_all(sent, "ch", 0, 0, tiled=True)
    grads = got.astype(F32).sum(axis=0).astype(BF)
    pooled_four = got[:, 272:, :16].transpose(1, 0, 2)[:, None]

    (g2,) = call(
        shallow_back_kernel,
        (shape((160, 128), F32),),
        [
            pltpu.VMEM((4, 192, 768), BF),
            pltpu.VMEM((12, 32, 1024), BF),
            pltpu.VMEM((10, 48, 1280), BF),
            pltpu.SemaphoreType.DMA((3,)),
        ],
        1 << 32,
        (
            pos, own_near, own_far, near, far, w3b,
            const(shift_straight), const(shift_cross), const(spread_two),
            sl2_mid, sl2_edge, vx_mid, vx_edge,
        ),
        far_in=(11, 12),
    )
    pieces = jnp.concatenate(
        [grads.reshape(32, 9, 128), g2.astype(BF).reshape(32, 5, 128)], axis=1
    )
    pieces = lax.all_to_all(pieces, "gz", 0, 0, tiled=True).astype(F32).sum(axis=0)
    two = to_all(pieces[9:].astype(BF), "ch").astype(F32).sum(axis=0)
    whole = to_all(jnp.concatenate([pieces[:9], two], axis=0).astype(BF), "gz")
    four, three, two = call(
        write_kernel,
        (shape((216, 128), F32), shape((27, 4, 64), F32), shape((3, 144, 32), F32)),
        [],
        1 << 20,
        (pos, whole),
    )
    grad_four = four.reshape(3, 3, 3, 8, 128).transpose(4, 3, 0, 1, 2)
    grad_three = three.reshape(3, 3, 3, 4, 64).transpose(4, 3, 0, 1, 2)
    grad_two = two.reshape(3, 3, 3, 16, 32).transpose(4, 3, 0, 1, 2)
    return (pooled_four, grad_two, grad_three, grad_four)


def solution(mesh):
    in_specs = (
        P(None, "gz", "ch", None),
        P(),
        P(None, "ch", None, None, None),
        P(None, "ch", None, None, None),
        P("ch", "gz", None, None),
    )
    out_specs = (
        P("ch", "gz", None, None),
        P(),
        P(None, "ch", None, None, None),
        P(None, "ch", None, None, None),
    )
    return jax.shard_map(body, mesh=mesh, in_specs=in_specs, out_specs=out_specs, check_vma=False)
```

```python
import jax
import jax.numpy as jnp
import numpy as np
from jax import lax
from jax.experimental import pallas as pl
from jax.experimental.pallas import tpu as pltpu
from jax.sharding import PartitionSpec as P

BF = jnp.bfloat16
F32 = jnp.float32
VMEM_LIMIT = 12 * 1024 * 1024


def grid(*extents):
    return np.meshgrid(*[np.arange(n) for n in extents], indexing="ij")


def shift_rows():
    out = np.zeros((128, 2, 128), np.float32)
    for x in range(128):
        if x > 0:
            out[x - 1, 0, x] = 1
        if x < 127:
            out[x + 1, 1, x] = 1
    return out.reshape(128, 256)


def shift_halves():
    out = np.zeros((2, 64, 2, 2, 64), np.float32)
    for h in range(2):
        for x in range(64):
            if x > 0:
                out[h, x - 1, 0, h, x] = 1
            if x < 63:
                out[h, x + 1, 1, h, x] = 1
    return out.reshape(128, 256)


def shift_straight():
    side = shift_halves()
    return np.concatenate([side[:, :128], np.eye(128, dtype=np.float32), side[:, 128:]], 1)


def shift_cross():
    straight = shift_straight()
    out = np.zeros((256, 384), np.float32)
    out[64:128] = straight[0:64]
    out[128:192] = straight[64:128]
    return out


def pool_two():
    out = np.zeros((2, 64, 2, 2, 64), np.float32)
    for h in range(2):
        for x in range(64):
            out[h, x, :, h, x] = 0.125
    return out.reshape(256, 128)


def pool_three():
    out = np.zeros((2, 2, 32, 2, 2, 2, 32), np.float32)
    for yc in range(2):
        for zc in range(2):
            for x in range(32):
                out[yc, zc, x, :, zc, yc, x] = 0.125
    return out.reshape(256, 128)


def gather_planes():
    out = np.zeros((5, 2, 2, 32, 2, 8, 32), np.float32)
    for b in range(5):
        for yy in range(2):
            y = 2 * b + yy - 1
            if 0 <= y < 8:
                for zz in range(2):
                    for x in range(32):
                        out[b, zz, yy, x, zz, y, x] = 1
    return out.reshape(640, 512)


def shift_planes():
    out = np.zeros((8, 32, 3, 8, 32), np.float32)
    for kx in range(3):
        for y in range(8):
            for x in range(32):
                if 0 <= x + kx - 1 < 32:
                    out[y, x + kx - 1, kx, y, x] = 1
    return out.reshape(256, 768)


def pool_four():
    out = np.zeros((8, 16, 2, 128), np.float32)
    for x in range(16):
        out[2:4, x, :, x] = 0.125
    return out.reshape(256, 128)


def spread_three():
    out = np.zeros((2, 8, 32, 6, 2, 32, 2), np.float32)
    for r in range(6):
        cell = (r - 1) // 2 + 1
        for h in range(2):
            for x in range(32):
                out[h, cell, x, r, h, x, :] = 0.125
    return out.reshape(512, 768)


def spread_two():
    out = np.zeros((2, 64, 2, 64, 2), np.float32)
    for h in range(2):
        for x in range(64):
            out[h, x, h, x, :] = 0.125
    return out.reshape(128, 256)


def const(build):
    return jnp.asarray(build(), BF)


def dot(a, b):
    return lax.dot_general(a, b, (((1,), (0,)), ((), ())), preferred_element_type=F32)


def dot_nt(a, b):
    return lax.dot_general(a, b, (((1,), (1,)), ((), ())), preferred_element_type=F32)


def fold_rows(parts):
    third = parts.shape[0] // 3
    total = parts[:third]
    for ky in (1, 2):
        total = total + pltpu.roll(parts[ky * third : (ky + 1) * third], 256 - 32 * ky, 1)
    return total


def sigmoid(u):
    return 0.5 * jnp.tanh(0.5 * u) + 0.5


def act_of(u, s):
    return u * (0.3 + 0.7 * s)


def slope_of(u, s):
    return 0.3 + 0.7 * (s + u * s * (1.0 - s))


def call(kernel, out_shape, scratch, flops, args, far_in=(), far_out=()):
    def place(far):
        return pl.BlockSpec(memory_space=pltpu.HBM if far else pltpu.VMEM)

    specs = [pl.BlockSpec(memory_space=pltpu.SMEM)] + [
        place(n in far_in) for n in range(1, len(args))
    ]
    args = [
        pltpu.with_memory_space_constraint(a, pltpu.HBM) if n in far_in else a
        for n, a in enumerate(args)
    ]
    return pl.pallas_call(
        kernel,
        out_shape=tuple(
            pltpu.HBM(o.shape, o.dtype) if n in far_out else o for n, o in enumerate(out_shape)
        ),
        in_specs=specs,
        out_specs=tuple(place(n in far_out) for n in range(len(out_shape))),
        scratch_shapes=scratch,
        compiler_params=pltpu.CompilerParams(vmem_limit_bytes=VMEM_LIMIT),
        cost_estimate=pl.CostEstimate(flops=flops, bytes_accessed=1 << 20, transcendentals=0),
    )(*args)


def shift_plane(field, shift, out):
    sides = dot(field, shift)
    for y in range(14):
        lanes = slice(y * 128, y * 128 + 128)
        rows = slice(y * 16, y * 16 + 16)
        out[0:16, lanes] = sides[rows, :128].astype(BF)
        out[16:32, lanes] = field[rows]
        out[32:48, lanes] = sides[rows, 128:].astype(BF)


def layer_two(pos, zc, planes, filters, sums, slopes):
    zg = 4 * pos[0] + zc - 1
    z_in = jnp.logical_and(zg >= 0, zg < 128)
    for q, (ya, yb) in enumerate(((1, 2), (3, 4), (0, 5))):
        rhs = jnp.concatenate(
            [
                jnp.concatenate(
                    [
                        plane[:, (2 * ya + yy) * 128 : (2 * ya + yy + 1) * 128],
                        plane[:, (2 * yb + yy) * 128 : (2 * yb + yy + 1) * 128],
                    ],
                    axis=1,
                )
                for plane in planes
                for yy in range(4)
            ],
            axis=0,
        )
        pre = dot(filters, rhs)
        s = sigmoid(pre)
        a = act_of(pre, s)
        if q < 2 and slopes is not None:
            slopes[:, q * 256 : q * 256 + 256] = slope_of(pre, s).astype(BF)
        total = (a[0:32] + a[32:64]) + (a[64:96] + a[96:128])
        for c, yc in enumerate((ya, yb)):
            yg = 4 * pos[1] + yc - 1
            inside = jnp.logical_and(z_in, jnp.logical_and(yg >= 0, yg < 32))
            cell = jnp.where(inside, total[:, c * 128 : c * 128 + 128], 0.0)
            sums[yc * 32 : yc * 32 + 32] = cell.astype(BF)


def inner_forward_kernel(pos, mid, w2, shift2, sums, slopes_far, vx_far, vm, slopes, sems):
    shift = shift2[...]

    @pl.loop(0, 8, unroll=2)
    def _(z):
        shift_plane(mid[z].reshape(224, 128), shift, vm.at[z])

    vx_copy = pltpu.make_async_copy(vm.at[:, :, 256:1536], vx_far, sems.at[0])
    vx_copy.start()
    filters = w2[...]
    for n in range(2):
        planes = [vm.at[1 + 2 * n + zz] for zz in range(4)]
        layer_two(pos, n + 2, planes, filters, sums.at[n], slopes.at[n])
    slopes_copy = pltpu.make_async_copy(slopes, slopes_far, sems.at[1])
    slopes_copy.start()
    vx_copy.wait()
    slopes_copy.wait()


def outer_forward_kernel(
    pos, near, mid, far, inner, w2, shift2, pool2, shift3, pool3, vq, pool3_out, slopes_far, vx_far,
    sums, slopes, vh, sems,
):
    odd = pos[0] % 2 == 1
    pool3_out[...] = pool3[...]
    shift = shift2[...]
    for z in range(3):
        one = near[z].reshape(224, 128).astype(F32)
        two = far[z].reshape(224, 128).astype(F32)
        shift_plane(jnp.where(odd, one, two).astype(BF), shift, vh.at[z])
        shift_plane(jnp.where(odd, two, one).astype(BF), shift, vh.at[9 + z])
        shift_plane(mid[z].reshape(224, 128), shift, vh.at[3 + z])
        shift_plane(mid[5 + z].reshape(224, 128), shift, vh.at[6 + z])
    late = [
        pltpu.make_async_copy(vh.at[2, :, 256:1536], vx_far.at[0], sems.at[0]),
        pltpu.make_async_copy(vh.at[9, :, 256:1536], vx_far.at[1], sems.at[1]),
        pltpu.make_async_copy(slopes.at[0], slopes_far.at[0], sems.at[2]),
        pltpu.make_async_copy(slopes.at[1], slopes_far.at[1], sems.at[3]),
    ]
    late[0].start()
    late[1].start()
    filters = w2[...]
    held = [vh.at[z] for z in range(6)] + [None, None] + [vh.at[z] for z in range(6, 12)]
    for zc, at, slot in ((1, 1, 0), (4, 2, 1), (0, 0, None), (5, 3, None)):
        out = None if slot is None else slopes.at[slot]
        layer_two(pos, zc, held[2 * zc : 2 * zc + 4], filters, sums.at[at], out)
        if slot is not None:
            late[2 + slot].start()

    pool = pool2[...]
    halves = shift3[...]
    cells = [sums[0], sums[1], inner[0], inner[1], sums[2], sums[3]]
    for j in range(4):
        pair = jnp.concatenate([cells[j], cells[j + 2]], axis=1)
        pooled = dot(pair, pool).astype(BF)
        sides = dot(pooled, halves)
        for y in range(6):
            rows = slice(y * 32, y * 32 + 32)
            lanes = slice(y * 128, y * 128 + 128)
            vq[j, 0:32, lanes] = sides[rows, :128].astype(BF)
            vq[j, 32:64, lanes] = pooled[rows]
            vq[j, 64:96, lanes] = sides[rows, 128:].astype(BF)
    for copy in late:
        copy.wait()


def middle_forward_kernel(pos, vq, w3, pool3, cot, sent, edges, sl3):
    sent[64:192] = cot[...]
    filters = w3[...]
    cells = [None, None]
    for zp in range(2):
        for n in range(2):
            blocks = [
                vq[zp + kz, :, (2 * n + ky) * 128 : (2 * n + ky + 2) * 128]
                for kz in range(3)
                for ky in range(3)
            ]
            pre = dot(filters, jnp.concatenate(blocks, axis=0))
            s = sigmoid(pre)
            sl3[zp, :, n * 256 : n * 256 + 256] = slope_of(pre, s).astype(BF)
            a = act_of(pre, s)
            part = a[:, :128] + a[:, 128:]
            cells[n] = part if zp == 0 else cells[n] + part
    both = jnp.concatenate(cells, axis=1).astype(BF)
    sent[0:64] = dot(both, pool3[...]).astype(BF)
    odd = pos[1] % 2
    for zp in range(2):
        top, bottom = sl3[zp, :, 384:512], sl3[zp, :, 0:128]
        edges[odd, zp * 64 : zp * 64 + 64] = top
        edges[1 - odd, zp * 64 : zp * 64 + 64] = bottom


def deep_kernel(
    pos, own3, near, far, in1, out1, in2, out2, w4f, w4b, pool4, sl3, planes_of, shift4, w3b, spread_far,
    p4, near_out, far_out, field, own,
    planes, back_in, d3, spread3, sems,
):
    spread_copy = pltpu.make_async_copy(spread_far, spread3, sems.at[0])
    spread_copy.start()
    odd, ch = pos[0] % 2, pos[1]

    def pick(cond, one, two):
        return jnp.where(cond, one.astype(F32), two.astype(F32)).astype(BF)

    def in_order(blocks):
        first, second, third = blocks
        return [pick(odd == 1, first, third), second, pick(odd == 1, third, first)]

    def neighbour(inside, outside, upper, rows):
        one, two = inside[rows], outside[rows]
        return pick(upper, one, two), pick(upper, two, one)

    odd_y, odd_pair = ch % 2 == 1, ch % 4 >= 2
    mine = jnp.concatenate([near[0:64], own3[0:64], far[0:64]], axis=0)
    below1, above1 = neighbour(in1, out1, odd_y, slice(0, 192))
    below2, above2 = neighbour(in2, out2, odd_pair, slice(0, 192))
    parts = [
        jnp.concatenate(in_order([p[0:64], p[64:128], p[128:192]]), axis=0)
        for p in (below2, below1, mine, above1, above2)
    ]
    cots = in_order([near[64:192], own3[64:192], far[64:192]])
    edge_low, edge_high = neighbour(in1, out1, odd_y, slice(192, 320))
    flat = dot(jnp.concatenate(parts, axis=1), planes_of[...]).astype(BF)
    for zb in range(3):
        for zz in range(2):
            p = 2 * zb + zz
            planes[p * 64 : p * 64 + 64] = flat[zb * 64 : zb * 64 + 64, zz * 256 : zz * 256 + 256]
    for kx in range(3):
        moved = dot(planes[...], shift4[:, kx * 256 : kx * 256 + 256]).astype(BF)
        for p in range(6):
            field[p, kx * 64 : kx * 64 + 64] = moved[p * 64 : p * 64 + 64]

    row = lax.broadcasted_iota(jnp.int32, (128, 256), 0)
    lane = lax.broadcasted_iota(jnp.int32, (128, 256), 1)
    source_y, source_x = row // 16, row % 16
    y, x = lane // 32, lane % 32
    match = (source_x == x // 2) & (source_y == ch - 1 + y // 2) & (y < 6)
    spread = jnp.where(match, 0.125, 0.0).astype(BF)
    inner = lax.broadcasted_iota(jnp.int32, (128, 256), 1) // 64 == 1

    filters = w4f[...]
    pooled = None
    deltas = []
    for z in range(4):
        pre = fold_rows(dot(filters, field[z : z + 3].reshape(576, 256)))
        s = sigmoid(pre)
        wide = dot(cots[(z + 1) // 2], spread)
        delta = wide * slope_of(pre, s)
        deltas.append(delta.astype(BF))
        if z in (1, 2):
            own[z - 1] = jnp.where(inner, delta, 0.0).astype(BF)
            a = act_of(pre, s)
            pooled = a if pooled is None else pooled + a
    high = pooled.astype(BF)
    low = (pooled - high.astype(F32)).astype(BF)
    p4[...] = dot(high, pool4[...]) + dot(low, pool4[...])

    stacked = jnp.concatenate(deltas, axis=0)
    for kx in range(3):
        moved = dot(stacked, shift4[:, kx * 256 : kx * 256 + 256]).astype(BF)
        for z in range(4):
            back_in[z, kx * 128 : kx * 128 + 128] = moved[z * 128 : z * 128 + 128]
    filters = w4b[...]
    back = [
        fold_rows(dot(filters, back_in[z : z + 3].reshape(1152, 256))).astype(BF)
        for z in range(2)
    ]
    spread_copy.wait()
    wide = dot(jnp.concatenate(back, axis=1), spread3[...])
    for r in range(6):
        yg = 4 * ch + r - 1
        inside = jnp.logical_and(yg >= 0, yg < 32)
        lanes = slice(r * 128, r * 128 + 128)
        value = jnp.where(inside, wide[:, lanes], 0.0)
        for zp in range(2):
            rows = slice(zp * 64, zp * 64 + 64)
            if r == 0:
                slope = edge_low[rows]
            elif r == 5:
                slope = edge_high[rows]
            else:
                slope = sl3[zp, :, (r - 1) * 128 : r * 128]
            d3[zp, :, lanes] = (value * slope.astype(F32)).astype(BF)
    near_out[...] = d3[1 - odd]
    far_out[...] = d3[odd]


def own_packs(pos, near, far):
    odd = pos[0] % 2 == 1
    one, two = near[...].astype(F32), far[...].astype(F32)
    return jnp.where(odd, one, two).astype(BF), jnp.where(odd, two, one).astype(BF)


def grads_kernel(pos, field, own, near, far, p4, vq, sent, out):
    packs = own_packs(pos, near, far)
    rows = []
    for ky in range(3):
        moved = [own[z].astype(F32) for z in range(2)]
        if ky > 0:
            moved = [pltpu.roll(m, 32 * ky, 1) for m in moved]
        rows.append(jnp.concatenate([m.astype(BF) for m in moved], axis=1))
    right = jnp.concatenate(rows, axis=0)
    for kz in range(3):
        left = jnp.concatenate([field[1 + kz], field[2 + kz]], axis=1)
        res = dot_nt(left, right)
        for k in range(9):
            for c in range(8):
                at = (kz * 9 + k) * 8
                row, lane = k % 3 * 64 + c * 8, k // 3 * 128
                out[c, at : at + 8] = res[row : row + 8, lane : lane + 128]
    total = None
    zero = jnp.zeros((64, 512), BF)
    for j in range(4):
        rows = []
        for kz in range(3):
            zp = j - kz
            rows.append(packs[zp][:, 128:640] if 0 <= zp < 2 else zero)
        left = jnp.concatenate(
            [vq[j, :, ky * 128 : ky * 128 + 512] for ky in range(3)], axis=0
        )
        res = dot_nt(left, jnp.concatenate(rows, axis=0))
        total = res if total is None else total + res
    for k in range(9):
        for c in range(8):
            at = 216 + k * 4
            piece = total[k * 32 + c * 4 : k * 32 + c * 4 + 4]
            out[c, at : at + 4] = piece[:, :128]
            at, lanes = (252 + k * 4, slice(0, 64)) if k < 5 else (232 + k * 4, slice(64, 128))
            out[c, at : at + 4, lanes] = piece[:, 128:]
    for c in range(8):
        out[c, 268:272, 64:128] = jnp.zeros((4, 64), F32)
        out[c, 272:288] = p4[c * 16 : c * 16 + 16]
        sent[c] = out[c].astype(BF)


def shallow_back_kernel(
    pos, own_near, own_far, near, far, w3b, straight, cross, spread2, sl2_mid, sl2_edge, vx_mid, vx_edge,
    g2, ds, d2, vx, sems,
):
    vx_copies = [
        pltpu.make_async_copy(vx_mid, vx.at[1:9], sems.at[0]),
        pltpu.make_async_copy(vx_edge.at[0], vx.at[0], sems.at[1]),
        pltpu.make_async_copy(vx_edge.at[1], vx.at[9], sems.at[2]),
    ]
    for copy in vx_copies:
        copy.start()
    sl2 = (sl2_edge.at[0], sl2_mid.at[0], sl2_mid.at[1], sl2_edge.at[1])

    def rows_of(value):
        return jnp.concatenate([value[:, y * 128 : y * 128 + 128] for y in range(6)], axis=0)

    odd = pos[0] % 2 == 1
    one, two = rows_of(near).astype(F32), rows_of(far).astype(F32)
    above = jnp.where(odd, one, two).astype(BF)
    below = jnp.where(odd, two, one).astype(BF)
    first, second = [rows_of(pack) for pack in own_packs(pos, own_near, own_far)]
    direct, across = straight[...], cross[...]
    sources = (
        (jnp.concatenate([above, second], axis=1), across),
        (first, direct),
        (second, direct),
        (jnp.concatenate([first, below], axis=1), across),
    )
    for j, (source, matrix) in enumerate(sources):
        moved = dot(source, matrix).astype(BF)
        for y in range(6):
            for kx in range(3):
                piece = moved[y * 64 : y * 64 + 64, kx * 128 : kx * 128 + 128]
                ds[j, kx * 64 : kx * 64 + 64, y * 128 : y * 128 + 128] = piece

    for z in (0, 1, 10, 11):
        d2[z] = jnp.zeros((32, 1024), BF)
    filters = w3b[...]
    backs = []
    for zp in range(2):
        parts = dot(filters, ds[zp : zp + 3].reshape(576, 768))
        for y in range(4):
            back = parts[0:32, y * 128 : y * 128 + 128]
            for ky in (1, 2):
                back = back + parts[ky * 32 : ky * 32 + 32, (y + ky) * 128 : (y + ky + 1) * 128]
            backs.append(back.astype(BF))
    wide = dot(jnp.concatenate(backs, axis=0), spread2[...])
    for zp in range(2):
        for y in range(4):
            at = (zp * 4 + y) * 32
            for h in range(2):
                value = wide[at : at + 32, h * 128 : h * 128 + 128]
                z = zp + 2 * h
                for dz in range(2):
                    for dy in range(2):
                        rows = slice((dz * 2 + dy) * 32, (dz * 2 + dy) * 32 + 32)
                        slope = sl2[z][rows, y * 128 : y * 128 + 128].astype(F32)
                        lanes = slice((2 * y + dy) * 128, (2 * y + dy) * 128 + 128)
                        d2[2 * z + dz + 2, :, lanes] = (value * slope).astype(BF)

    vx_copies[0].wait()
    total = None
    for z in (1, 2, 3, 4, 5, 6, 7, 8, 0, 9):
        if z == 0:
            vx_copies[1].wait()
            vx_copies[2].wait()
        left = jnp.concatenate(
            [vx[z, :, ky * 128 : ky * 128 + 1024] for ky in range(3)], axis=0
        )
        right = jnp.concatenate([d2[z + 2 - kz] for kz in range(3)], axis=0)
        part = dot_nt(left, right)
        total = part if total is None else total + part
    g2[...] = jnp.zeros((160, 128), BF)
    g2[0:144, 0:96] = total.astype(BF)


def write_kernel(pos, whole, four, three, two):
    deep = whole[:, 0:9].astype(F32).reshape(288, 128)
    four[...] = deep[:216]
    for k in range(9):
        low = deep[216 + k * 4 : 220 + k * 4]
        at, lanes = (252 + k * 4, slice(0, 64)) if k < 5 else (232 + k * 4, slice(64, 128))
        high = deep[at : at + 4, lanes]
        three[k] = low[:, 0:64]
        three[9 + k] = low[:, 64:128]
        three[18 + k] = high
    shallow = whole[:, 9:14].astype(F32).reshape(160, 128)
    for kz in range(3):
        two[kz] = shallow[:144, kz * 32 : kz * 32 + 32]


def swap(one, two, axis, step=1):
    count = lax.axis_size(axis)
    inside = [(i, i ^ step) for i in range(count)]
    outside = [(i, i + step) for i in range(count - step) if i % (2 * step) >= step]
    outside = outside + [(b, a) for a, b in outside]
    return lax.ppermute(one, axis, inside), lax.ppermute(two, axis, outside)


def swap_cores(value):
    return lax.ppermute(value, "gz", [(i, i ^ 1) for i in range(lax.axis_size("gz"))])


def to_all(piece, axis):
    count = lax.axis_size(axis)
    copies = jnp.broadcast_to(piece[None], (count,) + piece.shape)
    return lax.all_to_all(copies, axis, 0, 0, tiled=True)


def band(filters):
    taps = filters.transpose(0, 2, 3, 4, 1).reshape(32, 3, 3, 48)
    rows = [
        jnp.pad(taps, ((0, 0), (dz, 1 - dz), (dy, 1 - dy), (0, 0)))
        for dz in range(2)
        for dy in range(2)
    ]
    return jnp.stack(rows).reshape(128, 768)


def body(volume, filters_two, filters_three, filters_four, cotangent):
    gz, ch = lax.axis_index("gz"), lax.axis_index("ch")
    pos = jnp.stack([gz, ch]).astype(jnp.int32)
    odd_z, odd_y = gz % 2, ch % 2
    shape = jax.ShapeDtypeStruct

    field = volume.transpose(1, 2, 0, 3)
    near, far = swap(
        lax.dynamic_slice_in_dim(volume, 5 * (1 - odd_y), 3, 2).transpose(1, 2, 0, 3),
        lax.dynamic_slice_in_dim(volume, 5 * odd_y, 3, 2).transpose(1, 2, 0, 3),
        "ch",
    )
    low = jnp.where(odd_y == 1, near, far)
    high = jnp.where(odd_y == 1, far, near)
    mid = jnp.concatenate([low, field, high], axis=1)

    four = filters_four.transpose(2, 3, 4, 1, 0).reshape(216, 128)
    three = filters_three.transpose(2, 3, 4, 1, 0).reshape(108, 64)
    three = jnp.pad(three, ((0, 0), (0, 64)))
    cot = cotangent.reshape(16, 128)
    held = jnp.concatenate(
        [
            cot,
            lax.dynamic_slice_in_dim(four, 108 * odd_z, 108, 0),
            lax.dynamic_slice_in_dim(three, 54 * odd_z, 54, 0),
        ],
        axis=0,
    )
    held = jnp.broadcast_to(held[None], (8, 178, 128))
    near, far = swap(
        lax.dynamic_slice_in_dim(mid, 5 * (1 - odd_z), 3, 0),
        lax.dynamic_slice_in_dim(mid, 5 * odd_z, 3, 0),
        "gz",
    )
    near, two = lax.optimization_barrier((near, filters_two))
    w2 = band(two)
    all_of = lax.all_to_all(held, "ch", 0, 0, tiled=True)
    mine, cots = lax.optimization_barrier((all_of[:, 16:], all_of[:, :16].reshape(128, 128)))
    other = swap_cores(mine)
    first = jnp.where(odd_z == 1, other, mine)
    second = jnp.where(odd_z == 1, mine, other)
    four = jnp.concatenate([first[:, :108], second[:, :108]], axis=1).reshape(8, 27, 8, 128)
    three = jnp.concatenate([first[:, 108:, :64], second[:, 108:, :64]], axis=1)
    three = three.reshape(8, 27, 4, 64)
    w3f = three.transpose(3, 1, 0, 2).reshape(64, 864)
    back = three[:, ::-1].reshape(8, 3, 3, 3, 4, 64)
    w3b = back.transpose(2, 0, 4, 1, 3, 5).reshape(96, 576)
    w4f = four.reshape(8, 3, 3, 3, 8, 128).transpose(2, 5, 1, 3, 0, 4).reshape(384, 576)
    back = four[:, ::-1].reshape(8, 3, 3, 3, 8, 128)
    w4b = back.transpose(2, 0, 4, 1, 3, 5).reshape(192, 1152)

    inner, sl2_mid, vx_mid = call(
        inner_forward_kernel,
        (
            shape((2, 192, 128), BF),
            shape((2, 128, 512), BF),
            shape((8, 48, 1280), BF),
        ),
        [
            pltpu.VMEM((8, 48, 1792), BF),
            pltpu.VMEM((2, 128, 512), BF),
            pltpu.SemaphoreType.DMA((2,)),
        ],
        1 << 31,
        (pos, mid, w2, const(shift_rows)),
        far_out=(1, 2),
    )
    vq, pool3, sl2_edge, vx_edge = call(
        outer_forward_kernel,
        (
            shape((4, 96, 768), BF),
            shape((256, 128), BF),
            shape((2, 128, 512), BF),
            shape((2, 48, 1280), BF),
        ),
        [
            pltpu.VMEM((4, 192, 128), BF),
            pltpu.VMEM((2, 128, 512), BF),
            pltpu.VMEM((12, 48, 1792), BF),
            pltpu.SemaphoreType.DMA((4,)),
        ],
        1 << 32,
        (
            pos, near, mid, far, inner, w2,
            const(shift_rows), const(pool_two), const(shift_halves), const(pool_three),
        ),
        far_out=(2, 3),
    )
    sent, edges, sl3 = call(
        middle_forward_kernel,
        (
            shape((192, 128), BF),
            shape((2, 128, 128), BF),
            shape((2, 64, 512), BF),
        ),
        [],
        1 << 30,
        (pos, vq, w3f, pool3, cots),
    )
    near, far = swap(sent, sent, "gz")
    near, w4f, w4b, w3b = lax.optimization_barrier((near, w4f, w4b, w3b))
    planes = jnp.concatenate([near[:64], sent[:64], far[:64]], axis=0)
    in1, out1 = swap(
        jnp.concatenate([planes, edges[0]], axis=0),
        jnp.concatenate([planes, edges[1]], axis=0),
        "ch",
    )
    in2, out2 = swap(planes, planes, "ch", 2)
    p4, own_near, own_far, field4, own4 = call(
        deep_kernel,
        (
            shape((128, 128), F32),
            shape((64, 768), BF),
            shape((64, 768), BF),
            shape((6, 192, 256), BF),
            shape((2, 128, 256), BF),
        ),
        [
            pltpu.VMEM((384, 256), BF),
            pltpu.VMEM((4, 384, 256), BF),
            pltpu.VMEM((2, 64, 768), BF),
            pltpu.VMEM((512, 768), BF),
            pltpu.SemaphoreType.DMA((1,)),
        ],
        1 << 32,
        (
            pos, sent, near, far, in1, out1, in2, out2,
            w4f, w4b, const(pool_four), sl3, const(gather_planes), const(shift_planes),
            w3b, const(spread_three),
        ),
        far_in=(14, 15),
    )
    near, far = swap(own_near, own_far, "gz")
    (sent,) = call(
        grads_kernel,
        (shape((8, 288, 128), BF),),
        [pltpu.VMEM((8, 288, 128), F32)],
        1 << 31,
        (pos, field4, own4, own_near, own_far, p4, vq),
    )
    got = lax.all_to_all(sent, "ch", 0, 0, tiled=True)
    grads = got.astype(F32).sum(axis=0).astype(BF)
    pooled_four = got[:, 272:, :16].transpose(1, 0, 2)[:, None]

    (g2,) = call(
        shallow_back_kernel,
        (shape((160, 128), BF),),
        [
            pltpu.VMEM((4, 192, 768), BF),
            pltpu.VMEM((12, 32, 1024), BF),
            pltpu.VMEM((10, 48, 1280), BF),
            pltpu.SemaphoreType.DMA((3,)),
        ],
        1 << 32,
        (
            pos, own_near, own_far, near, far, w3b,
            const(shift_straight), const(shift_cross), const(spread_two),
            sl2_mid, sl2_edge, vx_mid, vx_edge,
        ),
        far_in=(11, 12),
    )
    pieces = jnp.concatenate(
        [grads.reshape(32, 9, 128), g2.reshape(32, 5, 128)], axis=1
    )
    pieces = lax.all_to_all(pieces, "gz", 0, 0, tiled=True).astype(F32).sum(axis=0)
    two = to_all(pieces[9:].astype(BF), "ch").astype(F32).sum(axis=0)
    whole = to_all(jnp.concatenate([pieces[:9], two], axis=0).astype(BF), "gz")
    four, three, two = call(
        write_kernel,
        (shape((216, 128), F32), shape((27, 4, 64), F32), shape((3, 144, 32), F32)),
        [],
        1 << 20,
        (pos, whole),
    )
    grad_four = four.reshape(3, 3, 3, 8, 128).transpose(4, 3, 0, 1, 2)
    grad_three = three.reshape(3, 3, 3, 4, 64).transpose(4, 3, 0, 1, 2)
    grad_two = two.reshape(3, 3, 3, 16, 32).transpose(4, 3, 0, 1, 2)
    return (pooled_four, grad_two, grad_three, grad_four)


def solution(mesh):
    in_specs = (
        P(None, "gz", "ch", None),
        P(),
        P(None, "ch", None, None, None),
        P(None, "ch", None, None, None),
        P("ch", "gz", None, None),
    )
    out_specs = (
        P("ch", "gz", None, None),
        P(),
        P(None, "ch", None, None, None),
        P(None, "ch", None, None, None),
    )
    return jax.shard_map(body, mesh=mesh, in_specs=in_specs, out_specs=out_specs, check_vma=False)
```

```python
import jax
import jax.numpy as jnp
import numpy as np
from jax import lax
from jax.experimental import pallas as pl
from jax.experimental.pallas import tpu as pltpu
from jax.sharding import PartitionSpec as P

BF = jnp.bfloat16
F32 = jnp.float32
VMEM_LIMIT = 12 * 1024 * 1024


def grid(*extents):
    return np.meshgrid(*[np.arange(n) for n in extents], indexing="ij")


def shift_rows():
    out = np.zeros((128, 2, 128), np.float32)
    for x in range(128):
        if x > 0:
            out[x - 1, 0, x] = 1
        if x < 127:
            out[x + 1, 1, x] = 1
    return out.reshape(128, 256)


def shift_halves():
    out = np.zeros((2, 64, 2, 2, 64), np.float32)
    for h in range(2):
        for x in range(64):
            if x > 0:
                out[h, x - 1, 0, h, x] = 1
            if x < 63:
                out[h, x + 1, 1, h, x] = 1
    return out.reshape(128, 256)


def shift_straight():
    side = shift_halves()
    return np.concatenate([side[:, :128], np.eye(128, dtype=np.float32), side[:, 128:]], 1)


def shift_cross():
    straight = shift_straight()
    out = np.zeros((256, 384), np.float32)
    out[64:128] = straight[0:64]
    out[128:192] = straight[64:128]
    return out


def pool_two():
    out = np.zeros((2, 64, 2, 2, 64), np.float32)
    for h in range(2):
        for x in range(64):
            out[h, x, :, h, x] = 0.125
    return out.reshape(256, 128)


def pool_three():
    out = np.zeros((2, 2, 32, 2, 2, 2, 32), np.float32)
    for yc in range(2):
        for zc in range(2):
            for x in range(32):
                out[yc, zc, x, :, zc, yc, x] = 0.125
    return out.reshape(256, 128)


def gather_planes():
    out = np.zeros((5, 2, 2, 32, 2, 8, 32), np.float32)
    for b in range(5):
        for yy in range(2):
            y = 2 * b + yy - 1
            if 0 <= y < 8:
                for zz in range(2):
                    for x in range(32):
                        out[b, zz, yy, x, zz, y, x] = 1
    return out.reshape(640, 512)


def shift_planes():
    out = np.zeros((8, 32, 3, 8, 32), np.float32)
    for kx in range(3):
        for y in range(8):
            for x in range(32):
                if 0 <= x + kx - 1 < 32:
                    out[y, x + kx - 1, kx, y, x] = 1
    return out.reshape(256, 768)


def pool_four():
    out = np.zeros((8, 16, 2, 128), np.float32)
    for x in range(16):
        out[2:4, x, :, x] = 0.125
    return out.reshape(256, 128)


def spread_three():
    out = np.zeros((2, 8, 32, 6, 2, 32, 2), np.float32)
    for r in range(6):
        cell = (r - 1) // 2 + 1
        for h in range(2):
            for x in range(32):
                out[h, cell, x, r, h, x, :] = 0.125
    return out.reshape(512, 768)


def spread_two():
    out = np.zeros((2, 64, 2, 64, 2), np.float32)
    for h in range(2):
        for x in range(64):
            out[h, x, h, x, :] = 0.125
    return out.reshape(128, 256)


def const(build):
    return jnp.asarray(build(), BF)


def dot(a, b):
    return lax.dot_general(a, b, (((1,), (0,)), ((), ())), preferred_element_type=F32)


def dot_nt(a, b):
    return lax.dot_general(a, b, (((1,), (1,)), ((), ())), preferred_element_type=F32)


def fold_rows(parts):
    third = parts.shape[0] // 3
    total = parts[:third]
    for ky in (1, 2):
        total = total + pltpu.roll(parts[ky * third : (ky + 1) * third], 256 - 32 * ky, 1)
    return total


def sigmoid(u):
    return 0.5 * jnp.tanh(0.5 * u) + 0.5


def act_of(u, s):
    return u * (0.3 + 0.7 * s)


def slope_of(u, s):
    return 0.3 + 0.7 * (s + u * s * (1.0 - s))


def call(kernel, out_shape, scratch, flops, args, far_in=(), far_out=()):
    def place(far):
        return pl.BlockSpec(memory_space=pltpu.HBM if far else pltpu.VMEM)

    specs = [pl.BlockSpec(memory_space=pltpu.SMEM)] + [
        place(n in far_in) for n in range(1, len(args))
    ]
    args = [
        pltpu.with_memory_space_constraint(a, pltpu.HBM) if n in far_in else a
        for n, a in enumerate(args)
    ]
    return pl.pallas_call(
        kernel,
        out_shape=tuple(
            pltpu.HBM(o.shape, o.dtype) if n in far_out else o for n, o in enumerate(out_shape)
        ),
        in_specs=specs,
        out_specs=tuple(place(n in far_out) for n in range(len(out_shape))),
        scratch_shapes=scratch,
        compiler_params=pltpu.CompilerParams(vmem_limit_bytes=VMEM_LIMIT),
        cost_estimate=pl.CostEstimate(flops=flops, bytes_accessed=1 << 20, transcendentals=0),
    )(*args)


def shift_plane(field, shift, out):
    sides = dot(field, shift)
    for y in range(14):
        lanes = slice(y * 128, y * 128 + 128)
        rows = slice(y * 16, y * 16 + 16)
        out[0:16, lanes] = sides[rows, :128].astype(BF)
        out[16:32, lanes] = field[rows]
        out[32:48, lanes] = sides[rows, 128:].astype(BF)


def layer_two(pos, zc, planes, filters, sums, slopes):
    zg = 4 * pos[0] + zc - 1
    z_in = jnp.logical_and(zg >= 0, zg < 128)
    for q, (ya, yb) in enumerate(((1, 2), (3, 4), (0, 5))):
        rhs = jnp.concatenate(
            [
                jnp.concatenate(
                    [
                        plane[:, (2 * ya + yy) * 128 : (2 * ya + yy + 1) * 128],
                        plane[:, (2 * yb + yy) * 128 : (2 * yb + yy + 1) * 128],
                    ],
                    axis=1,
                )
                for plane in planes
                for yy in range(4)
            ],
            axis=0,
        )
        pre = dot(filters, rhs)
        s = sigmoid(pre)
        a = act_of(pre, s)
        if q < 2 and slopes is not None:
            slopes[:, q * 256 : q * 256 + 256] = slope_of(pre, s).astype(BF)
        total = (a[0:32] + a[32:64]) + (a[64:96] + a[96:128])
        for c, yc in enumerate((ya, yb)):
            yg = 4 * pos[1] + yc - 1
            inside = jnp.logical_and(z_in, jnp.logical_and(yg >= 0, yg < 32))
            cell = jnp.where(inside, total[:, c * 128 : c * 128 + 128], 0.0)
            sums[yc * 32 : yc * 32 + 32] = cell.astype(BF)


def inner_forward_kernel(pos, mid, w2, shift2, sums, slopes_far, vx_far, vm, slopes, sems):
    shift = shift2[...]

    @pl.loop(0, 8, unroll=2)
    def _(z):
        shift_plane(mid[z].reshape(224, 128), shift, vm.at[z])

    vx_copy = pltpu.make_async_copy(vm.at[:, :, 256:1536], vx_far, sems.at[0])
    vx_copy.start()
    filters = w2[...]
    for n in range(2):
        planes = [vm.at[1 + 2 * n + zz] for zz in range(4)]
        layer_two(pos, n + 2, planes, filters, sums.at[n], slopes.at[n])
    slopes_copy = pltpu.make_async_copy(slopes, slopes_far, sems.at[1])
    slopes_copy.start()
    vx_copy.wait()
    slopes_copy.wait()


def outer_forward_kernel(
    pos, near, mid, far, inner, w2, shift2, pool2, shift3, pool3, vq, pool3_out, slopes_far, vx_far,
    sums, slopes, vh, sems,
):
    odd = pos[0] % 2 == 1
    pool3_out[...] = pool3[...]
    shift = shift2[...]
    for z in range(3):
        one = near[z].reshape(224, 128).astype(F32)
        two = far[z].reshape(224, 128).astype(F32)
        shift_plane(jnp.where(odd, one, two).astype(BF), shift, vh.at[z])
        shift_plane(jnp.where(odd, two, one).astype(BF), shift, vh.at[9 + z])
        shift_plane(mid[z].reshape(224, 128), shift, vh.at[3 + z])
        shift_plane(mid[5 + z].reshape(224, 128), shift, vh.at[6 + z])
    late = [
        pltpu.make_async_copy(vh.at[2, :, 256:1536], vx_far.at[0], sems.at[0]),
        pltpu.make_async_copy(vh.at[9, :, 256:1536], vx_far.at[1], sems.at[1]),
        pltpu.make_async_copy(slopes.at[0], slopes_far.at[0], sems.at[2]),
        pltpu.make_async_copy(slopes.at[1], slopes_far.at[1], sems.at[3]),
    ]
    late[0].start()
    late[1].start()
    filters = w2[...]
    held = [vh.at[z] for z in range(6)] + [None, None] + [vh.at[z] for z in range(6, 12)]
    for zc, at, slot in ((1, 1, 0), (4, 2, 1), (0, 0, None), (5, 3, None)):
        out = None if slot is None else slopes.at[slot]
        layer_two(pos, zc, held[2 * zc : 2 * zc + 4], filters, sums.at[at], out)
        if slot is not None:
            late[2 + slot].start()

    pool = pool2[...]
    halves = shift3[...]
    cells = [sums[0], sums[1], inner[0], inner[1], sums[2], sums[3]]
    for j in range(4):
        pair = jnp.concatenate([cells[j], cells[j + 2]], axis=1)
        pooled = dot(pair, pool).astype(BF)
        sides = dot(pooled, halves)
        for y in range(6):
            rows = slice(y * 32, y * 32 + 32)
            lanes = slice(y * 128, y * 128 + 128)
            vq[j, 0:32, lanes] = sides[rows, :128].astype(BF)
            vq[j, 32:64, lanes] = pooled[rows]
            vq[j, 64:96, lanes] = sides[rows, 128:].astype(BF)
    for copy in late:
        copy.wait()


def middle_forward_kernel(pos, vq, w3, pool3, cot, sent, edges, sl3):
    sent[64:192] = cot[...]
    filters = w3[...]
    cells = [None, None]
    for zp in range(2):
        for n in range(2):
            blocks = [
                vq[zp + kz, :, (2 * n + ky) * 128 : (2 * n + ky + 2) * 128]
                for kz in range(3)
                for ky in range(3)
            ]
            pre = dot(filters, jnp.concatenate(blocks, axis=0))
            s = sigmoid(pre)
            sl3[zp, :, n * 256 : n * 256 + 256] = slope_of(pre, s).astype(BF)
            a = act_of(pre, s)
            part = a[:, :128] + a[:, 128:]
            cells[n] = part if zp == 0 else cells[n] + part
    both = jnp.concatenate(cells, axis=1).astype(BF)
    sent[0:64] = dot(both, pool3[...]).astype(BF)
    odd = pos[1] % 2
    for zp in range(2):
        top, bottom = sl3[zp, :, 384:512], sl3[zp, :, 0:128]
        edges[odd, zp * 64 : zp * 64 + 64] = top
        edges[1 - odd, zp * 64 : zp * 64 + 64] = bottom


def deep_kernel(
    pos, own3, near, far, in1, out1, in2, out2, w4f, w4b, pool4, sl3, planes_of, shift4, w3b, spread_far,
    p4, near_out, far_out, field, own,
    planes, back_in, d3, spread3, sems,
):
    spread_copy = pltpu.make_async_copy(spread_far, spread3, sems.at[0])
    spread_copy.start()
    odd, ch = pos[0] % 2, pos[1]

    def pick(cond, one, two):
        return jnp.where(cond, one.astype(F32), two.astype(F32)).astype(BF)

    def in_order(blocks):
        first, second, third = blocks
        return [pick(odd == 1, first, third), second, pick(odd == 1, third, first)]

    def neighbour(inside, outside, upper, rows):
        one, two = inside[rows], outside[rows]
        return pick(upper, one, two), pick(upper, two, one)

    odd_y, odd_pair = ch % 2 == 1, ch % 4 >= 2
    mine = jnp.concatenate([near[0:64], own3[0:64], far[0:64]], axis=0)
    below1, above1 = neighbour(in1, out1, odd_y, slice(0, 192))
    below2, above2 = neighbour(in2, out2, odd_pair, slice(0, 192))
    parts = [
        jnp.concatenate(in_order([p[0:64], p[64:128], p[128:192]]), axis=0)
        for p in (below2, below1, mine, above1, above2)
    ]
    cots = in_order([near[64:192], own3[64:192], far[64:192]])
    edge_low, edge_high = neighbour(in1, out1, odd_y, slice(192, 320))
    flat = dot(jnp.concatenate(parts, axis=1), planes_of[...]).astype(BF)
    for zb in range(3):
        for zz in range(2):
            p = 2 * zb + zz
            planes[p * 64 : p * 64 + 64] = flat[zb * 64 : zb * 64 + 64, zz * 256 : zz * 256 + 256]
    for kx in range(3):
        moved = dot(planes[...], shift4[:, kx * 256 : kx * 256 + 256]).astype(BF)
        for p in range(6):
            field[p, kx * 64 : kx * 64 + 64] = moved[p * 64 : p * 64 + 64]

    row = lax.broadcasted_iota(jnp.int32, (128, 256), 0)
    lane = lax.broadcasted_iota(jnp.int32, (128, 256), 1)
    source_y, source_x = row // 16, row % 16
    y, x = lane // 32, lane % 32
    match = (source_x == x // 2) & (source_y == ch - 1 + y // 2) & (y < 6)
    spread = jnp.where(match, 0.125, 0.0).astype(BF)
    inner = lax.broadcasted_iota(jnp.int32, (128, 256), 1) // 64 == 1

    filters = w4f[...]
    pooled = None
    deltas = []
    for z in range(4):
        pre = fold_rows(dot(filters, field[z : z + 3].reshape(576, 256)))
        s = sigmoid(pre)
        wide = dot(cots[(z + 1) // 2], spread)
        delta = wide * slope_of(pre, s)
        deltas.append(delta.astype(BF))
        if z in (1, 2):
            own[z - 1] = jnp.where(inner, delta, 0.0).astype(BF)
            a = act_of(pre, s)
            pooled = a if pooled is None else pooled + a
    high = pooled.astype(BF)
    low = (pooled - high.astype(F32)).astype(BF)
    p4[...] = dot(high, pool4[...]) + dot(low, pool4[...])

    stacked = jnp.concatenate(deltas, axis=0)
    for kx in range(3):
        moved = dot(stacked, shift4[:, kx * 256 : kx * 256 + 256]).astype(BF)
        for z in range(4):
            back_in[z, kx * 128 : kx * 128 + 128] = moved[z * 128 : z * 128 + 128]
    filters = w4b[...]
    back = [
        fold_rows(dot(filters, back_in[z : z + 3].reshape(1152, 256))).astype(BF)
        for z in range(2)
    ]
    spread_copy.wait()
    wide = dot(jnp.concatenate(back, axis=1), spread3[...])
    for r in range(6):
        yg = 4 * ch + r - 1
        inside = jnp.logical_and(yg >= 0, yg < 32)
        lanes = slice(r * 128, r * 128 + 128)
        value = jnp.where(inside, wide[:, lanes], 0.0)
        for zp in range(2):
            rows = slice(zp * 64, zp * 64 + 64)
            if r == 0:
                slope = edge_low[rows]
            elif r == 5:
                slope = edge_high[rows]
            else:
                slope = sl3[zp, :, (r - 1) * 128 : r * 128]
            d3[zp, :, lanes] = (value * slope.astype(F32)).astype(BF)
    near_out[...] = d3[1 - odd]
    far_out[...] = d3[odd]


def own_packs(pos, near, far):
    odd = pos[0] % 2 == 1
    one, two = near[...].astype(F32), far[...].astype(F32)
    return jnp.where(odd, one, two).astype(BF), jnp.where(odd, two, one).astype(BF)


def grads_kernel(pos, field, own, near, far, p4, vq, sent, out):
    packs = own_packs(pos, near, far)
    rows = []
    for ky in range(3):
        moved = [own[z].astype(F32) for z in range(2)]
        if ky > 0:
            moved = [pltpu.roll(m, 32 * ky, 1) for m in moved]
        rows.append(jnp.concatenate([m.astype(BF) for m in moved], axis=1))
    right = jnp.concatenate(rows, axis=0)
    for kz in range(3):
        left = jnp.concatenate([field[1 + kz], field[2 + kz]], axis=1)
        res = dot_nt(left, right)
        for k in range(9):
            for c in range(8):
                at = (kz * 9 + k) * 8
                row, lane = k % 3 * 64 + c * 8, k // 3 * 128
                out[c, at : at + 8] = res[row : row + 8, lane : lane + 128]
    total = None
    zero = jnp.zeros((64, 512), BF)
    for j in range(4):
        rows = []
        for kz in range(3):
            zp = j - kz
            rows.append(packs[zp][:, 128:640] if 0 <= zp < 2 else zero)
        left = jnp.concatenate(
            [vq[j, :, ky * 128 : ky * 128 + 512] for ky in range(3)], axis=0
        )
        res = dot_nt(left, jnp.concatenate(rows, axis=0))
        total = res if total is None else total + res
    for k in range(9):
        for c in range(8):
            at = 216 + k * 4
            piece = total[k * 32 + c * 4 : k * 32 + c * 4 + 4]
            out[c, at : at + 4] = piece[:, :128]
            at, lanes = (252 + k * 4, slice(0, 64)) if k < 5 else (232 + k * 4, slice(64, 128))
            out[c, at : at + 4, lanes] = piece[:, 128:]
    for c in range(8):
        out[c, 268:272, 64:128] = jnp.zeros((4, 64), F32)
        out[c, 272:288] = p4[c * 16 : c * 16 + 16]
        sent[c] = out[c].astype(BF)


def shallow_back_kernel(
    pos, own_near, own_far, near, far, w3b, straight, cross, spread2, sl2_mid, sl2_edge, vx_mid, vx_edge,
    g2, ds, d2, vx, sems,
):
    vx_copies = [
        pltpu.make_async_copy(vx_mid, vx.at[1:9], sems.at[0]),
        pltpu.make_async_copy(vx_edge.at[0], vx.at[0], sems.at[1]),
        pltpu.make_async_copy(vx_edge.at[1], vx.at[9], sems.at[2]),
    ]
    for copy in vx_copies:
        copy.start()
    sl2 = (sl2_edge.at[0], sl2_mid.at[0], sl2_mid.at[1], sl2_edge.at[1])

    def rows_of(value):
        return jnp.concatenate([value[:, y * 128 : y * 128 + 128] for y in range(6)], axis=0)

    odd = pos[0] % 2 == 1
    one, two = rows_of(near).astype(F32), rows_of(far).astype(F32)
    above = jnp.where(odd, one, two).astype(BF)
    below = jnp.where(odd, two, one).astype(BF)
    first, second = [rows_of(pack) for pack in own_packs(pos, own_near, own_far)]
    direct, across = straight[...], cross[...]
    sources = (
        (jnp.concatenate([above, second], axis=1), across),
        (first, direct),
        (second, direct),
        (jnp.concatenate([first, below], axis=1), across),
    )
    for j, (source, matrix) in enumerate(sources):
        moved = dot(source, matrix).astype(BF)
        for y in range(6):
            for kx in range(3):
                piece = moved[y * 64 : y * 64 + 64, kx * 128 : kx * 128 + 128]
                ds[j, kx * 64 : kx * 64 + 64, y * 128 : y * 128 + 128] = piece

    for z in (0, 1, 10, 11):
        d2[z] = jnp.zeros((32, 1024), BF)
    filters = w3b[...]
    backs = []
    for zp in range(2):
        parts = dot(filters, ds[zp : zp + 3].reshape(576, 768))
        for y in range(4):
            back = parts[0:32, y * 128 : y * 128 + 128]
            for ky in (1, 2):
                back = back + parts[ky * 32 : ky * 32 + 32, (y + ky) * 128 : (y + ky + 1) * 128]
            backs.append(back.astype(BF))
    wide = dot(jnp.concatenate(backs, axis=0), spread2[...])
    for zp in range(2):
        for y in range(4):
            at = (zp * 4 + y) * 32
            for h in range(2):
                value = wide[at : at + 32, h * 128 : h * 128 + 128]
                z = zp + 2 * h
                for dz in range(2):
                    for dy in range(2):
                        rows = slice((dz * 2 + dy) * 32, (dz * 2 + dy) * 32 + 32)
                        slope = sl2[z][rows, y * 128 : y * 128 + 128].astype(F32)
                        lanes = slice((2 * y + dy) * 128, (2 * y + dy) * 128 + 128)
                        d2[2 * z + dz + 2, :, lanes] = (value * slope).astype(BF)

    vx_copies[0].wait()
    total = None
    for z in (1, 2, 3, 4, 5, 6, 7, 8, 0, 9):
        if z == 0:
            vx_copies[1].wait()
            vx_copies[2].wait()
        left = jnp.concatenate(
            [vx[z, :, ky * 128 : ky * 128 + 1024] for ky in range(3)], axis=0
        )
        right = jnp.concatenate([d2[z + 2 - kz] for kz in range(3)], axis=0)
        part = dot_nt(left, right)
        total = part if total is None else total + part
    g2[...] = jnp.zeros((160, 128), F32)
    g2[0:144, 0:96] = total


def write_kernel(pos, whole, four, three, two):
    deep = whole[:, 0:9].astype(F32).reshape(288, 128)
    four[...] = deep[:216]
    for k in range(9):
        low = deep[216 + k * 4 : 220 + k * 4]
        at, lanes = (252 + k * 4, slice(0, 64)) if k < 5 else (232 + k * 4, slice(64, 128))
        high = deep[at : at + 4, lanes]
        three[k] = low[:, 0:64]
        three[9 + k] = low[:, 64:128]
        three[18 + k] = high
    shallow = whole[:, 9:14].astype(F32).reshape(160, 128)
    for kz in range(3):
        two[kz] = shallow[:144, kz * 32 : kz * 32 + 32]


def swap(one, two, axis, step=1):
    count = lax.axis_size(axis)
    inside = [(i, i ^ step) for i in range(count)]
    outside = [(i, i + step) for i in range(count - step) if i % (2 * step) >= step]
    outside = outside + [(b, a) for a, b in outside]
    return lax.ppermute(one, axis, inside), lax.ppermute(two, axis, outside)


def swap_cores(value):
    return lax.ppermute(value, "gz", [(i, i ^ 1) for i in range(lax.axis_size("gz"))])


def to_all(piece, axis):
    count = lax.axis_size(axis)
    copies = jnp.broadcast_to(piece[None], (count,) + piece.shape)
    return lax.all_to_all(copies, axis, 0, 0, tiled=True)


def band(filters):
    taps = filters.transpose(0, 2, 3, 4, 1).reshape(32, 3, 3, 48)
    rows = [
        jnp.pad(taps, ((0, 0), (dz, 1 - dz), (dy, 1 - dy), (0, 0)))
        for dz in range(2)
        for dy in range(2)
    ]
    return jnp.stack(rows).reshape(128, 768)


def body(volume, filters_two, filters_three, filters_four, cotangent):
    gz, ch = lax.axis_index("gz"), lax.axis_index("ch")
    pos = jnp.stack([gz, ch]).astype(jnp.int32)
    odd_z, odd_y = gz % 2, ch % 2
    shape = jax.ShapeDtypeStruct

    field = volume.transpose(1, 2, 0, 3)
    near, far = swap(
        lax.dynamic_slice_in_dim(volume, 5 * (1 - odd_y), 3, 2).transpose(1, 2, 0, 3),
        lax.dynamic_slice_in_dim(volume, 5 * odd_y, 3, 2).transpose(1, 2, 0, 3),
        "ch",
    )
    low = jnp.where(odd_y == 1, near, far)
    high = jnp.where(odd_y == 1, far, near)
    mid = jnp.concatenate([low, field, high], axis=1)

    four = filters_four.transpose(2, 3, 4, 1, 0).reshape(216, 128)
    three = filters_three.transpose(2, 3, 4, 1, 0).reshape(108, 64)
    three = jnp.pad(three, ((0, 0), (0, 64)))
    cot = cotangent.reshape(16, 128)
    held = jnp.concatenate(
        [
            cot,
            lax.dynamic_slice_in_dim(four, 108 * odd_z, 108, 0),
            lax.dynamic_slice_in_dim(three, 54 * odd_z, 54, 0),
        ],
        axis=0,
    )
    held = jnp.broadcast_to(held[None], (8, 178, 128))
    near, far = swap(
        lax.dynamic_slice_in_dim(mid, 5 * (1 - odd_z), 3, 0),
        lax.dynamic_slice_in_dim(mid, 5 * odd_z, 3, 0),
        "gz",
    )
    near, two = lax.optimization_barrier((near, filters_two))
    w2 = band(two)
    all_of = lax.all_to_all(held, "ch", 0, 0, tiled=True)
    mine, cots = lax.optimization_barrier((all_of[:, 16:], all_of[:, :16].reshape(128, 128)))
    other = swap_cores(mine)
    first = jnp.where(odd_z == 1, other, mine)
    second = jnp.where(odd_z == 1, mine, other)
    four = jnp.concatenate([first[:, :108], second[:, :108]], axis=1).reshape(8, 27, 8, 128)
    three = jnp.concatenate([first[:, 108:, :64], second[:, 108:, :64]], axis=1)
    three = three.reshape(8, 27, 4, 64)
    w3f = three.transpose(3, 1, 0, 2).reshape(64, 864)
    back = three[:, ::-1].reshape(8, 3, 3, 3, 4, 64)
    w3b = back.transpose(2, 0, 4, 1, 3, 5).reshape(96, 576)
    w4f = four.reshape(8, 3, 3, 3, 8, 128).transpose(2, 5, 1, 3, 0, 4).reshape(384, 576)
    back = four[:, ::-1].reshape(8, 3, 3, 3, 8, 128)
    w4b = back.transpose(2, 0, 4, 1, 3, 5).reshape(192, 1152)

    inner, sl2_mid, vx_mid = call(
        inner_forward_kernel,
        (
            shape((2, 192, 128), BF),
            shape((2, 128, 512), BF),
            shape((8, 48, 1280), BF),
        ),
        [
            pltpu.VMEM((8, 48, 1792), BF),
            pltpu.VMEM((2, 128, 512), BF),
            pltpu.SemaphoreType.DMA((2,)),
        ],
        1 << 31,
        (pos, mid, w2, const(shift_rows)),
        far_out=(1, 2),
    )
    vq, pool3, sl2_edge, vx_edge = call(
        outer_forward_kernel,
        (
            shape((4, 96, 768), BF),
            shape((256, 128), BF),
            shape((2, 128, 512), BF),
            shape((2, 48, 1280), BF),
        ),
        [
            pltpu.VMEM((4, 192, 128), BF),
            pltpu.VMEM((2, 128, 512), BF),
            pltpu.VMEM((12, 48, 1792), BF),
            pltpu.SemaphoreType.DMA((4,)),
        ],
        1 << 32,
        (
            pos, near, mid, far, inner, w2,
            const(shift_rows), const(pool_two), const(shift_halves), const(pool_three),
        ),
        far_out=(2, 3),
    )
    sent, edges, sl3 = call(
        middle_forward_kernel,
        (
            shape((192, 128), BF),
            shape((2, 128, 128), BF),
            shape((2, 64, 512), BF),
        ),
        [],
        1 << 30,
        (pos, vq, w3f, pool3, cots),
    )
    near, far = swap(sent, sent, "gz")
    near, w4f, w4b, w3b = lax.optimization_barrier((near, w4f, w4b, w3b))
    planes = jnp.concatenate([near[:64], sent[:64], far[:64]], axis=0)
    in1, out1 = swap(
        jnp.concatenate([planes, edges[0]], axis=0),
        jnp.concatenate([planes, edges[1]], axis=0),
        "ch",
    )
    in2, out2 = swap(planes, planes, "ch", 2)
    p4, own_near, own_far, field4, own4 = call(
        deep_kernel,
        (
            shape((128, 128), F32),
            shape((64, 768), BF),
            shape((64, 768), BF),
            shape((6, 192, 256), BF),
            shape((2, 128, 256), BF),
        ),
        [
            pltpu.VMEM((384, 256), BF),
            pltpu.VMEM((4, 384, 256), BF),
            pltpu.VMEM((2, 64, 768), BF),
            pltpu.VMEM((512, 768), BF),
            pltpu.SemaphoreType.DMA((1,)),
        ],
        1 << 32,
        (
            pos, sent, near, far, in1, out1, in2, out2,
            w4f, w4b, const(pool_four), sl3, const(gather_planes), const(shift_planes),
            w3b, const(spread_three),
        ),
        far_in=(14, 15),
    )
    near, far = swap(own_near, own_far, "gz")
    (sent,) = call(
        grads_kernel,
        (shape((8, 288, 128), BF),),
        [pltpu.VMEM((8, 288, 128), F32)],
        1 << 34,
        (pos, field4, own4, own_near, own_far, p4, vq),
    )
    got = lax.all_to_all(sent, "ch", 0, 0, tiled=True)
    grads = got.astype(F32).sum(axis=0).astype(BF)
    pooled_four = got[:, 272:, :16].transpose(1, 0, 2)[:, None]

    (g2,) = call(
        shallow_back_kernel,
        (shape((160, 128), F32),),
        [
            pltpu.VMEM((4, 192, 768), BF),
            pltpu.VMEM((12, 32, 1024), BF),
            pltpu.VMEM((10, 48, 1280), BF),
            pltpu.SemaphoreType.DMA((3,)),
        ],
        1 << 32,
        (
            pos, own_near, own_far, near, far, w3b,
            const(shift_straight), const(shift_cross), const(spread_two),
            sl2_mid, sl2_edge, vx_mid, vx_edge,
        ),
        far_in=(11, 12),
    )
    pieces = jnp.concatenate(
        [grads.reshape(32, 9, 128), g2.astype(BF).reshape(32, 5, 128)], axis=1
    )
    pieces = lax.all_to_all(pieces, "gz", 0, 0, tiled=True).astype(F32).sum(axis=0)
    two = to_all(pieces[9:].astype(BF), "ch").astype(F32).sum(axis=0)
    whole = to_all(jnp.concatenate([pieces[:9], two], axis=0).astype(BF), "gz")
    four, three, two = call(
        write_kernel,
        (shape((216, 128), F32), shape((27, 4, 64), F32), shape((3, 144, 32), F32)),
        [],
        1 << 20,
        (pos, whole),
    )
    grad_four = four.reshape(3, 3, 3, 8, 128).transpose(4, 3, 0, 1, 2)
    grad_three = three.reshape(3, 3, 3, 4, 64).transpose(4, 3, 0, 1, 2)
    grad_two = two.reshape(3, 3, 3, 16, 32).transpose(4, 3, 0, 1, 2)
    return (pooled_four, grad_two, grad_three, grad_four)


def solution(mesh):
    in_specs = (
        P(None, "gz", "ch", None),
        P(),
        P(None, "ch", None, None, None),
        P(None, "ch", None, None, None),
        P("ch", "gz", None, None),
    )
    out_specs = (
        P("ch", "gz", None, None),
        P(),
        P(None, "ch", None, None, None),
        P(None, "ch", None, None, None),
    )
    return jax.shard_map(body, mesh=mesh, in_specs=in_specs, out_specs=out_specs, check_vma=False)
```
